128 devices in a mesh: section: 2 (over core), shard: 2 (over z_lo), replica: 32 (over y, x, z_hi).
Axes of the slice: x: 4, y: 4, z: 4 (z_hi: 2, z_lo: 2; z = z_hi * 2 + z_lo), core: 2. Of those that a mesh axis runs over, the one named last changes fastest.
Arguments:
- block_in: bfloat16 [2, 8192, 768], P(None, ('shard', 'replica')), may hold values from -6 to 6
- cotangent: bfloat16 [2, 8192, 768], P(None, ('shard', 'replica')), may hold values from -6 to 6
- lengths: int32 [2, 64, 4], P(None, ('shard', 'replica')), may hold values from 1 to 64, 128 in all within a row
- routes: int32 [2, 2, 8192, 1], P('section', None, ('shard', 'replica')), may hold values from 0 to 31; in each aligned block of 128 rows (0 to 127, 128 to 255, ..., all dimensions but the last counted through in order) at most 6 rows name the same one
- query_weight: bfloat16 [2, 768, 768], P('section', 'shard'), may hold values from -0.21875 to 0.21875
- key_weight: bfloat16 [2, 768, 768], P('section', 'shard'), may hold values from -0.21875 to 0.21875
- value_weight: bfloat16 [2, 768, 768], P('section', 'shard'), may hold values from -0.21875 to 0.21875
- out_weight: bfloat16 [2, 768, 768], P('section', 'shard'), may hold values from -0.875 to 0.875
- attn_gain: bfloat16 [2, 768], P('section', 'shard'), may hold values from 0.25 to 1.75
- moe_gain: bfloat16 [2, 768], P('section', 'shard'), may hold values from 0.25 to 1.75
- router: bfloat16 [2, 768, 32], P('section', 'shard'), may hold values from -0.109375 to 0.109375
- rel_table: bfloat16 [2, 32, 12], P('section', 'shard'), may hold values from -6 to 6
- expert_in: bfloat16 [2, 32, 768, 3072], P('section', 'replica', None, 'shard'), may hold values from -0.3125 to 0.3125
- expert_out: bfloat16 [2, 32, 3072, 768], P('section', 'replica', 'shard'), may hold values from -6 to 6
Outputs:
- section_out: bfloat16 [2, 2, 8192, 768], P('section', None, ('shard', 'replica'))
- input_grad: bfloat16 [2, 2, 8192, 768], P('section', None, ('shard', 'replica'))
- query_grad: float32 [2, 768, 768], P('section', 'shard')
- key_grad: float32 [2, 768, 768], P('section', 'shard')
- value_grad: float32 [2, 768, 768], P('section', 'shard')
- out_grad: float32 [2, 768, 768], P('section', 'shard')
- attn_gain_grad: float32 [2, 768], P('section', 'shard')
- moe_gain_grad: float32 [2, 768], P('section', 'shard')
- router_grad: float32 [2, 768, 32], P('section', 'shard')
- rel_table_grad: float32 [2, 32, 12], P('section', 'shard')
- expert_in_grad: float32 [2, 32, 768, 3072], P('section', 'replica', None, 'shard')
- expert_out_grad: float32 [2, 32, 3072, 768], P('section', 'replica', 'shard')
The draws below stay inside these ranges and needn't reach their ends.
Inputs may be any that keep to these rules, and one draw needn't show every extreme that they name: `lengths`: in every row the last entry is a padding run, whose tokens belong to no sequence and go to no expert; the other entries are sequences laid out in order. `routes`: within each micro-batch of each layer, at most 6 of the 128 rows of one device name one expert, and some device's rows name some expert exactly 6 times. Routes of padding tokens are ignored.
All inputs are finite; a program needn't handle non-finite values.
Results may differ from the reference program's by a relative error of at most 0.03.
Values may be sent and summed in bfloat16 or wider, within the bound.
No kernel may reach another device: no remote copies, remote signals or barrier semaphores. Data moves between devices by JAX's collectives and lax.ppermute only.
A program may use at most 192 MiB of HBM per device.

```python
import math
from functools import partial
import jax
import jax.numpy as jnp
import numpy as np
from jax import lax

D = 768
HEADS = 12
HEAD_DIM = 64
FF = 3072
NB = 32
MAXDIST = 128
MICRO = 2
DOCS = 4
TOK_MB = 128
LONGEST = 64
CAP = 6
EXPERTS = 32
DATA_DEVS = 64
ROWS = 8192
SECTIONS = 2


def block_scale(own_key, shape, pieces, least, largest):
    level = 1.0
    for dim, shards_of in pieces:
        draws = jax.random.uniform(jax.random.fold_in(jax.random.fold_in(own_key, 6), dim), (shards_of,), jnp.float32, least / len(pieces), largest / len(pieces))
        level = level * jnp.repeat(jnp.exp(draws), shape[dim] // shards_of).reshape((-1,) + (1,) * (len(shape) - 1 - dim))
    return level


def profile(number_of, total, most, slope):
    loads = [(1 << 20) // math.isqrt(grade ** slope) + 1 for grade in range(2, number_of + 1)]
    spare, given = total - most - (number_of - 1), [1] * (number_of - 1)
    while spare > 0:
        candidates = [i for i in range(number_of - 1) if given[i] < most]
        whole, remaining = sum([loads[i] for i in candidates]), spare
        for i in candidates:
            extra = min(most - given[i], max(1, remaining * loads[i] // whole), spare)
            given[i] = given[i] + extra
            spare = spare - extra
    return np.array([most] + given)


def ragged(own_key, amount, total, most, lean):
    if amount == 2:
        one = jax.random.randint(own_key, (), max(1, total - most), min(most, total - 1) + 1)
        return jnp.stack([one, total - one])
    sizes = jnp.asarray(profile(amount, total, most, lean), jnp.int32)
    twos = (amount - 1) // 2
    giver, sink = sizes[1:1 + 2 * twos:2], sizes[2:2 + 2 * twos:2]
    margin = jnp.minimum(giver - 1, most - sink)
    shifted = jax.random.randint(jax.random.fold_in(own_key, 1), (twos,), 0, 1 << 20) % (margin + 1)
    sizes = sizes.at[1:1 + 2 * twos:2].set(giver - shifted).at[2:2 + 2 * twos:2].set(sink + shifted)
    return sizes[jax.random.permutation(jax.random.fold_in(own_key, 2), amount)]


def deal_out(rng, own, number, rows, number_of, top, bound, skew):
    ranking = jax.random.permutation(rng, number_of)
    packed, usual = load_shares(number_of, rows * top, bound, skew, True), load_shares(number_of, rows * top, bound, skew, False)
    places = jnp.arange(number_of)

    def named(tallies, rotation):
        used = int((tallies > 0).sum())
        fixed = max(1, used // 4)
        passed = fixed + (places - fixed + rotation * (used - fixed)) % max(1, number_of - fixed)
        return jnp.zeros((number_of,), jnp.int32).at[ranking[jnp.where(places < fixed, places, passed)]].set(jnp.asarray(tallies, jnp.int32))

    tallies = jnp.where(number % 4 == 0, named(packed, number // 4), named(usual, number - number // 4 - 1))
    mixed = jax.random.permutation(jax.random.fold_in(own, 3), number_of)
    giver, taker = mixed[0:number_of // 2 * 2:2], mixed[1:number_of // 2 * 2:2]
    slack = jnp.minimum(tallies[giver] - 1, bound - tallies[taker]) // 2
    slack = jnp.where((giver == ranking[0]) | (taker == ranking[0]) | (tallies[taker] == 0), 0, jnp.maximum(slack, 0))
    passed = jax.random.randint(jax.random.fold_in(own, 4), (number_of // 2,), 0, 1 << 20) % (slack + 1)
    tallies = tallies.at[giver].add(-passed).at[taker].add(passed)
    labels = jnp.searchsorted(jnp.cumsum(tallies), jnp.arange(rows * top), side="right").astype(jnp.int32)
    listing = labels.reshape(top, rows).T
    listing = listing[jax.random.permutation(jax.random.fold_in(own, 1), rows)]
    rotation = jax.random.randint(jax.random.fold_in(own, 2), (rows, 1), 0, top)
    return jnp.take_along_axis(listing, (jnp.arange(top)[None, :] + rotation) % top, axis=1)


def load_shares(count, total, most, lean, full):
    portions = [(1 << 20) // math.isqrt(grade ** lean) + 1 for grade in range(1, count + 1)]
    largest = most if full else min(most, max(-(-total // count), total * portions[0] // sum(portions)))
    least = 1 if total - largest >= count - 1 else 0
    given, spare = [largest] + [least] * (count - 1), total - largest - least * (count - 1)
    while spare > 0:
        movable = [i for i in range(1, count) if given[i] < largest] or [i for i in range(1, count) if given[i] < most]
        whole, remaining = sum([portions[i] for i in movable]), spare
        for i in movable:
            extra = min(most - given[i], max(1, remaining * portions[i] // whole), spare)
            given[i] = given[i] + extra
            spare = spare - extra
    return np.array(given)


def normal_values(own_key, dims, deviation, reach, split=(), kind=jnp.bfloat16):
    factor_of = block_scale(own_key, dims, split, -0.22, 0.18) if split else 1.0
    array = jax.random.normal(own_key, dims, jnp.float32) * deviation * factor_of
    return jnp.minimum(jnp.maximum(array, -reach), reach).astype(kind)


def setup_inputs(seed: int = 0) -> dict:
    keys = jax.random.split(jax.random.key(seed), 15)
    block_in = normal_values(keys[0], (MICRO, ROWS, D), 1.0, 6.0, ((1, 64),))
    cotangent = normal_values(keys[1], (MICRO, ROWS, D), 1.0, 6.0, ((1, 64),))
    lengths = jax.vmap(lambda own: ragged(own, DOCS, TOK_MB, LONGEST, 1))(jax.random.split(keys[2], MICRO * DATA_DEVS)).reshape((MICRO, DATA_DEVS, DOCS)).astype(jnp.int32)
    routes_keys = jax.random.split(jax.random.fold_in(keys[3], 1), SECTIONS * MICRO * ROWS // TOK_MB)
    routes_turns = jax.random.permutation(jax.random.fold_in(keys[3], 3), SECTIONS * MICRO * ROWS // TOK_MB)
    routes = jax.vmap(lambda own, number: deal_out(jax.random.fold_in(keys[3], 2), own, number, TOK_MB, EXPERTS, 1, CAP, 1))(routes_keys, routes_turns).reshape((SECTIONS, MICRO, ROWS, 1))
    query_weight = normal_values(keys[4], (SECTIONS, D, D), D ** -0.5, 0.21875, ((0, 2), (1, 2)))
    key_weight = normal_values(keys[5], (SECTIONS, D, D), D ** -0.5, 0.21875, ((0, 2), (1, 2)))
    value_weight = normal_values(keys[6], (SECTIONS, D, D), D ** -0.5, 0.21875, ((0, 2), (1, 2)))
    out_weight = normal_values(keys[7], (SECTIONS, D, D), (D // 16) ** -0.5, 0.875, ((0, 2), (1, 2)))
    attn_gain = jnp.clip(1.0 + 0.15 * jax.random.normal(keys[8], (SECTIONS, D), jnp.float32), 0.25, 1.75).astype(jnp.bfloat16)
    moe_gain = jnp.clip(1.0 + 0.15 * jax.random.normal(keys[9], (SECTIONS, D), jnp.float32), 0.25, 1.75).astype(jnp.bfloat16)
    router = normal_values(keys[10], (SECTIONS, D, EXPERTS), (4 * D) ** -0.5, 0.109375, ((0, 2), (1, 2)))
    rel_table = normal_values(keys[11], (SECTIONS, NB, HEADS), 1.0, 6.0, ((0, 2), (1, 2)))
    expert_in = normal_values(keys[12], (SECTIONS, EXPERTS, D, FF), (D // 2) ** -0.5, 0.3125, ((0, 2), (1, 32), (3, 2)))
    expert_out = normal_values(keys[13], (SECTIONS, EXPERTS, FF, D), (max(1, FF // (2 * EXPERTS * EXPERTS))) ** -0.5, 6.0, ((0, 2), (1, 32), (2, 2)))
    return dict(block_in=block_in, cotangent=cotangent, lengths=lengths, routes=routes, query_weight=query_weight, key_weight=key_weight, value_weight=value_weight, out_weight=out_weight, attn_gain=attn_gain, moe_gain=moe_gain, router=router, rel_table=rel_table, expert_in=expert_in, expert_out=expert_out)


@jax.custom_vjp
def low(v):
    return lax.optimization_barrier(v.astype(jnp.bfloat16)).astype(jnp.float32)

@jax.custom_vjp
def low_back(v):
    return v

def low_keep(v):
    return (low(v), None)

def low_pass(kept, grad):
    return (grad,)

def back_keep(v):
    return (v, None)

def back_low(kept, grad):
    return (low(grad),)
low.defvjp(low_keep, low_pass)
low_back.defvjp(back_keep, back_low)
norm_eps = 1e-06
highest = lax.Precision.HIGHEST

def bucket_table(length):
    distance = np.maximum(np.arange(length)[:, None] - np.arange(length)[None, :], 0)
    exact_count = NB // 2
    log_ratio = np.log(np.maximum(distance, 1) / exact_count) / np.log(MAXDIST / exact_count)
    far_bucket = exact_count + np.floor(log_ratio * (NB - exact_count)).astype(np.int32)
    return np.where(distance < exact_count, distance, np.minimum(far_bucket, NB - 1)).astype(np.int32)

def rms_scale(values_in, gain_vector):
    return values_in * lax.rsqrt(lax.optimization_barrier(jnp.mean(values_in * values_in, axis=-1, keepdims=True)) + norm_eps) * gain_vector

def segment_ids(doc_lengths, length):
    doc_ends = jnp.cumsum(doc_lengths, dtype=jnp.int32)
    places = jnp.arange(length, dtype=jnp.int32)
    return lax.optimization_barrier(jnp.sum((places[:, None] >= doc_ends[None, :]).astype(jnp.int32), axis=1, dtype=jnp.int32))

def dispatch_table(route_ids, routed, experts, capacity):
    expert_ids = jnp.arange(experts, dtype=jnp.int32)
    route_hot = ((route_ids[:, None] == expert_ids[None, :]) & routed[:, None]).astype(jnp.int32)
    before = jnp.cumsum(route_hot, axis=0, dtype=jnp.int32) - route_hot
    slot_ids = lax.optimization_barrier(jnp.sum(route_hot * (before + expert_ids[None, :] * capacity), axis=1, dtype=jnp.int32))
    slot_ids = jnp.where(routed, slot_ids, -1)
    return jnp.arange(experts * capacity, dtype=jnp.int32)[:, None] == slot_ids[None, :]

def layer_block(inflow, doc_lengths, route_ids, weights, buckets):
    query_full, key_full, value_full, out_full, attn_scale, moe_scale, router_full, table_full, expert_in_full, expert_out_full = weights
    devices_here, row_count, model_width = inflow.shape
    places = jnp.arange(row_count, dtype=jnp.int32)
    segment = jax.vmap(lambda lens_row: segment_ids(lens_row, row_count))(doc_lengths)
    routed = segment < DOCS - 1
    attend_mask = (segment[:, :, None] == segment[:, None, :]) & (places[:, None] >= places[None, :])[None]
    normed_one = low(rms_scale(inflow, attn_scale))

    def project(matrix):
        return low_back(low(jnp.einsum('drc,ce->dre', normed_one, matrix, precision=highest)))
    queries = project(query_full).reshape(devices_here, row_count, HEADS, HEAD_DIM)
    key_rows = project(key_full).reshape(devices_here, row_count, HEADS, HEAD_DIM)
    value_rows = project(value_full).reshape(devices_here, row_count, HEADS, HEAD_DIM)
    rel_bias = jnp.transpose(jnp.take(table_full, buckets, axis=0), (2, 0, 1))
    raw_scores = low_back(jnp.einsum('dqhc,dkhc->dhqk', queries, key_rows, precision=highest) * HEAD_DIM ** (-0.5) + rel_bias[None])
    masked = jnp.where(attend_mask[:, None], raw_scores, -1e+30)
    row_max = lax.optimization_barrier(jnp.max(masked, axis=-1, keepdims=True))
    exponent = jnp.exp(masked - row_max)
    attn_prob = exponent / lax.optimization_barrier(jnp.sum(exponent, axis=-1, keepdims=True))
    mixed = low_back(low(jnp.einsum('dhqk,dkhc->dqhc', low(attn_prob), value_rows, precision=highest)))
    mixed = mixed.reshape(devices_here, row_count, model_width)
    resid = inflow + low_back(jnp.einsum('drc,ce->dre', mixed, out_full, precision=highest))
    normed_two = low(rms_scale(resid, moe_scale))
    logits = low_back(jnp.einsum('drc,ce->dre', normed_two, router_full, precision=highest))
    logit_exp = jnp.exp(logits - lax.optimization_barrier(jnp.max(logits, axis=-1, keepdims=True)))
    router_prob = logit_exp / lax.optimization_barrier(jnp.sum(logit_exp, axis=-1, keepdims=True))
    route_hot = (route_ids[..., None] == jnp.arange(EXPERTS, dtype=jnp.int32)).astype(jnp.float32)
    gate_value = lax.optimization_barrier(jnp.sum(router_prob * route_hot, axis=-1))
    slot_table = jax.vmap(lambda ids_row, routed_row: dispatch_table(ids_row, routed_row, EXPERTS, CAP))(route_ids, routed)
    slot_table = slot_table.astype(jnp.float32)
    outgoing = low_back(jnp.einsum('dsr,drc->dsc', slot_table, normed_two, precision=highest))
    outgoing = outgoing.reshape(devices_here, EXPERTS, CAP, model_width)
    hidden_pre = low_back(jnp.einsum('decx,exf->decf', outgoing, expert_in_full, precision=highest))
    hidden_act = low(jax.nn.gelu(hidden_pre))
    expert_made = low_back(low(jnp.einsum('decf,efx->decx', hidden_act, expert_out_full, precision=highest)))
    expert_made = expert_made.reshape(devices_here, EXPERTS * CAP, model_width)
    combined = jnp.einsum('dsr,dsc->drc', slot_table, expert_made, precision=highest)
    return resid + gate_value[..., None] * combined

def micro_step(batch_items, weights, buckets):
    return layer_block(batch_items[0], batch_items[1], batch_items[2], weights, buckets)

def reference(block_in, cotangent, lengths, routes, query_weight, key_weight, value_weight, out_weight, attn_gain, moe_gain, router, rel_table, expert_in, expert_out):
    buckets = jnp.asarray(bucket_table(TOK_MB))
    params = tuple((member.astype(jnp.float32) for member in (query_weight, key_weight, value_weight, out_weight, attn_gain, moe_gain, router, rel_table, expert_in, expert_out)))
    start_rows = block_in.astype(jnp.float32).reshape(MICRO, DATA_DEVS, TOK_MB, D)
    route_ids = routes.reshape(SECTIONS, MICRO, DATA_DEVS, TOK_MB)
    probes = jnp.zeros((SECTIONS, MICRO, DATA_DEVS, TOK_MB, D), jnp.float32)

    def run_sections(start_rows, probes, params):
        produced = []
        current = start_rows
        for section_number in range(SECTIONS):
            weights = tuple((member[section_number] for member in params))
            step_fn = jax.checkpoint(partial(micro_step, weights=weights, buckets=buckets))
            result = lax.map(step_fn, (current, lengths, route_ids[section_number]))
            produced.append(result)
            if section_number + 1 < SECTIONS:
                current = low_back(low(result)) + probes[section_number + 1]
        return jnp.stack(produced)
    produced, pullback = jax.vjp(run_sections, start_rows, probes, params)
    cotangent_rows = cotangent.astype(jnp.float32).reshape(1, MICRO, DATA_DEVS, TOK_MB, D)
    cotangents = jnp.concatenate([jnp.zeros((SECTIONS - 1, MICRO, DATA_DEVS, TOK_MB, D), jnp.float32), cotangent_rows], axis=0)
    grad_start, grad_probes, grad_params = pullback(cotangents)
    input_grad = jnp.concatenate([grad_start[None], grad_probes[1:]], axis=0)
    input_grad = input_grad.astype(jnp.bfloat16).reshape(SECTIONS, MICRO, ROWS, D)
    section_out = produced.astype(jnp.bfloat16).reshape(SECTIONS, MICRO, ROWS, D)
    return (section_out, input_grad, grad_params[0], grad_params[1], grad_params[2], grad_params[3], grad_params[4], grad_params[5], grad_params[6], grad_params[7], grad_params[8], grad_params[9])
```

```python
import functools

import jax
import jax.numpy as jnp
import numpy as np
from jax import lax
from jax.experimental import pallas as pl
from jax.experimental.pallas import tpu as pltpu
from jax.sharding import PartitionSpec as P

HEADS = 12
HEAD_DIM = 64
NB = 32
MAXDIST = 128
DOCS = 4
ROWS = 128
WIDTH = 768
HALF = 384
EXPERTS = 32
SLOTS = 8
MIB = 1024 * 1024
BF = jnp.bfloat16
F32 = jnp.float32

norm_eps = 1e-06
BOTH = ("shard", "replica")


def bucket_of_distance(length):
    distance = np.arange(length)
    exact_count = NB // 2
    log_ratio = np.log(np.maximum(distance, 1) / exact_count) / np.log(MAXDIST / exact_count)
    far_bucket = exact_count + np.floor(log_ratio * (NB - exact_count)).astype(np.int32)
    return np.where(distance < exact_count, distance, np.minimum(far_bucket, NB - 1)).astype(
        np.int32
    )


def swap(block):
    return lax.ppermute(block, "section", [(0, 1), (1, 0)])


def dot(left, right):
    return jnp.dot(left, right, preferred_element_type=F32)


def dot_t(left, right):
    return lax.dot_general(left, right, (((1,), (1,)), ((), ())), preferred_element_type=F32)


def t_dot(left, right):
    return lax.dot_general(left, right, (((0,), (0,)), ((), ())), preferred_element_type=F32)


def in_halves(matrix, lower):
    first, second = matrix[:, :HALF], matrix[:, HALF:]
    return jnp.where(lower, first, second), jnp.where(lower, second, first)


def project(matrix, lower, own_ref, other_ref):
    own_part, other_part = in_halves(matrix, lower)
    return dot(own_part, own_ref[...]) + dot(other_part, other_ref[...])


def project_back(matrix, lower, own_ref, other_ref):
    own_part = dot_t(matrix, own_ref[...])
    other_part = dot_t(matrix, other_ref[...])
    return jnp.concatenate(
        [jnp.where(lower, own_part, other_part), jnp.where(lower, other_part, own_part)], axis=1
    )


def segments(info_ref, axis):
    places = lax.broadcasted_iota(jnp.int32, (ROWS, ROWS), axis)
    found = jnp.zeros((ROWS, ROWS), jnp.int32)
    for run in range(DOCS):
        found = found + (places >= info_ref[2 + run]).astype(jnp.int32)
    return found


def attend_mask(info_ref):
    rows = lax.broadcasted_iota(jnp.int32, (ROWS, ROWS), 0)
    columns = lax.broadcasted_iota(jnp.int32, (ROWS, ROWS), 1)
    return (segments(info_ref, 0) == segments(info_ref, 1)) & (columns <= rows)


def head_prob(queries_own, key_pair, bias_ref, head, mask):
    bias = pltpu.roll(
        jnp.broadcast_to(bias_ref[head : head + 1, :], (ROWS, ROWS)),
        0,
        axis=1,
        stride=1,
        stride_axis=0,
    )
    scores = dot_t(queries_own, key_pair) * HEAD_DIM ** (-0.5) + bias
    scores = jnp.where(mask, scores, -1e30)
    exponent = jnp.exp(scores - jnp.max(scores, axis=-1, keepdims=True))
    return exponent / jnp.sum(exponent, axis=-1, keepdims=True)


def pair_masks():
    lane = lax.broadcasted_iota(jnp.int32, (ROWS, 2 * HEAD_DIM), 1)
    return lane < HEAD_DIM


def only(first, head_in_pair, pair):
    keep = first if head_in_pair == 0 else jnp.logical_not(first)
    return jnp.where(keep, pair, jnp.zeros_like(pair))


def route_hot(routes_ref):
    experts = lax.broadcasted_iota(jnp.int32, (ROWS, EXPERTS), 1)
    return (routes_ref[...] == experts).astype(F32)


def token_slots(routes_ref, info_ref, hot):
    routed = segments(info_ref, 0)[:, :1] < DOCS - 1
    routed_hot = jnp.where(routed, hot, 0.0)
    rows = lax.broadcasted_iota(jnp.int32, (ROWS, ROWS), 0)
    columns = lax.broadcasted_iota(jnp.int32, (ROWS, ROWS), 1)
    earlier = dot((columns < rows).astype(BF), routed_hot.astype(BF))
    place = jnp.sum(routed_hot * earlier, axis=-1, keepdims=True).astype(jnp.int32)
    return jnp.where(routed, place, -1), routes_ref[...]


def slot_table(place, route, group, offset, count):
    lanes = lax.broadcasted_iota(jnp.int32, (ROWS, count), 1) % (EXPERTS * group)
    wanted = jnp.where(place >= 0, route * group + offset + place, -1)
    return (lanes == wanted).astype(BF)


def forward_attention(
    inputs_f, info_ref, routes_ref, weights, gains_ref, router_ref, bias_ref, outs
):
    lower = info_ref[1] == 0
    query, query_o, key, key_o, value, value_o, out, out_o = weights
    n1_ref, q_ref, k_ref, v_ref, mixed_ref, resid_ref, n2_ref, prob_ref, gate_ref = outs
    scale = lax.rsqrt(jnp.mean(inputs_f * inputs_f, axis=-1, keepdims=True) + norm_eps)
    normed = (inputs_f * scale * gains_ref[0:1, :]).astype(BF)
    n1_ref[...] = normed
    q_ref[...] = project(normed, lower, query, query_o).astype(BF)
    k_ref[...] = project(normed, lower, key, key_o).astype(BF)
    v_ref[...] = project(normed, lower, value, value_o).astype(BF)
    mask = attend_mask(info_ref)
    first = pair_masks()
    for pair in range(HEADS // 2):
        here = slice(pair * 128, pair * 128 + 128)
        q_pair, k_pair, v_pair = q_ref[:, here], k_ref[:, here], v_ref[:, here]
        made = []
        for member in range(2):
            prob = head_prob(only(first, member, q_pair), k_pair, bias_ref, 2 * pair + member, mask)
            made.append(dot(prob.astype(BF), v_pair))
        mixed_ref[:, here] = jnp.where(first, made[0], made[1]).astype(BF)
    resid = inputs_f + project(mixed_ref[...], lower, out, out_o)
    resid_ref[...] = resid
    scale = lax.rsqrt(jnp.mean(resid * resid, axis=-1, keepdims=True) + norm_eps)
    normed_two = (resid * scale * gains_ref[1:2, :]).astype(BF)
    n2_ref[...] = normed_two
    logits = dot(normed_two, router_ref[...])
    logit_exp = jnp.exp(logits - jnp.max(logits, axis=-1, keepdims=True))
    prob = logit_exp / jnp.sum(logit_exp, axis=-1, keepdims=True)
    prob_ref[...] = prob
    hot = route_hot(routes_ref)
    gate = jnp.sum(prob * hot, axis=-1, keepdims=True)
    gate_ref[...] = gate
    place, route = token_slots(routes_ref, info_ref, hot)
    return normed_two, gate, place, route


def first_forward_kernel(info_ref, routes_ref, x_ref, *refs):
    weights, (gains_ref, router_ref, bias_ref), outs = refs[:8], refs[8:11], refs[11:20]
    send_ref = refs[20]
    normed_two, _, place, route = forward_attention(
        x_ref[...].astype(F32), info_ref, routes_ref, weights, gains_ref, router_ref, bias_ref, outs
    )
    table = slot_table(place, route, SLOTS, 0, EXPERTS * SLOTS)
    rows = t_dot(table, normed_two).astype(BF)
    send_ref[: EXPERTS * SLOTS, :] = rows
    send_ref[EXPERTS * SLOTS :, :] = rows


def second_forward_kernel(
    info_ref, routes_ref, routes_before_ref, resid_ref, gate_ref, back_ref, cot_ref, *refs
):
    weights, (gains_ref, router_ref, bias_ref), outs = refs[:8], refs[8:11], refs[11:20]
    send_ref, x_ref, combined_ref = refs[20:23]
    place, route = token_slots(routes_before_ref, info_ref, route_hot(routes_before_ref))
    combined = dot(slot_table(place, route, SLOTS, 0, 2 * EXPERTS * SLOTS), back_ref[...])
    combined_ref[...] = combined
    inputs = (resid_ref[...] + gate_ref[...] * combined).astype(BF)
    x_ref[...] = inputs
    normed_two, gate, place, route = forward_attention(
        inputs.astype(F32), info_ref, routes_ref, weights, gains_ref, router_ref, bias_ref, outs
    )
    made_grad = (gate * cot_ref[...].astype(F32)).astype(BF)
    group = 2 * SLOTS
    rows = t_dot(slot_table(place, route, group, 0, EXPERTS * group), normed_two)
    rows = rows + t_dot(slot_table(place, route, group, SLOTS, EXPERTS * group), made_grad)
    rows = rows.astype(BF)
    send_ref[: EXPERTS * group, :] = rows
    send_ref[EXPERTS * group :, :] = rows


def backward_attention(
    grad_out,
    combined,
    grad_two_rows,
    info_ref,
    routes_ref,
    kept,
    weights,
    gains_ref,
    router_ref,
    bias_ref,
    outs,
):
    lower = info_ref[1] == 0
    query, query_o, key, key_o, value, value_o, out, out_o = weights
    x_ref, q_ref, k_ref, v_ref, resid_ref, n2_ref, prob_ref, gate_ref = kept
    grads_ref, input_grad_ref, gain_grad_ref, router_grad_ref, diag_ref = outs
    hot = route_hot(routes_ref)
    grad_gate = jnp.sum(grad_out * combined, axis=-1, keepdims=True)
    grad_logits = (grad_gate * gate_ref[...] * (hot - prob_ref[...])).astype(BF)
    router_grad_ref[...] = t_dot(grad_logits, n2_ref[...])
    grad_two = dot_t(grad_logits, router_ref[...]) + grad_two_rows
    resid = resid_ref[...]
    scale = lax.rsqrt(jnp.mean(resid * resid, axis=-1, keepdims=True) + norm_eps)
    gain_grad_ref[1:2, :] = jnp.sum(grad_two * resid * scale, axis=0, keepdims=True)
    gained = gains_ref[1:2, :] * grad_two
    grad_resid = (
        grad_out
        + scale * gained
        - resid * (scale * scale * scale) * jnp.mean(resid * gained, axis=-1, keepdims=True)
    )
    grad_attn = grad_resid.astype(BF)
    grads_ref[3] = grad_attn
    grad_mixed = project_back(grad_attn, lower, out, out_o).astype(BF)
    mask = attend_mask(info_ref)
    first = pair_masks()
    rows = lax.broadcasted_iota(jnp.int32, (ROWS, ROWS), 0)
    columns = lax.broadcasted_iota(jnp.int32, (ROWS, ROWS), 1)
    flip = (rows + columns == ROWS - 1).astype(BF)
    for pair in range(HEADS // 2):
        here = slice(pair * 128, pair * 128 + 128)
        q_pair, k_pair, v_pair = q_ref[:, here], k_ref[:, here], v_ref[:, here]
        mixed_pair = grad_mixed[:, here]
        made = []
        for member in range(2):
            head = 2 * pair + member
            prob = head_prob(only(first, member, q_pair), k_pair, bias_ref, head, mask)
            grad_prob = dot_t(only(first, member, mixed_pair), v_pair)
            grad_value = t_dot(prob.astype(BF), mixed_pair)
            grad_scores = prob * (grad_prob - jnp.sum(prob * grad_prob, axis=-1, keepdims=True))
            grad_scores = grad_scores.astype(BF)
            turned = pltpu.roll(
                dot(flip, grad_scores), 0, axis=1, stride=1, stride_axis=0
            )
            diag_ref[head : head + 1, :] = jnp.sum(turned, axis=0, keepdims=True)
            made.append(
                (
                    dot(grad_scores, k_pair) * HEAD_DIM ** (-0.5),
                    t_dot(grad_scores, q_pair) * HEAD_DIM ** (-0.5),
                    grad_value,
                )
            )
        for number in range(3):
            grads_ref[number, :, here] = jnp.where(
                first, made[0][number], made[1][number]
            ).astype(BF)
    diag_ref[HEADS:, :] = jnp.zeros((16 - HEADS, ROWS), F32)
    grad_one = project_back(grads_ref[0], lower, query, query_o)
    grad_one = grad_one + project_back(grads_ref[1], lower, key, key_o)
    grad_one = grad_one + project_back(grads_ref[2], lower, value, value_o)
    inputs = x_ref[...].astype(F32)
    scale = lax.rsqrt(jnp.mean(inputs * inputs, axis=-1, keepdims=True) + norm_eps)
    gain_grad_ref[0:1, :] = jnp.sum(grad_one * inputs * scale, axis=0, keepdims=True)
    gain_grad_ref[2:, :] = jnp.zeros((6, WIDTH), F32)
    gained = gains_ref[0:1, :] * grad_one
    input_grad = (
        grad_resid
        + scale * gained
        - inputs * (scale * scale * scale) * jnp.mean(inputs * gained, axis=-1, keepdims=True)
    ).astype(BF)
    input_grad_ref[...] = input_grad
    return input_grad


def last_backward_kernel(
    info_ref, routes_ref, routes_before_ref, gate_before_ref, cot_ref, back_ref, *refs
):
    kept, weights, (gains_ref, router_ref, bias_ref) = refs[:8], refs[8:16], refs[16:19]
    outs, result_ref, send_ref = refs[19:24], refs[24], refs[25]
    gate_ref, resid_ref = kept[7], kept[4]
    place, route = token_slots(routes_ref, info_ref, route_hot(routes_ref))
    group = 2 * SLOTS
    combined = dot(slot_table(place, route, group, 0, 2 * EXPERTS * group), back_ref[...])
    grad_rows = dot(slot_table(place, route, group, SLOTS, 2 * EXPERTS * group), back_ref[...])
    result_ref[...] = (resid_ref[...] + gate_ref[...] * combined).astype(BF)
    input_grad = backward_attention(
        cot_ref[...].astype(F32),
        combined,
        grad_rows,
        info_ref,
        routes_ref,
        kept,
        weights,
        gains_ref,
        router_ref,
        bias_ref,
        outs,
    )
    made_grad = (gate_before_ref[...] * input_grad.astype(F32)).astype(BF)
    place, route = token_slots(routes_before_ref, info_ref, route_hot(routes_before_ref))
    rows = t_dot(slot_table(place, route, SLOTS, 0, EXPERTS * SLOTS), made_grad).astype(BF)
    send_ref[: EXPERTS * SLOTS, :] = rows
    send_ref[EXPERTS * SLOTS :, :] = rows


def first_backward_kernel(info_ref, routes_ref, combined_ref, grad_ref, back_ref, *refs):
    kept, weights, (gains_ref, router_ref, bias_ref) = refs[:8], refs[8:16], refs[16:19]
    outs = refs[19:24]
    place, route = token_slots(routes_ref, info_ref, route_hot(routes_ref))
    grad_rows = dot(slot_table(place, route, SLOTS, 0, 2 * EXPERTS * SLOTS), back_ref[...])
    backward_attention(
        grad_ref[...].astype(F32),
        combined_ref[...],
        grad_rows,
        info_ref,
        routes_ref,
        kept,
        weights,
        gains_ref,
        router_ref,
        bias_ref,
        outs,
    )


def weight_grad_kernel(info_ref, n1_ref, mixed_ref, grads_ref, keep_ref, send_ref):
    lower = info_ref[0] == 0
    for number in range(4):
        left_ref = mixed_ref if number == 3 else n1_ref
        kept, sent = in_halves(grads_ref[number], lower)
        for half in range(2):
            left = left_ref[:, half * HALF : half * HALF + HALF]
            keep_ref[half, number] = t_dot(left, kept).astype(BF)
            send_ref[half, number] = t_dot(left, sent).astype(BF)


def gelu_parts(hidden):
    slope = np.sqrt(2 / np.pi).astype(np.float32)
    square = hidden * hidden
    curve = jnp.tanh(slope * hidden * (1.0 + 0.044715 * square))
    gate = 0.5 * (1.0 + curve)
    grad = gate + 0.5 * hidden * (1.0 - curve * curve) * slope * (1.0 + 3 * 0.044715 * square)
    return hidden * gate, grad


def expert_forward_kernel(rows_ref, in_ref, out_ref, made_ref, made_sum):
    step = pl.program_id(0)
    act, _ = gelu_parts(dot(rows_ref[...], in_ref[...]))
    made = dot(act.astype(BF), out_ref[...])

    @pl.when(step == 0)
    def _():
        made_sum[...] = made

    @pl.when(step > 0)
    def _():
        made_sum[...] += made

    @pl.when(step == pl.num_programs(0) - 1)
    def _():
        made_ref[...] = made_sum[...].astype(BF)


def expert_backward_kernel(
    rows_ref, grad_ref, in_ref, out_ref, back_ref, in_grad_ref, out_grad_ref, rows_sum
):
    step = pl.program_id(0)
    act, slope = gelu_parts(dot(rows_ref[...], in_ref[...]))
    grad_pre = (slope * dot_t(grad_ref[...], out_ref[...])).astype(BF)
    out_grad_ref[...] = t_dot(act.astype(BF), grad_ref[...]).astype(BF)
    in_grad_ref[...] = t_dot(rows_ref[...], grad_pre).astype(BF)
    back = dot_t(grad_pre, in_ref[...])

    @pl.when(step == 0)
    def _():
        rows_sum[...] = back

    @pl.when(step > 0)
    def _():
        rows_sum[...] += back

    @pl.when(step == pl.num_programs(0) - 1)
    def _():
        back_ref[...] = rows_sum[...].astype(BF)


def expert_both_kernel(
    both_ref, in_ref, out_ref, back_ref, in_grad_ref, out_grad_ref, rows, grads, made_sum, rows_sum
):
    step = pl.program_id(0)
    pieces = both_ref.shape[0] // (2 * SLOTS)

    @pl.when(step == 0)
    def _():
        for piece in range(0, pieces, 2):
            block = both_ref[piece * 16 : piece * 16 + 32, :].astype(F32)
            rows[piece * 8 : piece * 8 + 16, :] = jnp.concatenate(
                [block[0:8], block[16:24]], axis=0
            ).astype(BF)
            grads[piece * 8 : piece * 8 + 16, :] = jnp.concatenate(
                [block[8:16], block[24:32]], axis=0
            ).astype(BF)

    act, slope = gelu_parts(dot(rows[...], in_ref[...]))
    act = act.astype(BF)
    grad_pre = (slope * dot_t(grads[...], out_ref[...])).astype(BF)
    out_grad_ref[...] = t_dot(act, grads[...]).astype(BF)
    in_grad_ref[...] = t_dot(rows[...], grad_pre).astype(BF)
    made = dot(act, out_ref[...])
    back = dot_t(grad_pre, in_ref[...])

    @pl.when(step == 0)
    def _():
        made_sum[...] = made
        rows_sum[...] = back

    @pl.when(step > 0)
    def _():
        made_sum[...] += made
        rows_sum[...] += back

    @pl.when(step == pl.num_programs(0) - 1)
    def _():
        for piece in range(pieces):
            back_ref[piece * 16 : piece * 16 + 16, :] = jnp.concatenate(
                [made_sum[piece * 8 : piece * 8 + 8], rows_sum[piece * 8 : piece * 8 + 8]], axis=0
            ).astype(BF)


def shape(dims, kind=BF):
    return jax.ShapeDtypeStruct(dims, kind)


SMEM = pl.BlockSpec(memory_space=pltpu.SMEM)
VMEM = pl.BlockSpec(memory_space=pltpu.VMEM)


def whole_call(kernel, out_shape, name, limit, *operands):
    return pl.pallas_call(
        kernel,
        out_shape=out_shape,
        in_specs=[SMEM] + [VMEM] * (len(operands) - 1),
        out_specs=[VMEM] * len(out_shape),
        name=name,
        compiler_params=pltpu.CompilerParams(vmem_limit_bytes=limit * MIB),
    )(*operands)


BLOCK = 256


def expert_call(kernel, row_arrays, w_in, w_out, out_shape, scratch, name):
    hidden = w_in.shape[1]
    fixed = lambda array: pl.BlockSpec(array.shape, lambda step: (0, 0))
    in_block = pl.BlockSpec((WIDTH, BLOCK), lambda step: (0, step))
    out_block = pl.BlockSpec((BLOCK, WIDTH), lambda step: (step, 0))
    out_specs = [fixed(out_shape[0])] + [in_block, out_block][: len(out_shape) - 1]
    return pl.pallas_call(
        kernel,
        grid=(hidden // BLOCK,),
        out_shape=out_shape,
        in_specs=[fixed(array) for array in row_arrays] + [in_block, out_block],
        out_specs=out_specs,
        scratch_shapes=scratch,
        name=name,
        compiler_params=pltpu.CompilerParams(vmem_limit_bytes=40 * MIB),
    )(*row_arrays, w_in, w_out)


def forward_shapes():
    tokens = shape((ROWS, WIDTH))
    return [
        tokens,
        tokens,
        tokens,
        tokens,
        tokens,
        shape((ROWS, WIDTH), F32),
        tokens,
        shape((ROWS, EXPERTS), F32),
        shape((ROWS, 1), F32),
    ]


def backward_shapes():
    return [
        shape((4, ROWS, WIDTH)),
        shape((ROWS, WIDTH)),
        shape((8, WIDTH), F32),
        shape((EXPERTS, WIDTH), F32),
        shape((16, ROWS), F32),
    ]


def exchange(block):
    dims = block.shape
    pieces = lax.all_to_all(
        block.reshape((64, dims[0] // 64, dims[1])), BOTH, split_axis=0, concat_axis=0, tiled=True
    )
    return pieces.reshape(dims)


def shards(
    block_in,
    cotangent,
    lengths,
    routes,
    query_weight,
    key_weight,
    value_weight,
    out_weight,
    attn_gain,
    moe_gain,
    router,
    rel_table,
    expert_in,
    expert_out,
):
    core = lax.axis_index("section")
    half = lax.axis_index("shard")
    first_core = core == 0
    lower = half == 0

    def pick(left, right):
        return jnp.where(first_core, left, right)

    small = jnp.concatenate(
        [
            attn_gain.reshape(-1),
            moe_gain.reshape(-1),
            router.reshape(-1),
            rel_table.reshape(-1),
            jnp.zeros((64,), BF),
        ]
    ).reshape(-1, 128)
    small_other = lax.ppermute(small, "shard", [(0, 1), (1, 0)])
    small_full = jnp.stack([jnp.where(lower, small, small_other), jnp.where(lower, small_other, small)])
    small_swapped = swap(small_full)

    weights_own = [w[0] for w in (query_weight, key_weight, value_weight, out_weight)]
    weights_swapped = [swap(w) for w in weights_own]

    def across(block, section):
        base = 2 * section
        return lax.ppermute(
            block, ("section", "shard"), [(base, base + 1), (base + 1, base)]
        )

    weights = [[], []]
    arrived = [across(w, 0) for w in weights_own]
    others = [pick(w, swap(w)) for w in arrived]
    for own, swapped, other in zip(weights_own, weights_swapped, others):
        weights[0] += [pick(own, swapped), other]
    later = lax.optimization_barrier(tuple(weights_own) + (arrived[3],))[:4]
    arrived = [across(w, 1) for w in later]
    others = [pick(swap(w), w) for w in arrived]
    for own, swapped, other in zip(weights_own, weights_swapped, others):
        weights[1] += [pick(swapped, own), other]

    experts_own = [expert_in[0, 0], expert_out[0, 0]]
    experts_swapped = [swap(w) for w in experts_own]
    experts = [
        [pick(o, s) for o, s in zip(experts_own, experts_swapped)],
        [pick(s, o) for o, s in zip(experts_own, experts_swapped)],
    ]

    bucket_hot = np.eye(NB, dtype=np.float32)[bucket_of_distance(ROWS)]
    turned = bucket_hot[(-np.arange(ROWS)) % ROWS]

    def unpack(packed):
        flat = packed.reshape(2, -1)
        gain_one = flat[:, :HALF].reshape(1, WIDTH)
        gain_two = flat[:, HALF:WIDTH].reshape(1, WIDTH)
        router_full = flat[:, WIDTH : WIDTH + HALF * EXPERTS].reshape(WIDTH, EXPERTS)
        table_full = flat[:, WIDTH + HALF * EXPERTS :][:, : NB // 2 * HEADS].reshape(NB, HEADS)
        gains = jnp.concatenate([gain_one, gain_two, jnp.zeros((6, WIDTH), BF)]).astype(F32)
        bias = lax.dot_general(
            table_full,
            jnp.asarray(turned, BF),
            (((0,), (1,)), ((), ())),
            preferred_element_type=F32,
        )
        return [gains, router_full, jnp.pad(bias, ((0, 4), (0, 0)))]

    params = [
        unpack(pick(small_full, small_swapped)),
        unpack(pick(small_swapped, small_full)),
    ]

    routes_other = swap(pick(routes[0, 1], routes[0, 0]))
    routes_mine = pick(routes[0, 0], routes[0, 1])
    layer_routes = [pick(routes_mine, routes_other), pick(routes_other, routes_mine)]
    runs = pick(lengths[0, 0], lengths[1, 0])
    info = jnp.concatenate(
        [jnp.stack([core, half]).astype(jnp.int32), jnp.cumsum(runs, dtype=jnp.int32)]
    )
    inputs = pick(block_in[0], block_in[1])
    outer = pick(cotangent[0], cotangent[1])

    *kept0, send = whole_call(
        first_forward_kernel,
        forward_shapes() + [shape((512, WIDTH))],
        "attend_first",
        32,
        info,
        layer_routes[0],
        inputs,
        *weights[0],
        *params[0],
    )
    rows0 = exchange(send)
    (made,) = expert_call(
        expert_forward_kernel,
        [rows0],
        *experts[0],
        [shape((512, WIDTH))],
        [pltpu.VMEM((512, WIDTH), F32)],
        "expert_first",
    )
    back = exchange(made)
    n10, q0, k0, v0, mixed0, resid0, n20, prob0, gate0 = kept0
    *kept1, send, middle, combined0 = whole_call(
        second_forward_kernel,
        forward_shapes()
        + [shape((1024, WIDTH)), shape((ROWS, WIDTH)), shape((ROWS, WIDTH), F32)],
        "attend_second",
        36,
        info,
        layer_routes[1],
        layer_routes[0],
        resid0,
        gate0,
        back,
        outer,
        *weights[1],
        *params[1],
    )
    both = exchange(send)
    grad_shapes = [shape(experts_own[0].shape), shape(experts_own[1].shape)]
    back, in_grad1, out_grad1 = expert_call(
        expert_both_kernel,
        [both],
        *experts[1],
        [shape((1024, WIDTH))] + grad_shapes,
        [pltpu.VMEM((512, WIDTH), BF)] * 2 + [pltpu.VMEM((512, WIDTH), F32)] * 2,
        "expert_second",
    )
    back = exchange(back)
    n11, q1, k1, v1, mixed1, resid1, n21, prob1, gate1 = kept1
    *grads1, result, send = whole_call(
        last_backward_kernel,
        backward_shapes() + [shape((ROWS, WIDTH)), shape((512, WIDTH))],
        "attend_second_back",
        36,
        info,
        layer_routes[1],
        layer_routes[0],
        gate0,
        outer,
        back,
        middle,
        q1,
        k1,
        v1,
        resid1,
        n21,
        prob1,
        gate1,
        *weights[1],
        *params[1],
    )
    made_grads = exchange(send)
    back, in_grad0, out_grad0 = expert_call(
        expert_backward_kernel,
        [rows0, made_grads],
        *experts[0],
        [shape((512, WIDTH))] + grad_shapes,
        [pltpu.VMEM((512, WIDTH), F32)],
        "expert_first_back",
    )
    back = exchange(back)
    grads0 = whole_call(
        first_backward_kernel,
        backward_shapes(),
        "attend_first_back",
        36,
        info,
        layer_routes[0],
        combined0,
        grads1[1],
        back,
        inputs,
        q0,
        k0,
        v0,
        resid0,
        n20,
        prob0,
        gate0,
        *weights[0],
        *params[0],
    )

    def small_rows(gain_grad, router_grad, diag):
        table = lax.dot_general(
            diag[:HEADS],
            jnp.asarray(bucket_hot[::-1]),
            (((1,), (0,)), ((), ())),
            precision=lax.Precision.HIGHEST,
            preferred_element_type=F32,
        )
        table = jnp.transpose(table.reshape(HEADS, 2, NB // 2), (1, 0, 2))
        table = jnp.pad(table, ((0, 0), (0, 0), (0, HALF - NB // 2)))
        gains = jnp.transpose(gain_grad[:2].reshape(2, 2, HALF), (1, 0, 2))
        others = jnp.concatenate([gains, table, jnp.zeros((2, EXPERTS - HEADS - 2, HALF), F32)], axis=1)
        routers = jnp.transpose(router_grad.reshape(EXPERTS, 2, HALF), (1, 0, 2))
        return jnp.stack([routers, others], axis=2).astype(BF).reshape(64, 2, HALF)

    def reduce_layer(n1, mixed, grads):
        keep, send = whole_call(
            weight_grad_kernel,
            [shape((2, 4, HALF, HALF))] * 2,
            "weight_grads",
            24,
            info,
            n1,
            mixed,
            grads[0],
        )
        big = (keep.astype(F32) + swap(send).astype(F32)).astype(BF).reshape(64, 48, HALF)
        extra = jnp.pad(small_rows(*grads[2:]), ((0, 0), (0, 6), (0, 0)))
        pieces = jnp.concatenate([big, extra], axis=1)
        pieces = lax.all_to_all(pieces, BOTH, split_axis=0, concat_axis=0, tiled=True)
        total = jnp.sum(pieces.astype(F32), axis=0).astype(BF)
        spread = jnp.broadcast_to(total[None], (32,) + total.shape)
        return lax.all_to_all(spread, "replica", split_axis=0, concat_axis=0, tiled=True)

    whole1 = reduce_layer(n11, mixed1, grads1)
    whole0 = reduce_layer(n10, mixed0, grads0)
    kept = pick(whole0, whole1)
    got = swap(pick(whole1, whole0))
    left, right = pick(kept, got), pick(got, kept)
    full = jnp.concatenate([left[:, :48], right[:, :48]], axis=2).astype(F32)
    full = full.reshape(4, HALF, WIDTH)
    smalls = kept[:, 48:50].astype(F32) + got[:, 48:50].astype(F32)
    router_grad = jnp.transpose(smalls[:, 0], (1, 0))
    table_grad = jnp.transpose(smalls[2 : 2 + HEADS, 1, : NB // 2], (1, 0))

    def expert_total(first, second):
        received = swap(pick(second, first))
        return pick(first, second).astype(F32) + received.astype(F32)

    def by_micro(first, second):
        mine, theirs = pick(first, second), swap(pick(second, first))
        return jnp.stack([pick(mine, theirs), pick(theirs, mine)])

    section_out = by_micro(middle, result)
    input_grad = by_micro(grads0[1], grads1[1])
    return (
        section_out[None],
        input_grad[None],
        full[0][None],
        full[1][None],
        full[2][None],
        full[3][None],
        smalls[0, 1][None],
        smalls[1, 1][None],
        router_grad[None],
        table_grad[None],
        expert_total(in_grad0, in_grad1)[None, None],
        expert_total(out_grad0, out_grad1)[None, None],
    )


def solution(mesh):
    in_specs = (
        P(None, ("shard", "replica"), None),
        P(None, ("shard", "replica"), None),
        P(None, ("shard", "replica"), None),
        P("section", None, ("shard", "replica"), None),
        P("section", "shard", None),
        P("section", "shard", None),
        P("section", "shard", None),
        P("section", "shard", None),
        P("section", "shard"),
        P("section", "shard"),
        P("section", "shard", None),
        P("section", "shard", None),
        P("section", "replica", None, "shard"),
        P("section", "replica", "shard", None),
    )
    out_specs = (
        P("section", None, ("shard", "replica"), None),
        P("section", None, ("shard", "replica"), None),
        P("section", "shard", None),
        P("section", "shard", None),
        P("section", "shard", None),
        P("section", "shard", None),
        P("section", "shard"),
        P("section", "shard"),
        P("section", "shard", None),
        P("section", "shard", None),
        P("section", "replica", None, "shard"),
        P("section", "replica", "shard", None),
    )
    return jax.shard_map(shards, mesh=mesh, in_specs=in_specs, out_specs=out_specs, check_vma=False)
```

```python
import jax
import jax.numpy as jnp
import numpy as np
from jax import lax
from jax.experimental import pallas as pl
from jax.experimental.pallas import tpu as pltpu
from jax.sharding import PartitionSpec as P

HEADS = 12
HEAD_DIM = 64
NB = 32
MAXDIST = 128
DOCS = 4
ROWS = 128
WIDTH = 768
HALF = 384
EXPERTS = 32
SLOTS = 8
MIB = 1024 * 1024
BF = jnp.bfloat16
F32 = jnp.float32

norm_eps = 1e-06
BOTH = ("shard", "replica")


def bucket_of_distance(length):
    distance = np.arange(length)
    exact_count = NB // 2
    log_ratio = np.log(np.maximum(distance, 1) / exact_count) / np.log(MAXDIST / exact_count)
    far_bucket = exact_count + np.floor(log_ratio * (NB - exact_count)).astype(np.int32)
    return np.where(distance < exact_count, distance, np.minimum(far_bucket, NB - 1)).astype(
        np.int32
    )


def swap(block):
    return lax.ppermute(block, "section", [(0, 1), (1, 0)])


def dot(left, right):
    return jnp.dot(left, right, preferred_element_type=F32)


def dot_t(left, right):
    return lax.dot_general(left, right, (((1,), (1,)), ((), ())), preferred_element_type=F32)


def t_dot(left, right):
    return lax.dot_general(left, right, (((0,), (0,)), ((), ())), preferred_element_type=F32)


def in_halves(matrix, lower):
    first, second = matrix[:, :HALF], matrix[:, HALF:]
    return jnp.where(lower, first, second), jnp.where(lower, second, first)


PARTS = 4


class Weights:
    def __init__(self, info_ref, layer, sources, buffers, sems, order):
        self.sources, self.buffers, self.sems, self.here = sources, buffers, sems, set()
        for matrix in order:
            for number in (2 * matrix, 2 * matrix + 1):

                @pl.when(info_ref[0] == layer)
                def _():
                    self.copy(number, 0).start()

                @pl.when(info_ref[0] != layer)
                def _():
                    self.copy(number, 1).start()

    def copy(self, number, place):
        return pltpu.make_async_copy(
            self.sources[2 * number + place], self.buffers.at[number], self.sems.at[number]
        )

    def take(self, number):
        if number not in self.here:
            self.here.add(number)
            self.copy(number, 0).wait()
        return self.buffers[number]

    def pair(self, matrix):
        return self.take(2 * matrix), self.take(2 * matrix + 1)


def project(matrix, lower, halves):
    own_part, other_part = in_halves(matrix, lower)
    return dot(own_part, halves[0]) + dot(other_part, halves[1])


def project_back(matrix, lower, halves):
    own_part = dot_t(matrix, halves[0])
    other_part = dot_t(matrix, halves[1])
    return jnp.concatenate(
        [jnp.where(lower, own_part, other_part), jnp.where(lower, other_part, own_part)], axis=1
    )


def segments(info_ref, axis):
    places = lax.broadcasted_iota(jnp.int32, (ROWS, ROWS), axis)
    found = jnp.zeros((ROWS, ROWS), jnp.int32)
    for run in range(DOCS):
        found = found + (places >= info_ref[2 + run]).astype(jnp.int32)
    return found


def attend_mask(info_ref):
    rows = lax.broadcasted_iota(jnp.int32, (ROWS, ROWS), 0)
    columns = lax.broadcasted_iota(jnp.int32, (ROWS, ROWS), 1)
    return (segments(info_ref, 0) == segments(info_ref, 1)) & (columns <= rows)


def head_prob(queries_own, key_pair, bias_ref, head, mask):
    bias = pltpu.roll(
        jnp.broadcast_to(bias_ref[head + 2 : head + 3, :], (ROWS, ROWS)),
        0,
        axis=1,
        stride=1,
        stride_axis=0,
    )
    scores = dot_t(queries_own, key_pair) * HEAD_DIM ** (-0.5) + bias
    scores = jnp.where(mask, scores, -1e30)
    exponent = jnp.exp(scores - jnp.max(scores, axis=-1, keepdims=True))
    return exponent / jnp.sum(exponent, axis=-1, keepdims=True)


def pair_masks():
    lane = lax.broadcasted_iota(jnp.int32, (ROWS, 2 * HEAD_DIM), 1)
    return lane < HEAD_DIM


def only(first, head_in_pair, pair):
    keep = first if head_in_pair == 0 else jnp.logical_not(first)
    return jnp.where(keep, pair, jnp.zeros_like(pair))


def route_hot(routes_ref):
    experts = lax.broadcasted_iota(jnp.int32, (ROWS, EXPERTS), 1)
    return (routes_ref[...] == experts).astype(F32)


def token_slots(routes_ref, info_ref, hot):
    routed = segments(info_ref, 0)[:, :1] < DOCS - 1
    routed_hot = jnp.where(routed, hot, 0.0)
    rows = lax.broadcasted_iota(jnp.int32, (ROWS, ROWS), 0)
    columns = lax.broadcasted_iota(jnp.int32, (ROWS, ROWS), 1)
    earlier = dot((columns < rows).astype(BF), routed_hot.astype(BF))
    place = jnp.sum(routed_hot * earlier, axis=-1, keepdims=True).astype(jnp.int32)
    return jnp.where(routed, place, -1), routes_ref[...]


def slot_table(place, route, group, offset, count):
    lanes = lax.broadcasted_iota(jnp.int32, (ROWS, count), 1) % (EXPERTS * group)
    wanted = jnp.where(place >= 0, route * group + offset + place, -1)
    return (lanes == wanted).astype(BF)


def unpack_small(small_ref, hot_ref, lower, gains_ref, bias_ref):
    own, other = small_ref[0].astype(F32).T, small_ref[1].astype(F32).T
    gains = (own[32:40, :], other[32:40, :])
    gains_ref[...] = jnp.concatenate(
        [jnp.where(lower, gains[0], gains[1]), jnp.where(lower, gains[1], gains[0])], axis=1
    )
    low_hot, high_hot = hot_ref[: NB // 2, :], hot_ref[NB // 2 :, :]
    bias = dot(own[32:48, : NB // 2].astype(BF), jnp.where(lower, low_hot, high_hot))
    bias = bias + dot(other[32:48, : NB // 2].astype(BF), jnp.where(lower, high_hot, low_hot))
    bias_ref[...] = bias


def forward_attention(inputs_f, info_ref, routes_ref, weights, small_ref, hot_ref, outs):
    lower = info_ref[1] == 0
    n1_ref, q_ref, k_ref, v_ref, mixed_ref, resid_ref, n2_ref, prob_ref, gate_ref = outs[:9]
    gains_ref, bias_ref = outs[9:]
    unpack_small(small_ref, hot_ref, lower, gains_ref, bias_ref)
    scale = lax.rsqrt(jnp.mean(inputs_f * inputs_f, axis=-1, keepdims=True) + norm_eps)
    normed = (inputs_f * scale * gains_ref[0:1, :]).astype(BF)
    n1_ref[...] = normed
    q_ref[...] = project(normed, lower, weights.pair(0)).astype(BF)
    k_ref[...] = project(normed, lower, weights.pair(1)).astype(BF)
    v_ref[...] = project(normed, lower, weights.pair(2)).astype(BF)
    mask = attend_mask(info_ref)
    first = pair_masks()
    for pair in range(HEADS // 2):
        here = slice(pair * 128, pair * 128 + 128)
        q_pair, k_pair, v_pair = q_ref[:, here], k_ref[:, here], v_ref[:, here]
        made = []
        for member in range(2):
            prob = head_prob(only(first, member, q_pair), k_pair, bias_ref, 2 * pair + member, mask)
            made.append(dot(prob.astype(BF), v_pair))
        mixed_ref[:, here] = jnp.where(first, made[0], made[1]).astype(BF)
    resid = inputs_f + project(mixed_ref[...], lower, weights.pair(3))
    resid_ref[...] = resid
    scale = lax.rsqrt(jnp.mean(resid * resid, axis=-1, keepdims=True) + norm_eps)
    normed_two = (resid * scale * gains_ref[1:2, :]).astype(BF)
    n2_ref[...] = normed_two
    logits = project(normed_two, lower, (small_ref[0], small_ref[1]))[:, :EXPERTS]
    logit_exp = jnp.exp(logits - jnp.max(logits, axis=-1, keepdims=True))
    prob = logit_exp / jnp.sum(logit_exp, axis=-1, keepdims=True)
    prob_ref[...] = prob
    hot = route_hot(routes_ref)
    gate = jnp.sum(prob * hot, axis=-1, keepdims=True)
    gate_ref[...] = gate
    place, route = token_slots(routes_ref, info_ref, hot)
    return normed_two, gate, place, route


def first_forward_kernel(info_ref, routes_ref, x_ref, *refs):
    (small_ref, hot_ref), outs, send_ref = refs[16:18], refs[18:29], refs[29]
    weights = Weights(info_ref, 0, refs[:16], refs[30], refs[31], (0, 1, 2, 3))
    normed_two, _, place, route = forward_attention(
        x_ref[info_ref[0]].astype(F32), info_ref, routes_ref, weights, small_ref, hot_ref, outs
    )
    table = slot_table(place, route, SLOTS, 0, EXPERTS * SLOTS)
    rows = t_dot(table, normed_two).astype(BF)
    send_ref[: EXPERTS * SLOTS, :] = rows
    send_ref[EXPERTS * SLOTS :, :] = rows


def second_forward_kernel(
    info_ref, routes_ref, routes_before_ref, resid_ref, gate_ref, back_ref, cot_ref, *refs
):
    (small_ref, hot_ref), outs = refs[16:18], refs[18:29]
    send_ref, x_ref, combined_ref = refs[29:32]
    weights = Weights(info_ref, 1, refs[:16], refs[32], refs[33], (0, 1, 2, 3))
    place, route = token_slots(routes_before_ref, info_ref, route_hot(routes_before_ref))
    combined = dot(slot_table(place, route, SLOTS, 0, 2 * EXPERTS * SLOTS), back_ref[...])
    combined_ref[...] = combined
    inputs = (resid_ref[...] + gate_ref[...] * combined).astype(BF)
    x_ref[...] = inputs
    normed_two, gate, place, route = forward_attention(
        inputs.astype(F32), info_ref, routes_ref, weights, small_ref, hot_ref, outs
    )
    made_grad = (gate * cot_ref[info_ref[0]].astype(F32)).astype(BF)
    group = 2 * SLOTS
    rows = t_dot(slot_table(place, route, group, 0, EXPERTS * group), normed_two)
    rows = rows + t_dot(slot_table(place, route, group, SLOTS, EXPERTS * group), made_grad)
    rows = rows.astype(BF)
    send_ref[: EXPERTS * group, :] = rows
    send_ref[EXPERTS * group :, :] = rows


def backward_attention(
    inputs,
    grad_out,
    combined,
    grad_two_rows,
    info_ref,
    routes_ref,
    kept,
    weights,
    gains_ref,
    small_ref,
    bias_ref,
    outs,
):
    lower = info_ref[1] == 0
    q_ref, k_ref, v_ref, resid_ref, n2_ref, prob_ref, gate_ref = kept
    grads_ref, input_grad_ref, gain_grad_ref, router_grad_ref, diag_ref = outs
    hot = route_hot(routes_ref)
    grad_gate = jnp.sum(grad_out * combined, axis=-1, keepdims=True)
    grad_logits = (grad_gate * gate_ref[...] * (hot - prob_ref[...])).astype(BF)
    router_grad_ref[...] = t_dot(grad_logits, n2_ref[...])
    grad_logits = jnp.pad(grad_logits, ((0, 0), (0, ROWS - EXPERTS)))
    grad_two = project_back(grad_logits, lower, (small_ref[0], small_ref[1])) + grad_two_rows
    resid = resid_ref[...]
    scale = lax.rsqrt(jnp.mean(resid * resid, axis=-1, keepdims=True) + norm_eps)
    gain_grad_ref[1:2, :] = jnp.sum(grad_two * resid * scale, axis=0, keepdims=True)
    gained = gains_ref[1:2, :] * grad_two
    grad_resid = (
        grad_out
        + scale * gained
        - resid * (scale * scale * scale) * jnp.mean(resid * gained, axis=-1, keepdims=True)
    )
    grad_attn = grad_resid.astype(BF)
    grads_ref[3] = grad_attn
    grad_mixed = project_back(grad_attn, lower, weights.pair(3)).astype(BF)
    mask = attend_mask(info_ref)
    first = pair_masks()
    rows = lax.broadcasted_iota(jnp.int32, (ROWS, ROWS), 0)
    columns = lax.broadcasted_iota(jnp.int32, (ROWS, ROWS), 1)
    flip = (rows + columns == ROWS - 1).astype(BF)
    for pair in range(HEADS // 2):
        here = slice(pair * 128, pair * 128 + 128)
        q_pair, k_pair, v_pair = q_ref[:, here], k_ref[:, here], v_ref[:, here]
        mixed_pair = grad_mixed[:, here]
        made = []
        for member in range(2):
            head = 2 * pair + member
            prob = head_prob(only(first, member, q_pair), k_pair, bias_ref, head, mask)
            grad_prob = dot_t(only(first, member, mixed_pair), v_pair)
            grad_value = t_dot(prob.astype(BF), mixed_pair)
            grad_scores = prob * (grad_prob - jnp.sum(prob * grad_prob, axis=-1, keepdims=True))
            grad_scores = grad_scores.astype(BF)
            turned = pltpu.roll(
                dot(flip, grad_scores), 0, axis=1, stride=1, stride_axis=0
            )
            diag_ref[head : head + 1, :] = jnp.sum(turned, axis=0, keepdims=True)
            made.append(
                (
                    dot(grad_scores, k_pair) * HEAD_DIM ** (-0.5),
                    t_dot(grad_scores, q_pair) * HEAD_DIM ** (-0.5),
                    grad_value,
                )
            )
        for number in range(3):
            grads_ref[number, :, here] = jnp.where(
                first, made[0][number], made[1][number]
            ).astype(BF)
    diag_ref[HEADS:, :] = jnp.zeros((16 - HEADS, ROWS), F32)
    grad_one = project_back(grads_ref[0], lower, weights.pair(0))
    grad_one = grad_one + project_back(grads_ref[1], lower, weights.pair(1))
    grad_one = grad_one + project_back(grads_ref[2], lower, weights.pair(2))
    scale = lax.rsqrt(jnp.mean(inputs * inputs, axis=-1, keepdims=True) + norm_eps)
    gain_grad_ref[0:1, :] = jnp.sum(grad_one * inputs * scale, axis=0, keepdims=True)
    gain_grad_ref[2:, :] = jnp.zeros((6, WIDTH), F32)
    gained = gains_ref[0:1, :] * grad_one
    input_grad = (
        grad_resid
        + scale * gained
        - inputs * (scale * scale * scale) * jnp.mean(inputs * gained, axis=-1, keepdims=True)
    ).astype(BF)
    input_grad_ref[...] = input_grad
    return input_grad


def last_backward_kernel(
    info_ref, routes_ref, routes_before_ref, gate_before_ref, cot_ref, back_ref, *refs
):
    x_ref, kept, (gains_ref, small_ref, bias_ref) = refs[0], refs[1:8], refs[24:27]
    outs, result_ref, send_ref = refs[27:32], refs[32], refs[33]
    weights = Weights(info_ref, 1, refs[8:24], refs[34], refs[35], (3, 0, 1, 2))
    gate_ref, resid_ref = kept[6], kept[3]
    place, route = token_slots(routes_ref, info_ref, route_hot(routes_ref))
    group = 2 * SLOTS
    combined = dot(slot_table(place, route, group, 0, 2 * EXPERTS * group), back_ref[...])
    grad_rows = dot(slot_table(place, route, group, SLOTS, 2 * EXPERTS * group), back_ref[...])
    result_ref[...] = (resid_ref[...] + gate_ref[...] * combined).astype(BF)
    input_grad = backward_attention(
        x_ref[...].astype(F32),
        cot_ref[info_ref[0]].astype(F32),
        combined,
        grad_rows,
        info_ref,
        routes_ref,
        kept,
        weights,
        gains_ref,
        small_ref,
        bias_ref,
        outs,
    )
    made_grad = (gate_before_ref[...] * input_grad.astype(F32)).astype(BF)
    place, route = token_slots(routes_before_ref, info_ref, route_hot(routes_before_ref))
    rows = t_dot(slot_table(place, route, SLOTS, 0, EXPERTS * SLOTS), made_grad).astype(BF)
    send_ref[: EXPERTS * SLOTS, :] = rows
    send_ref[EXPERTS * SLOTS :, :] = rows


def first_backward_kernel(info_ref, routes_ref, combined_ref, grad_ref, back_ref, *refs):
    x_ref, kept, (gains_ref, small_ref, bias_ref) = refs[0], refs[1:8], refs[24:27]
    outs = refs[27:32]
    weights = Weights(info_ref, 0, refs[8:24], refs[32], refs[33], (3, 0, 1, 2))
    place, route = token_slots(routes_ref, info_ref, route_hot(routes_ref))
    grad_rows = dot(slot_table(place, route, SLOTS, 0, 2 * EXPERTS * SLOTS), back_ref[...])
    backward_attention(
        x_ref[info_ref[0]].astype(F32),
        grad_ref[...].astype(F32),
        combined_ref[...],
        grad_rows,
        info_ref,
        routes_ref,
        kept,
        weights,
        gains_ref,
        small_ref,
        bias_ref,
        outs,
    )


def weight_grad_kernel(info_ref, n1_ref, mixed_ref, grads_ref, keep_ref, send_ref):
    first_core = info_ref[0] == 0
    n1_turned, mixed_turned = n1_ref[...].T, mixed_ref[...].T
    for number in range(4):
        left = mixed_turned if number == 3 else n1_turned
        kept, sent = in_halves(grads_ref[number], first_core)
        for half in range(2):
            rows = left[half * HALF : half * HALF + HALF, :]
            keep_ref[half, number] = dot(rows, kept).astype(BF)
            send_ref[half, number] = dot(rows, sent).astype(BF)


def merge_kernel(*refs):
    far, out_far = refs[:5], refs[5]
    keep0_ref, got0_ref, keep1_ref, got1_ref, small_ref, out_ref, sems = refs[6:]
    near, size = refs[6:11], 64 // PARTS

    def copy(source, target, number, part):
        here = pl.ds(part * size, size)
        return pltpu.make_async_copy(source.at[here], target.at[here], sems.at[number, part])

    for part in range(PARTS):
        for number in range(5):
            copy(far[number], near[number], number, part).start()
    for part in range(PARTS):
        here = slice(part * size, part * size + size)
        for number in range(5):
            copy(far[number], near[number], number, part).wait()
        out_ref[here] = jnp.concatenate(
            [
                (keep0_ref[here].astype(F32) + got0_ref[here].astype(F32)).astype(BF),
                (keep1_ref[here].astype(F32) + got1_ref[here].astype(F32)).astype(BF),
                small_ref[here],
            ],
            axis=1,
        )
        copy(out_ref, out_far, 5, part).start()
    for part in range(PARTS):
        copy(out_ref, out_far, 5, part).wait()


def gelu_parts(hidden):
    slope = np.sqrt(2 / np.pi).astype(np.float32)
    square = hidden * hidden
    curve = jnp.tanh(slope * hidden * (1.0 + 0.044715 * square))
    gate = 0.5 * (1.0 + curve)
    grad = gate + 0.5 * hidden * (1.0 - curve * curve) * slope * (1.0 + 3 * 0.044715 * square)
    return hidden * gate, grad


class Chunks:
    def __init__(self, info_ref, layer, refs, win, wout, sems):
        self.info_ref, self.layer, self.refs = info_ref, layer, refs
        self.win, self.wout, self.sems = win, wout, sems
        for chunk in range(win.shape[0]):

            @pl.when(info_ref[0] == layer)
            def _():
                for copy in self.copies(0, chunk):
                    copy.start()

            @pl.when(info_ref[0] != layer)
            def _():
                for copy in self.copies(1, chunk):
                    copy.start()

    def copies(self, place, chunk):
        here = pl.ds(pl.multiple_of(chunk * BLOCK, BLOCK), BLOCK)
        return (
            pltpu.make_async_copy(
                self.refs[place].at[:, here], self.win.at[chunk], self.sems.at[0, chunk]
            ),
            pltpu.make_async_copy(
                self.refs[2 + place].at[here, :], self.wout.at[chunk], self.sems.at[1, chunk]
            ),
        )

    def take(self, chunk):
        for copy in self.copies(0, chunk):
            copy.wait()
        return self.win[chunk], self.wout[chunk]

    def grads_to(self, targets, din, dout, sems):
        self.targets, self.din, self.dout, self.out_sems = targets, din, dout, sems

    def grad_copies(self, place, chunk):
        here = pl.ds(pl.multiple_of(chunk * BLOCK, BLOCK), BLOCK)
        return (
            pltpu.make_async_copy(
                self.din.at[chunk], self.targets[2 * place].at[:, here], self.out_sems.at[0, chunk]
            ),
            pltpu.make_async_copy(
                self.dout.at[chunk],
                self.targets[2 * place + 1].at[here, :],
                self.out_sems.at[1, chunk],
            ),
        )

    def put(self, chunk):
        @pl.when(self.info_ref[0] == self.layer)
        def _():
            for copy in self.grad_copies(0, chunk):
                copy.start()

        @pl.when(self.info_ref[0] != self.layer)
        def _():
            for copy in self.grad_copies(1, chunk):
                copy.start()

    def finish(self):
        for chunk in range(self.din.shape[0]):
            for copy in self.grad_copies(0, chunk):
                copy.wait()


def expert_forward_kernel(info_ref, rows_ref, *refs):
    made_ref, win, wout, sems, made_sum = refs[4:]
    chunks = Chunks(info_ref, 0, refs[:4], win, wout, sems)
    made_sum[...] = jnp.zeros_like(made_sum)

    @pl.loop(0, win.shape[0])
    def _(chunk):
        w_in, w_out = chunks.take(chunk)
        act, _ = gelu_parts(dot(rows_ref[...], w_in))
        made_sum[...] += dot(act.astype(BF), w_out)

    made_ref[...] = made_sum[...].astype(BF)


def expert_backward_kernel(info_ref, rows_ref, grad_ref, *refs):
    back_ref, targets = refs[8], refs[9:13]
    win, wout, sems, din, dout, out_sems, rows_turned, rows_sum = refs[13:]
    chunks = Chunks(info_ref, 0, refs[:4], win, wout, sems)
    chunks.grads_to(targets, din, dout, out_sems)
    rows_sum[...] = jnp.zeros_like(rows_sum)
    rows_turned[...] = rows_ref[...].T

    @pl.loop(0, win.shape[0])
    def _(chunk):
        w_in, w_out = chunks.take(chunk)
        act, slope = gelu_parts(dot(rows_ref[...], w_in))
        grad_pre = (slope * dot_t(grad_ref[...], w_out)).astype(BF)
        dout[chunk] = t_dot(act.astype(BF), grad_ref[...]).astype(BF)
        din[chunk] = dot(rows_turned[...], grad_pre).astype(BF)
        chunks.put(chunk)
        rows_sum[...] += dot_t(grad_pre, w_in)

    back_ref[...] = rows_sum[...].astype(BF)
    chunks.finish()


def expert_both_kernel(info_ref, both_ref, *refs):
    back_ref, targets = refs[4], refs[5:9]
    win, wout, sems, din, dout, out_sems, rows, grads, rows_turned, made_sum, rows_sum = refs[9:]
    chunks = Chunks(info_ref, 1, refs[:4], win, wout, sems)
    chunks.grads_to(targets, din, dout, out_sems)
    pieces = both_ref.shape[0] // (2 * SLOTS)
    for piece in range(0, pieces, 2):
        block = both_ref[piece * 16 : piece * 16 + 32, :].astype(F32)
        rows[piece * 8 : piece * 8 + 16, :] = jnp.concatenate(
            [block[0:8], block[16:24]], axis=0
        ).astype(BF)
        grads[piece * 8 : piece * 8 + 16, :] = jnp.concatenate(
            [block[8:16], block[24:32]], axis=0
        ).astype(BF)
    made_sum[...] = jnp.zeros_like(made_sum)
    rows_sum[...] = jnp.zeros_like(rows_sum)
    rows_turned[...] = rows[...].T

    @pl.loop(0, win.shape[0])
    def _(chunk):
        w_in, w_out = chunks.take(chunk)
        act, slope = gelu_parts(dot(rows[...], w_in))
        act = act.astype(BF)
        grad_pre = (slope * dot_t(grads[...], w_out)).astype(BF)
        dout[chunk] = t_dot(act, grads[...]).astype(BF)
        din[chunk] = dot(rows_turned[...], grad_pre).astype(BF)
        chunks.put(chunk)
        made_sum[...] += dot(act, w_out)
        rows_sum[...] += dot_t(grad_pre, w_in)

    for piece in range(pieces):
        back_ref[piece * 16 : piece * 16 + 16, :] = jnp.concatenate(
            [made_sum[piece * 8 : piece * 8 + 8], rows_sum[piece * 8 : piece * 8 + 8]], axis=0
        ).astype(BF)
    chunks.finish()


def shape(dims, kind=BF):
    return jax.ShapeDtypeStruct(dims, kind)


SMEM = pl.BlockSpec(memory_space=pltpu.SMEM)
VMEM = pl.BlockSpec(memory_space=pltpu.VMEM)
HBM = pl.BlockSpec(memory_space=pltpu.HBM)
BLOCK = 512


def whole_call(kernel, out_shape, name, before, weights=(), after=(), **more):
    scratch = []
    if len(weights) == 16:
        scratch = [pltpu.VMEM((8, HALF, WIDTH), BF), pltpu.SemaphoreType.DMA((8,))]
    return pl.pallas_call(
        kernel,
        out_shape=out_shape,
        in_specs=[SMEM] + [VMEM] * (len(before) - 1) + [HBM] * len(weights) + [VMEM] * len(after),
        out_specs=more.pop("out_specs", [VMEM] * len(out_shape)),
        scratch_shapes=more.pop("scratch", scratch),
        name=name,
        compiler_params=pltpu.CompilerParams(vmem_limit_bytes=60 * MIB),
        **more,
    )(*before, *weights, *after)


def merge_call(sums, smalls):
    return pl.pallas_call(
        merge_kernel,
        out_shape=shape((64, 104, HALF)),
        in_specs=[HBM] * 5,
        out_specs=HBM,
        scratch_shapes=[pltpu.VMEM((64, 48, HALF), BF)] * 4
        + [pltpu.VMEM((64, 8, HALF), BF), pltpu.VMEM((64, 104, HALF), BF)]
        + [pltpu.SemaphoreType.DMA((6, PARTS))],
        name="merge_grads",
        compiler_params=pltpu.CompilerParams(vmem_limit_bytes=60 * MIB),
    )(*[part.reshape(64, 48, HALF) for part in sums], smalls)


def expert_scratch(hidden, grads):
    count = hidden // BLOCK
    moved = [
        pltpu.VMEM((count, WIDTH, BLOCK), BF),
        pltpu.VMEM((count, BLOCK, WIDTH), BF),
        pltpu.SemaphoreType.DMA((2, count)),
    ]
    return moved * (2 if grads else 1)


def forward_shapes():
    tokens = shape((ROWS, WIDTH))
    return [
        tokens,
        tokens,
        tokens,
        tokens,
        tokens,
        shape((ROWS, WIDTH), F32),
        tokens,
        shape((ROWS, EXPERTS), F32),
        shape((ROWS, 1), F32),
        shape((8, WIDTH), F32),
        shape((16, ROWS), F32),
    ]


def backward_shapes():
    return [
        shape((4, ROWS, WIDTH)),
        shape((ROWS, WIDTH)),
        shape((8, WIDTH), F32),
        shape((EXPERTS, WIDTH), F32),
        shape((16, ROWS), F32),
    ]


def exchange(block):
    dims = block.shape
    pieces = lax.all_to_all(
        block.reshape((64, dims[0] // 64, dims[1])), BOTH, split_axis=0, concat_axis=0, tiled=True
    )
    return pieces.reshape(dims)


def shards(
    block_in,
    cotangent,
    lengths,
    routes,
    query_weight,
    key_weight,
    value_weight,
    out_weight,
    attn_gain,
    moe_gain,
    router,
    rel_table,
    expert_in,
    expert_out,
):
    core = lax.axis_index("section")
    half = lax.axis_index("shard")
    first_core = core == 0
    lower = half == 0

    def pick(left, right):
        return jnp.where(first_core, left, right)

    small = jnp.concatenate(
        [
            router[0],
            attn_gain.reshape(HALF, 1),
            moe_gain.reshape(HALF, 1),
            jnp.pad(rel_table[0], ((0, HALF - NB // 2), (0, 82))),
        ],
        axis=1,
    )
    small_pair = jnp.stack([small, lax.ppermute(small, "shard", [(0, 1), (1, 0)])])
    small_swapped = swap(small_pair)

    weights_own = [w[0] for w in (query_weight, key_weight, value_weight, out_weight)]

    def cross_one_core(block, section, flip):
        pairs = []
        for part in range(64):
            source = section * 64 + part
            target = section * 64 + (part ^ 32 ^ flip)
            pairs.append((source, target))
        return lax.ppermute(block, ("section", "shard", "replica"), pairs)

    arrived0 = [cross_one_core(w, 0, number % 2) for number, w in enumerate(weights_own)]
    weights_swapped = [swap(w) for w in weights_own]
    passed0 = [swap(w) for w in arrived0[:3]]
    bucket_hot = np.eye(NB, dtype=np.float32)[bucket_of_distance(ROWS)]
    turned = bucket_hot[(-np.arange(ROWS)) % ROWS]

    turned_hot = jnp.asarray(turned.T, BF)
    params = [
        [pick(small_pair, small_swapped), turned_hot],
        [pick(small_swapped, small_pair), turned_hot],
    ]

    routes_other = swap(pick(routes[0, 1], routes[0, 0]))
    routes_mine = pick(routes[0, 0], routes[0, 1])
    layer_routes = [pick(routes_mine, routes_other), pick(routes_other, routes_mine)]
    runs = pick(lengths[0, 0], lengths[1, 0])
    info = jnp.concatenate(
        [jnp.stack([core, half]).astype(jnp.int32), jnp.cumsum(runs, dtype=jnp.int32)]
    )

    tied = lax.optimization_barrier((arrived0[3], params[0][0], params[1][0], info, *layer_routes))
    arrived0[3], params[0][0], params[1][0], info = tied[:4]
    layer_routes = list(tied[4:])
    passed0.append(swap(arrived0[3]))
    later = lax.optimization_barrier(tuple(weights_own) + tuple(arrived0))[:4]
    arrived1 = [cross_one_core(w, 1, number % 2) for number, w in enumerate(later)]
    passed1 = [swap(w) for w in arrived1]
    weights = [[], []]
    for number in range(4):
        own = [weights_own[number], weights_swapped[number]]
        weights[0] += own + [arrived0[number], passed0[number]]
        weights[1] += own + [arrived1[number], passed1[number]]
    experts = []
    for w in lax.optimization_barrier((expert_in[0, 0], expert_out[0, 0], *passed0))[:2]:
        experts += [w, swap(w)]

    *kept0, send = whole_call(
        first_forward_kernel,
        forward_shapes() + [shape((512, WIDTH))],
        "attend_first",
        [info, layer_routes[0], block_in],
        weights[0],
        params[0],
    )
    rows0 = exchange(send)
    hidden = expert_in.shape[3]
    sum_scratch = pltpu.VMEM((512, WIDTH), F32)
    (made,) = whole_call(
        expert_forward_kernel,
        [shape((512, WIDTH))],
        "expert_first",
        [info, rows0],
        experts,
        scratch=expert_scratch(hidden, False) + [sum_scratch],
    )
    back = exchange(made)
    n10, q0, k0, v0, mixed0, resid0, n20, prob0, gate0, gains0, bias0 = kept0
    *kept1, send, middle, combined0 = whole_call(
        second_forward_kernel,
        forward_shapes()
        + [shape((1024, WIDTH)), shape((ROWS, WIDTH)), shape((ROWS, WIDTH), F32)],
        "attend_second",
        [info, layer_routes[1], layer_routes[0], resid0, gate0, back, cotangent],
        weights[1],
        params[1],
    )
    both = exchange(send)
    grad_shapes = [shape((WIDTH, hidden)), shape((hidden, WIDTH))] * 2
    back, *expert_grads = whole_call(
        expert_both_kernel,
        [shape((1024, WIDTH))] + grad_shapes,
        "expert_second",
        [info, both],
        experts,
        out_specs=[VMEM] + [HBM] * 4,
        scratch=expert_scratch(hidden, True)
        + [pltpu.VMEM((512, WIDTH), BF)] * 2
        + [pltpu.VMEM((WIDTH, 512), BF)]
        + [sum_scratch] * 2,
    )
    back = exchange(back)
    n11, q1, k1, v1, mixed1, resid1, n21, prob1, gate1, gains1, bias1 = kept1
    *grads1, result, send = whole_call(
        last_backward_kernel,
        backward_shapes() + [shape((ROWS, WIDTH)), shape((512, WIDTH))],
        "attend_second_back",
        [info, layer_routes[1], layer_routes[0], gate0, cotangent, back]
        + [middle, q1, k1, v1, resid1, n21, prob1, gate1],
        weights[1],
        [gains1, params[1][0], bias1],
    )
    made_grads = exchange(send)
    back, *expert_grads = whole_call(
        expert_backward_kernel,
        [shape((512, WIDTH))] + grad_shapes,
        "expert_first_back",
        [info, rows0, made_grads],
        experts + expert_grads,
        out_specs=[VMEM] + [HBM] * 4,
        scratch=expert_scratch(hidden, True) + [pltpu.VMEM((WIDTH, 512), BF), sum_scratch],
        input_output_aliases={7: 1, 8: 2, 9: 3, 10: 4},
    )
    back = exchange(back)
    grads0 = whole_call(
        first_backward_kernel,
        backward_shapes(),
        "attend_first_back",
        [info, layer_routes[0], combined0, grads1[1], back]
        + [block_in, q0, k0, v0, resid0, n20, prob0, gate0],
        weights[0],
        [gains0, params[0][0], bias0],
    )

    def small_rows(gain_grad, router_grad, diag):
        table = lax.dot_general(
            diag[:HEADS],
            jnp.asarray(bucket_hot[::-1]),
            (((1,), (0,)), ((), ())),
            precision=lax.Precision.HIGHEST,
            preferred_element_type=F32,
        )
        table = jnp.transpose(table.reshape(HEADS, 2, NB // 2), (1, 0, 2))
        table = jnp.pad(table, ((0, 0), (0, 0), (0, HALF - NB // 2)))
        gains = jnp.transpose(gain_grad[:2].reshape(2, 2, HALF), (1, 0, 2))
        others = jnp.concatenate([gains, table, jnp.zeros((2, EXPERTS - HEADS - 2, HALF), F32)], axis=1)
        routers = jnp.transpose(router_grad.reshape(EXPERTS, 2, HALF), (1, 0, 2))
        return jnp.stack([routers, others], axis=2).astype(BF)

    def summed_cores(n1, mixed, grads):
        keep, send = whole_call(
            weight_grad_kernel,
            [shape((2, 4, HALF, HALF))] * 2,
            "weight_grads",
            [info, n1, mixed, grads[0]],
        )
        return keep, swap(send)

    keep1, got1 = summed_cores(n11, mixed1, grads1)
    small1 = small_rows(*grads1[2:]).reshape(64, 2, HALF)
    keep0, got0 = summed_cores(n10, mixed0, grads0)
    small0 = small_rows(*grads0[2:]).reshape(64, 2, HALF)
    expert_got = [swap(g) for g in expert_grads[2:]]
    keep0, *expert_got = lax.optimization_barrier((keep0, *expert_got))

    smalls = jnp.pad(small0, ((0, 0), (0, 6), (0, 0))) + jnp.pad(small1, ((0, 0), (2, 4), (0, 0)))
    pieces = merge_call([keep0, got0, keep1, got1], smalls)
    pieces = lax.all_to_all(pieces, BOTH, split_axis=0, concat_axis=0, tiled=True)
    total = jnp.sum(pieces.astype(F32), axis=0).astype(BF)
    expert_totals = [k.astype(F32) + g.astype(F32) for k, g in zip(expert_grads[:2], expert_got)]

    def by_micro(first, second):
        mine, theirs = pick(first, second), swap(pick(second, first))
        return jnp.stack([pick(mine, theirs), pick(theirs, mine)])

    section_out = by_micro(middle, result)
    input_grad = by_micro(grads0[1], grads1[1])
    total, section_out, input_grad, *expert_totals = lax.optimization_barrier(
        (total, section_out, input_grad, *expert_totals)
    )
    spread = jnp.broadcast_to(total[None], (32,) + total.shape)
    whole = lax.all_to_all(spread, "replica", split_axis=0, concat_axis=0, tiled=True)
    whole0 = jnp.concatenate([whole[:, :48], whole[:, 96:98]], axis=1)
    whole1 = jnp.concatenate([whole[:, 48:96], whole[:, 98:100]], axis=1)

    kept = pick(whole0, whole1)
    got = swap(pick(whole1, whole0))
    left, right = pick(kept, got), pick(got, kept)
    full = jnp.concatenate([left[:, :48], right[:, :48]], axis=2).astype(F32)
    full = full.reshape(4, HALF, WIDTH)
    smalls = kept[:, 48:50].astype(F32) + got[:, 48:50].astype(F32)
    router_grad = jnp.transpose(smalls[:, 0], (1, 0))
    table_grad = jnp.transpose(smalls[2 : 2 + HEADS, 1, : NB // 2], (1, 0))

    return (
        section_out[None],
        input_grad[None],
        full[0][None],
        full[1][None],
        full[2][None],
        full[3][None],
        smalls[0, 1][None],
        smalls[1, 1][None],
        router_grad[None],
        table_grad[None],
        expert_totals[0][None, None],
        expert_totals[1][None, None],
    )


def solution(mesh):
    in_specs = (
        P(None, ("shard", "replica"), None),
        P(None, ("shard", "replica"), None),
        P(None, ("shard", "replica"), None),
        P("section", None, ("shard", "replica"), None),
        P("section", "shard", None),
        P("section", "shard", None),
        P("section", "shard", None),
        P("section", "shard", None),
        P("section", "shard"),
        P("section", "shard"),
        P("section", "shard", None),
        P("section", "shard", None),
        P("section", "replica", None, "shard"),
        P("section", "replica", "shard", None),
    )
    out_specs = (
        P("section", None, ("shard", "replica"), None),
        P("section", None, ("shard", "replica"), None),
        P("section", "shard", None),
        P("section", "shard", None),
        P("section", "shard", None),
        P("section", "shard", None),
        P("section", "shard"),
        P("section", "shard"),
        P("section", "shard", None),
        P("section", "shard", None),
        P("section", "replica", None, "shard"),
        P("section", "replica", "shard", None),
    )
    return jax.shard_map(shards, mesh=mesh, in_specs=in_specs, out_specs=out_specs, check_vma=False)
```

```python
import jax
import jax.numpy as jnp
import numpy as np
from jax import lax
from jax.experimental import pallas as pl
from jax.experimental.pallas import tpu as pltpu
from jax.sharding import PartitionSpec as P

HEADS = 12
HEAD_DIM = 64
NB = 32
MAXDIST = 128
DOCS = 4
ROWS = 128
WIDTH = 768
HALF = 384
EXPERTS = 32
SLOTS = 8
MIB = 1024 * 1024
BF = jnp.bfloat16
F32 = jnp.float32

norm_eps = 1e-06
BOTH = ("shard", "replica")


def bucket_of_distance(length):
    distance = np.arange(length)
    exact_count = NB // 2
    log_ratio = np.log(np.maximum(distance, 1) / exact_count) / np.log(MAXDIST / exact_count)
    far_bucket = exact_count + np.floor(log_ratio * (NB - exact_count)).astype(np.int32)
    return np.where(distance < exact_count, distance, np.minimum(far_bucket, NB - 1)).astype(
        np.int32
    )


def swap(block):
    return lax.ppermute(block, "section", [(0, 1), (1, 0)])


def dot(left, right):
    return jnp.dot(left, right, preferred_element_type=F32)


def dot_t(left, right):
    return lax.dot_general(left, right, (((1,), (1,)), ((), ())), preferred_element_type=F32)


def t_dot(left, right):
    return lax.dot_general(left, right, (((0,), (0,)), ((), ())), preferred_element_type=F32)


def in_halves(matrix, lower):
    first, second = matrix[:, :HALF], matrix[:, HALF:]
    return jnp.where(lower, first, second), jnp.where(lower, second, first)


PARTS = 4


class Weights:
    def __init__(self, info_ref, layer, sources, buffers, sems, order):
        self.sources, self.buffers, self.sems, self.here = sources, buffers, sems, set()
        for matrix in order:
            for number in (2 * matrix, 2 * matrix + 1):

                @pl.when(info_ref[0] == layer)
                def _():
                    self.copy(number, 0).start()

                @pl.when(info_ref[0] != layer)
                def _():
                    self.copy(number, 1).start()

    def copy(self, number, place):
        return pltpu.make_async_copy(
            self.sources[2 * number + place], self.buffers.at[number], self.sems.at[number]
        )

    def take(self, number):
        if number not in self.here:
            self.here.add(number)
            self.copy(number, 0).wait()
        return self.buffers[number]

    def pair(self, matrix):
        return self.take(2 * matrix), self.take(2 * matrix + 1)


def project(matrix, lower, halves):
    own_part, other_part = in_halves(matrix, lower)
    return dot(own_part, halves[0]) + dot(other_part, halves[1])


def project_back(matrix, lower, halves):
    own_part = dot_t(matrix, halves[0])
    other_part = dot_t(matrix, halves[1])
    return jnp.concatenate(
        [jnp.where(lower, own_part, other_part), jnp.where(lower, other_part, own_part)], axis=1
    )


def segments(info_ref, axis):
    places = lax.broadcasted_iota(jnp.int32, (ROWS, ROWS), axis)
    found = jnp.zeros((ROWS, ROWS), jnp.int32)
    for run in range(DOCS):
        found = found + (places >= info_ref[2 + run]).astype(jnp.int32)
    return found


def attend_mask(info_ref):
    rows = lax.broadcasted_iota(jnp.int32, (ROWS, ROWS), 0)
    columns = lax.broadcasted_iota(jnp.int32, (ROWS, ROWS), 1)
    return (segments(info_ref, 0) == segments(info_ref, 1)) & (columns <= rows)


def head_prob(queries_own, key_pair, bias_ref, head, mask):
    bias = pltpu.roll(
        jnp.broadcast_to(bias_ref[head : head + 1, :], (ROWS, ROWS)),
        0,
        axis=1,
        stride=1,
        stride_axis=0,
    )
    scores = dot_t(queries_own, key_pair) * HEAD_DIM ** (-0.5) + bias
    scores = jnp.where(mask, scores, -1e30)
    exponent = jnp.exp(scores - jnp.max(scores, axis=-1, keepdims=True))
    return exponent / jnp.sum(exponent, axis=-1, keepdims=True)


def pair_masks():
    lane = lax.broadcasted_iota(jnp.int32, (ROWS, 2 * HEAD_DIM), 1)
    return lane < HEAD_DIM


def only(first, head_in_pair, pair):
    keep = first if head_in_pair == 0 else jnp.logical_not(first)
    return jnp.where(keep, pair, jnp.zeros_like(pair))


def route_hot(routes_ref):
    experts = lax.broadcasted_iota(jnp.int32, (ROWS, EXPERTS), 1)
    return (routes_ref[...] == experts).astype(F32)


def token_slots(routes_ref, info_ref, hot):
    routed = segments(info_ref, 0)[:, :1] < DOCS - 1
    routed_hot = jnp.where(routed, hot, 0.0)
    rows = lax.broadcasted_iota(jnp.int32, (ROWS, ROWS), 0)
    columns = lax.broadcasted_iota(jnp.int32, (ROWS, ROWS), 1)
    earlier = dot((columns < rows).astype(BF), routed_hot.astype(BF))
    place = jnp.sum(routed_hot * earlier, axis=-1, keepdims=True).astype(jnp.int32)
    return jnp.where(routed, place, -1), routes_ref[...]


def slot_table(place, route, group, offset, count):
    lanes = lax.broadcasted_iota(jnp.int32, (ROWS, count), 1) % (EXPERTS * group)
    wanted = jnp.where(place >= 0, route * group + offset + place, -1)
    return (lanes == wanted).astype(BF)


def pack_kernel(router_ref, gain_one_ref, gain_two_ref, table_ref, out_ref):
    table = jnp.pad(table_ref[...].astype(F32), ((0, 0), (0, HALF - HEADS)))
    out_ref[...] = jnp.concatenate(
        [
            router_ref[...].astype(F32).T,
            gain_one_ref[...].astype(F32),
            gain_two_ref[...].astype(F32),
            jnp.zeros((14, HALF), F32),
            table,
        ],
        axis=0,
    ).astype(BF)


def small_halves(info_ref, layer, small_refs):
    here = info_ref[0] == layer
    own = jnp.where(here, small_refs[0][...], small_refs[1][...])
    return own, jnp.where(here, small_refs[2][...], small_refs[3][...])


def unpack_small(small, hot_ref, lower, gains_ref, bias_ref):
    gains = [half[EXPERTS : EXPERTS + 16, :].astype(F32)[:8] for half in small]
    gains_ref[...] = jnp.concatenate(
        [jnp.where(lower, gains[0], gains[1]), jnp.where(lower, gains[1], gains[0])], axis=1
    )
    tables = [half[EXPERTS + 16 :, :ROWS] for half in small]
    low = jnp.where(lower, tables[0], tables[1])
    high = jnp.where(lower, tables[1], tables[0])
    bias = t_dot(low, hot_ref[: NB // 2, :]) + t_dot(high, hot_ref[NB // 2 :, :])
    bias_ref[...] = bias[:16, :]


def forward_attention(inputs_f, info_ref, routes_ref, weights, small, hot_ref, outs):
    lower = info_ref[1] == 0
    n1_ref, q_ref, k_ref, v_ref, mixed_ref, resid_ref, n2_ref, prob_ref, gate_ref = outs[:9]
    gains_ref, bias_ref = outs[9:]
    unpack_small(small, hot_ref, lower, gains_ref, bias_ref)
    scale = lax.rsqrt(jnp.mean(inputs_f * inputs_f, axis=-1, keepdims=True) + norm_eps)
    normed = (inputs_f * scale * gains_ref[0:1, :]).astype(BF)
    n1_ref[...] = normed
    q_ref[...] = project(normed, lower, weights.pair(0)).astype(BF)
    k_ref[...] = project(normed, lower, weights.pair(1)).astype(BF)
    v_ref[...] = project(normed, lower, weights.pair(2)).astype(BF)
    mask = attend_mask(info_ref)
    first = pair_masks()
    for pair in range(HEADS // 2):
        here = slice(pair * 128, pair * 128 + 128)
        q_pair, k_pair, v_pair = q_ref[:, here], k_ref[:, here], v_ref[:, here]
        made = []
        for member in range(2):
            prob = head_prob(only(first, member, q_pair), k_pair, bias_ref, 2 * pair + member, mask)
            made.append(dot(prob.astype(BF), v_pair))
        mixed_ref[:, here] = jnp.where(first, made[0], made[1]).astype(BF)
    resid = inputs_f + project(mixed_ref[...], lower, weights.pair(3))
    resid_ref[...] = resid
    scale = lax.rsqrt(jnp.mean(resid * resid, axis=-1, keepdims=True) + norm_eps)
    normed_two = (resid * scale * gains_ref[1:2, :]).astype(BF)
    n2_ref[...] = normed_two
    own_part, other_part = in_halves(normed_two, lower)
    logits = dot_t(own_part, small[0][:EXPERTS]) + dot_t(other_part, small[1][:EXPERTS])
    logit_exp = jnp.exp(logits - jnp.max(logits, axis=-1, keepdims=True))
    prob = logit_exp / jnp.sum(logit_exp, axis=-1, keepdims=True)
    prob_ref[...] = prob
    hot = route_hot(routes_ref)
    gate = jnp.sum(prob * hot, axis=-1, keepdims=True)
    gate_ref[...] = gate
    place, route = token_slots(routes_ref, info_ref, hot)
    return normed_two, gate, place, route


def first_forward_kernel(info_ref, routes_ref, x_ref, *refs):
    small, hot_ref = small_halves(info_ref, 0, refs[16:20]), refs[20]
    outs, send_ref = refs[21:32], refs[32]
    weights = Weights(info_ref, 0, refs[:16], refs[33], refs[34], (0, 1, 2, 3))
    normed_two, _, place, route = forward_attention(
        x_ref[info_ref[0]].astype(F32), info_ref, routes_ref, weights, small, hot_ref, outs
    )
    table = slot_table(place, route, SLOTS, 0, EXPERTS * SLOTS)
    rows = t_dot(table, normed_two).astype(BF)
    send_ref[: EXPERTS * SLOTS, :] = rows
    send_ref[EXPERTS * SLOTS :, :] = rows


def second_forward_kernel(
    info_ref, routes_ref, routes_before_ref, resid_ref, gate_ref, back_ref, cot_ref, *refs
):
    small, hot_ref, outs = small_halves(info_ref, 1, refs[16:20]), refs[20], refs[21:32]
    send_ref, x_ref, combined_ref = refs[32:35]
    weights = Weights(info_ref, 1, refs[:16], refs[35], refs[36], (0, 1, 2, 3))
    place, route = token_slots(routes_before_ref, info_ref, route_hot(routes_before_ref))
    combined = dot(slot_table(place, route, SLOTS, 0, 2 * EXPERTS * SLOTS), back_ref[...])
    combined_ref[...] = combined
    inputs = (resid_ref[...] + gate_ref[...] * combined).astype(BF)
    x_ref[...] = inputs
    normed_two, gate, place, route = forward_attention(
        inputs.astype(F32), info_ref, routes_ref, weights, small, hot_ref, outs
    )
    made_grad = (gate * cot_ref[info_ref[0]].astype(F32)).astype(BF)
    group = 2 * SLOTS
    rows = t_dot(slot_table(place, route, group, 0, EXPERTS * group), normed_two)
    rows = rows + t_dot(slot_table(place, route, group, SLOTS, EXPERTS * group), made_grad)
    rows = rows.astype(BF)
    send_ref[: EXPERTS * group, :] = rows
    send_ref[EXPERTS * group :, :] = rows


def backward_attention(
    inputs,
    grad_out,
    combined,
    grad_two_rows,
    info_ref,
    routes_ref,
    kept,
    weights,
    gains_ref,
    small,
    bias_ref,
    outs,
):
    lower = info_ref[1] == 0
    q_ref, k_ref, v_ref, resid_ref, n2_ref, prob_ref, gate_ref = kept
    grads_ref, input_grad_ref, gain_grad_ref, router_grad_ref, diag_ref = outs
    hot = route_hot(routes_ref)
    grad_gate = jnp.sum(grad_out * combined, axis=-1, keepdims=True)
    grad_logits = (grad_gate * gate_ref[...] * (hot - prob_ref[...])).astype(BF)
    router_grad_ref[...] = t_dot(grad_logits, n2_ref[...])
    own_part, other_part = dot(grad_logits, small[0][:EXPERTS]), dot(grad_logits, small[1][:EXPERTS])
    grad_two = grad_two_rows + jnp.concatenate(
        [jnp.where(lower, own_part, other_part), jnp.where(lower, other_part, own_part)], axis=1
    )
    resid = resid_ref[...]
    scale = lax.rsqrt(jnp.mean(resid * resid, axis=-1, keepdims=True) + norm_eps)
    gain_grad_ref[1:2, :] = jnp.sum(grad_two * resid * scale, axis=0, keepdims=True)
    gained = gains_ref[1:2, :] * grad_two
    grad_resid = (
        grad_out
        + scale * gained
        - resid * (scale * scale * scale) * jnp.mean(resid * gained, axis=-1, keepdims=True)
    )
    grad_attn = grad_resid.astype(BF)
    grads_ref[3] = grad_attn
    grad_mixed = project_back(grad_attn, lower, weights.pair(3)).astype(BF)
    mask = attend_mask(info_ref)
    first = pair_masks()
    rows = lax.broadcasted_iota(jnp.int32, (ROWS, ROWS), 0)
    columns = lax.broadcasted_iota(jnp.int32, (ROWS, ROWS), 1)
    flip = (rows + columns == ROWS - 1).astype(BF)
    for pair in range(HEADS // 2):
        here = slice(pair * 128, pair * 128 + 128)
        q_pair, k_pair, v_pair = q_ref[:, here], k_ref[:, here], v_ref[:, here]
        mixed_pair = grad_mixed[:, here]
        made = []
        for member in range(2):
            head = 2 * pair + member
            prob = head_prob(only(first, member, q_pair), k_pair, bias_ref, head, mask)
            grad_prob = dot_t(only(first, member, mixed_pair), v_pair)
            grad_value = t_dot(prob.astype(BF), mixed_pair)
            grad_scores = prob * (grad_prob - jnp.sum(prob * grad_prob, axis=-1, keepdims=True))
            grad_scores = grad_scores.astype(BF)
            turned = pltpu.roll(
                dot(flip, grad_scores), 0, axis=1, stride=1, stride_axis=0
            )
            diag_ref[head : head + 1, :] = jnp.sum(turned, axis=0, keepdims=True)
            made.append(
                (
                    dot(grad_scores, k_pair) * HEAD_DIM ** (-0.5),
                    t_dot(grad_scores, q_pair) * HEAD_DIM ** (-0.5),
                    grad_value,
                )
            )
        for number in range(3):
            grads_ref[number, :, here] = jnp.where(
                first, made[0][number], made[1][number]
            ).astype(BF)
    diag_ref[HEADS:, :] = jnp.zeros((16 - HEADS, ROWS), F32)
    grad_one = project_back(grads_ref[0], lower, weights.pair(0))
    grad_one = grad_one + project_back(grads_ref[1], lower, weights.pair(1))
    grad_one = grad_one + project_back(grads_ref[2], lower, weights.pair(2))
    scale = lax.rsqrt(jnp.mean(inputs * inputs, axis=-1, keepdims=True) + norm_eps)
    gain_grad_ref[0:1, :] = jnp.sum(grad_one * inputs * scale, axis=0, keepdims=True)
    gain_grad_ref[2:, :] = jnp.zeros((6, WIDTH), F32)
    gained = gains_ref[0:1, :] * grad_one
    input_grad = (
        grad_resid
        + scale * gained
        - inputs * (scale * scale * scale) * jnp.mean(inputs * gained, axis=-1, keepdims=True)
    ).astype(BF)
    input_grad_ref[...] = input_grad
    return input_grad


def last_backward_kernel(
    info_ref, routes_ref, routes_before_ref, gate_before_ref, cot_ref, back_ref, *refs
):
    x_ref, kept, gains_ref, bias_ref = refs[0], refs[1:8], refs[24], refs[29]
    small = small_halves(info_ref, 1, refs[25:29])
    outs, result_ref, send_ref = refs[30:35], refs[35], refs[36]
    weights = Weights(info_ref, 1, refs[8:24], refs[37], refs[38], (3, 0, 1, 2))
    gate_ref, resid_ref = kept[6], kept[3]
    place, route = token_slots(routes_ref, info_ref, route_hot(routes_ref))
    group = 2 * SLOTS
    combined = dot(slot_table(place, route, group, 0, 2 * EXPERTS * group), back_ref[...])
    grad_rows = dot(slot_table(place, route, group, SLOTS, 2 * EXPERTS * group), back_ref[...])
    result_ref[...] = (resid_ref[...] + gate_ref[...] * combined).astype(BF)
    input_grad = backward_attention(
        x_ref[...].astype(F32),
        cot_ref[info_ref[0]].astype(F32),
        combined,
        grad_rows,
        info_ref,
        routes_ref,
        kept,
        weights,
        gains_ref,
        small,
        bias_ref,
        outs,
    )
    made_grad = (gate_before_ref[...] * input_grad.astype(F32)).astype(BF)
    place, route = token_slots(routes_before_ref, info_ref, route_hot(routes_before_ref))
    rows = t_dot(slot_table(place, route, SLOTS, 0, EXPERTS * SLOTS), made_grad).astype(BF)
    send_ref[: EXPERTS * SLOTS, :] = rows
    send_ref[EXPERTS * SLOTS :, :] = rows


def first_backward_kernel(info_ref, routes_ref, combined_ref, grad_ref, back_ref, *refs):
    x_ref, kept, gains_ref, bias_ref = refs[0], refs[1:8], refs[24], refs[29]
    small = small_halves(info_ref, 0, refs[25:29])
    outs = refs[30:35]
    weights = Weights(info_ref, 0, refs[8:24], refs[35], refs[36], (3, 0, 1, 2))
    place, route = token_slots(routes_ref, info_ref, route_hot(routes_ref))
    grad_rows = dot(slot_table(place, route, SLOTS, 0, 2 * EXPERTS * SLOTS), back_ref[...])
    backward_attention(
        x_ref[info_ref[0]].astype(F32),
        grad_ref[...].astype(F32),
        combined_ref[...],
        grad_rows,
        info_ref,
        routes_ref,
        kept,
        weights,
        gains_ref,
        small,
        bias_ref,
        outs,
    )


def weight_grad_kernel(info_ref, n1_ref, mixed_ref, grads_ref, keep_ref, send_ref):
    first_core = info_ref[0] == 0
    n1_turned, mixed_turned = n1_ref[...].T, mixed_ref[...].T
    for number in range(4):
        left = mixed_turned if number == 3 else n1_turned
        kept, sent = in_halves(grads_ref[number], first_core)
        for half in range(2):
            rows = left[half * HALF : half * HALF + HALF, :]
            keep_ref[half, number] = dot(rows, kept).astype(BF)
            send_ref[half, number] = dot(rows, sent).astype(BF)


def merge_kernel(*refs):
    far, out_far = refs[:5], refs[5]
    keep0_ref, got0_ref, keep1_ref, got1_ref, small_ref, out_ref, sems = refs[6:]
    near, size = refs[6:11], 64 // PARTS

    def copy(source, target, number, part):
        here = pl.ds(part * size, size)
        return pltpu.make_async_copy(source.at[here], target.at[here], sems.at[number, part])

    for part in range(PARTS):
        for number in range(5):
            copy(far[number], near[number], number, part).start()
    for part in range(PARTS):
        here = slice(part * size, part * size + size)
        for number in range(5):
            copy(far[number], near[number], number, part).wait()
        out_ref[here] = jnp.concatenate(
            [
                (keep0_ref[here].astype(F32) + got0_ref[here].astype(F32)).astype(BF),
                (keep1_ref[here].astype(F32) + got1_ref[here].astype(F32)).astype(BF),
                small_ref[here],
            ],
            axis=1,
        )
        copy(out_ref, out_far, 5, part).start()
    for part in range(PARTS):
        copy(out_ref, out_far, 5, part).wait()


def gelu_parts(hidden):
    slope = np.sqrt(2 / np.pi).astype(np.float32)
    square = hidden * hidden
    curve = jnp.tanh(slope * hidden * (1.0 + 0.044715 * square))
    gate = 0.5 * (1.0 + curve)
    grad = gate + 0.5 * hidden * (1.0 - curve * curve) * slope * (1.0 + 3 * 0.044715 * square)
    return hidden * gate, grad


class Chunks:
    def __init__(self, info_ref, layer, refs, win, wout, sems):
        self.info_ref, self.layer, self.refs = info_ref, layer, refs
        self.win, self.wout, self.sems = win, wout, sems
        for chunk in range(win.shape[0]):

            @pl.when(info_ref[0] == layer)
            def _():
                for copy in self.copies(0, chunk):
                    copy.start()

            @pl.when(info_ref[0] != layer)
            def _():
                for copy in self.copies(1, chunk):
                    copy.start()

    def copies(self, place, chunk):
        here = pl.ds(pl.multiple_of(chunk * BLOCK, BLOCK), BLOCK)
        return (
            pltpu.make_async_copy(
                self.refs[place].at[:, here], self.win.at[chunk], self.sems.at[0, chunk]
            ),
            pltpu.make_async_copy(
                self.refs[2 + place].at[here, :], self.wout.at[chunk], self.sems.at[1, chunk]
            ),
        )

    def take(self, chunk):
        for copy in self.copies(0, chunk):
            copy.wait()
        return self.win[chunk], self.wout[chunk]

    def grads_to(self, targets, din, dout, sems):
        self.targets, self.din, self.dout, self.out_sems = targets, din, dout, sems

    def grad_copies(self, place, chunk):
        here = pl.ds(pl.multiple_of(chunk * BLOCK, BLOCK), BLOCK)
        return (
            pltpu.make_async_copy(
                self.din.at[chunk], self.targets[2 * place].at[:, here], self.out_sems.at[0, chunk]
            ),
            pltpu.make_async_copy(
                self.dout.at[chunk],
                self.targets[2 * place + 1].at[here, :],
                self.out_sems.at[1, chunk],
            ),
        )

    def put(self, chunk):
        @pl.when(self.info_ref[0] == self.layer)
        def _():
            for copy in self.grad_copies(0, chunk):
                copy.start()

        @pl.when(self.info_ref[0] != self.layer)
        def _():
            for copy in self.grad_copies(1, chunk):
                copy.start()

    def finish(self):
        for chunk in range(self.din.shape[0]):
            for copy in self.grad_copies(0, chunk):
                copy.wait()


def expert_forward_kernel(info_ref, rows_ref, *refs):
    made_ref, win, wout, sems, made_sum = refs[4:]
    chunks = Chunks(info_ref, 0, refs[:4], win, wout, sems)
    made_sum[...] = jnp.zeros_like(made_sum)

    @pl.loop(0, win.shape[0])
    def _(chunk):
        w_in, w_out = chunks.take(chunk)
        act, _ = gelu_parts(dot(rows_ref[...], w_in))
        made_sum[...] += dot(act.astype(BF), w_out)

    made_ref[...] = made_sum[...].astype(BF)


def expert_backward_kernel(info_ref, rows_ref, grad_ref, *refs):
    back_ref, targets = refs[8], refs[9:13]
    win, wout, sems, din, dout, out_sems, rows_turned, rows_sum = refs[13:]
    chunks = Chunks(info_ref, 0, refs[:4], win, wout, sems)
    chunks.grads_to(targets, din, dout, out_sems)
    rows_sum[...] = jnp.zeros_like(rows_sum)
    rows_turned[...] = rows_ref[...].T

    @pl.loop(0, win.shape[0])
    def _(chunk):
        w_in, w_out = chunks.take(chunk)
        act, slope = gelu_parts(dot(rows_ref[...], w_in))
        grad_pre = (slope * dot_t(grad_ref[...], w_out)).astype(BF)
        dout[chunk] = t_dot(act.astype(BF), grad_ref[...]).astype(BF)
        din[chunk] = dot(rows_turned[...], grad_pre).astype(BF)
        chunks.put(chunk)
        rows_sum[...] += dot_t(grad_pre, w_in)

    back_ref[...] = rows_sum[...].astype(BF)
    chunks.finish()


def expert_both_kernel(info_ref, both_ref, *refs):
    back_ref, targets = refs[4], refs[5:9]
    win, wout, sems, din, dout, out_sems, rows, grads, rows_turned, made_sum, rows_sum = refs[9:]
    chunks = Chunks(info_ref, 1, refs[:4], win, wout, sems)
    chunks.grads_to(targets, din, dout, out_sems)
    pieces = both_ref.shape[0] // (2 * SLOTS)
    for piece in range(0, pieces, 2):
        block = both_ref[piece * 16 : piece * 16 + 32, :].astype(F32)
        rows[piece * 8 : piece * 8 + 16, :] = jnp.concatenate(
            [block[0:8], block[16:24]], axis=0
        ).astype(BF)
        grads[piece * 8 : piece * 8 + 16, :] = jnp.concatenate(
            [block[8:16], block[24:32]], axis=0
        ).astype(BF)
    made_sum[...] = jnp.zeros_like(made_sum)
    rows_sum[...] = jnp.zeros_like(rows_sum)
    rows_turned[...] = rows[...].T

    @pl.loop(0, win.shape[0])
    def _(chunk):
        w_in, w_out = chunks.take(chunk)
        act, slope = gelu_parts(dot(rows[...], w_in))
        act = act.astype(BF)
        grad_pre = (slope * dot_t(grads[...], w_out)).astype(BF)
        dout[chunk] = t_dot(act, grads[...]).astype(BF)
        din[chunk] = dot(rows_turned[...], grad_pre).astype(BF)
        chunks.put(chunk)
        made_sum[...] += dot(act, w_out)
        rows_sum[...] += dot_t(grad_pre, w_in)

    for piece in range(pieces):
        back_ref[piece * 16 : piece * 16 + 16, :] = jnp.concatenate(
            [made_sum[piece * 8 : piece * 8 + 8], rows_sum[piece * 8 : piece * 8 + 8]], axis=0
        ).astype(BF)
    chunks.finish()


def shape(dims, kind=BF):
    return jax.ShapeDtypeStruct(dims, kind)


SMEM = pl.BlockSpec(memory_space=pltpu.SMEM)
VMEM = pl.BlockSpec(memory_space=pltpu.VMEM)
HBM = pl.BlockSpec(memory_space=pltpu.HBM)
BLOCK = 512


def whole_call(kernel, out_shape, name, before, weights=(), after=(), **more):
    scratch = []
    if len(weights) == 16:
        scratch = [pltpu.VMEM((8, HALF, WIDTH), BF), pltpu.SemaphoreType.DMA((8,))]
    return pl.pallas_call(
        kernel,
        out_shape=out_shape,
        in_specs=[SMEM] + [VMEM] * (len(before) - 1) + [HBM] * len(weights) + [VMEM] * len(after),
        out_specs=more.pop("out_specs", [VMEM] * len(out_shape)),
        scratch_shapes=more.pop("scratch", scratch),
        name=name,
        compiler_params=pltpu.CompilerParams(vmem_limit_bytes=60 * MIB),
        **more,
    )(*before, *weights, *after)


def merge_call(sums, smalls):
    return pl.pallas_call(
        merge_kernel,
        out_shape=shape((64, 104, HALF)),
        in_specs=[HBM] * 5,
        out_specs=HBM,
        scratch_shapes=[pltpu.VMEM((64, 48, HALF), BF)] * 4
        + [pltpu.VMEM((64, 8, HALF), BF), pltpu.VMEM((64, 104, HALF), BF)]
        + [pltpu.SemaphoreType.DMA((6, PARTS))],
        name="merge_grads",
        compiler_params=pltpu.CompilerParams(vmem_limit_bytes=60 * MIB),
    )(*[part.reshape(64, 48, HALF) for part in sums], smalls)


def expert_scratch(hidden, grads):
    count = hidden // BLOCK
    moved = [
        pltpu.VMEM((count, WIDTH, BLOCK), BF),
        pltpu.VMEM((count, BLOCK, WIDTH), BF),
        pltpu.SemaphoreType.DMA((2, count)),
    ]
    return moved * (2 if grads else 1)


def forward_shapes():
    tokens = shape((ROWS, WIDTH))
    return [
        tokens,
        tokens,
        tokens,
        tokens,
        tokens,
        shape((ROWS, WIDTH), F32),
        tokens,
        shape((ROWS, EXPERTS), F32),
        shape((ROWS, 1), F32),
        shape((8, WIDTH), F32),
        shape((16, ROWS), F32),
    ]


def backward_shapes():
    return [
        shape((4, ROWS, WIDTH)),
        shape((ROWS, WIDTH)),
        shape((8, WIDTH), F32),
        shape((EXPERTS, WIDTH), F32),
        shape((16, ROWS), F32),
    ]


def exchange(block):
    dims = block.shape
    pieces = lax.all_to_all(
        block.reshape((64, dims[0] // 64, dims[1])), BOTH, split_axis=0, concat_axis=0, tiled=True
    )
    return pieces.reshape(dims)


def shards(
    block_in,
    cotangent,
    lengths,
    routes,
    query_weight,
    key_weight,
    value_weight,
    out_weight,
    attn_gain,
    moe_gain,
    router,
    rel_table,
    expert_in,
    expert_out,
):
    core = lax.axis_index("section")
    half = lax.axis_index("shard")
    first_core = core == 0
    lower = half == 0

    def pick(left, right):
        return jnp.where(first_core, left, right)

    small = pl.pallas_call(
        pack_kernel, out_shape=shape((64, HALF)), name="pack_small"
    )(router[0], attn_gain, moe_gain, rel_table[0])
    small_arrived = lax.ppermute(small, "shard", [(0, 1), (1, 0)])

    weights_own = [w[0] for w in (query_weight, key_weight, value_weight, out_weight)]

    def cross_one_core(block, section, flip):
        pairs = []
        for part in range(64):
            source = section * 64 + part
            target = section * 64 + (part ^ 32 ^ flip)
            pairs.append((source, target))
        return lax.ppermute(block, ("section", "shard", "replica"), pairs)

    arrived0 = [cross_one_core(w, 0, number % 2) for number, w in enumerate(weights_own)]
    weights_swapped = [swap(w) for w in weights_own]
    small, small_arrived = lax.optimization_barrier((small, small_arrived, arrived0[0]))[:2]
    smalls = [small, swap(small), small_arrived, swap(small_arrived)]
    passed0 = [swap(w) for w in arrived0[:3]]
    bucket_hot = np.eye(NB, dtype=np.float32)[bucket_of_distance(ROWS)]
    turned = bucket_hot[(-np.arange(ROWS)) % ROWS]

    turned_hot = jnp.asarray(turned.T, BF)

    routes_other = swap(pick(routes[0, 1], routes[0, 0]))
    routes_mine = pick(routes[0, 0], routes[0, 1])
    layer_routes = [pick(routes_mine, routes_other), pick(routes_other, routes_mine)]
    runs = pick(lengths[0, 0], lengths[1, 0])
    info = jnp.concatenate(
        [jnp.stack([core, half]).astype(jnp.int32), jnp.cumsum(runs, dtype=jnp.int32)]
    )

    tied = lax.optimization_barrier(
        (arrived0[3], info, *layer_routes, *smalls, *weights_swapped)
    )
    arrived0[3], info = tied[:2]
    layer_routes, smalls, weights_swapped = list(tied[2:4]), list(tied[4:8]), list(tied[8:])
    passed0.append(swap(arrived0[3]))
    later = lax.optimization_barrier(tuple(weights_own) + tuple(arrived0))[:4]
    arrived1 = [cross_one_core(w, 1, number % 2) for number, w in enumerate(later)]
    passed1 = [swap(w) for w in arrived1]
    weights = [[], []]
    for number in range(4):
        own = [weights_own[number], weights_swapped[number]]
        weights[0] += own + [arrived0[number], passed0[number]]
        weights[1] += own + [arrived1[number], passed1[number]]
    experts = []
    for w in lax.optimization_barrier((expert_in[0, 0], expert_out[0, 0], *passed0))[:2]:
        experts += [w, swap(w)]

    *kept0, send = whole_call(
        first_forward_kernel,
        forward_shapes() + [shape((512, WIDTH))],
        "attend_first",
        [info, layer_routes[0], block_in],
        weights[0],
        [*smalls, turned_hot],
    )
    rows0 = exchange(send)
    hidden = expert_in.shape[3]
    sum_scratch = pltpu.VMEM((512, WIDTH), F32)
    (made,) = whole_call(
        expert_forward_kernel,
        [shape((512, WIDTH))],
        "expert_first",
        [info, rows0],
        experts,
        scratch=expert_scratch(hidden, False) + [sum_scratch],
    )
    back = exchange(made)
    n10, q0, k0, v0, mixed0, resid0, n20, prob0, gate0, gains0, bias0 = kept0
    *kept1, send, middle, combined0 = whole_call(
        second_forward_kernel,
        forward_shapes()
        + [shape((1024, WIDTH)), shape((ROWS, WIDTH)), shape((ROWS, WIDTH), F32)],
        "attend_second",
        [info, layer_routes[1], layer_routes[0], resid0, gate0, back, cotangent],
        weights[1],
        [*smalls, turned_hot],
    )
    both = exchange(send)
    grad_shapes = [shape((WIDTH, hidden)), shape((hidden, WIDTH))] * 2
    back, *expert_grads = whole_call(
        expert_both_kernel,
        [shape((1024, WIDTH))] + grad_shapes,
        "expert_second",
        [info, both],
        experts,
        out_specs=[VMEM] + [HBM] * 4,
        scratch=expert_scratch(hidden, True)
        + [pltpu.VMEM((512, WIDTH), BF)] * 2
        + [pltpu.VMEM((WIDTH, 512), BF)]
        + [sum_scratch] * 2,
    )
    back = exchange(back)
    n11, q1, k1, v1, mixed1, resid1, n21, prob1, gate1, gains1, bias1 = kept1
    *grads1, result, send = whole_call(
        last_backward_kernel,
        backward_shapes() + [shape((ROWS, WIDTH)), shape((512, WIDTH))],
        "attend_second_back",
        [info, layer_routes[1], layer_routes[0], gate0, cotangent, back]
        + [middle, q1, k1, v1, resid1, n21, prob1, gate1],
        weights[1],
        [gains1, *smalls, bias1],
    )
    made_grads = exchange(send)
    back, *expert_grads = whole_call(
        expert_backward_kernel,
        [shape((512, WIDTH))] + grad_shapes,
        "expert_first_back",
        [info, rows0, made_grads],
        experts + expert_grads,
        out_specs=[VMEM] + [HBM] * 4,
        scratch=expert_scratch(hidden, True) + [pltpu.VMEM((WIDTH, 512), BF), sum_scratch],
        input_output_aliases={7: 1, 8: 2, 9: 3, 10: 4},
    )
    back = exchange(back)
    grads0 = whole_call(
        first_backward_kernel,
        backward_shapes(),
        "attend_first_back",
        [info, layer_routes[0], combined0, grads1[1], back]
        + [block_in, q0, k0, v0, resid0, n20, prob0, gate0],
        weights[0],
        [gains0, *smalls, bias0],
    )

    def small_rows(gain_grad, router_grad, diag):
        table = lax.dot_general(
            diag[:HEADS],
            jnp.asarray(bucket_hot[::-1]),
            (((1,), (0,)), ((), ())),
            precision=lax.Precision.HIGHEST,
            preferred_element_type=F32,
        )
        table = jnp.transpose(table.reshape(HEADS, 2, NB // 2), (1, 0, 2))
        table = jnp.pad(table, ((0, 0), (0, 0), (0, HALF - NB // 2)))
        gains = jnp.transpose(gain_grad[:2].reshape(2, 2, HALF), (1, 0, 2))
        others = jnp.concatenate([gains, table, jnp.zeros((2, EXPERTS - HEADS - 2, HALF), F32)], axis=1)
        routers = jnp.transpose(router_grad.reshape(EXPERTS, 2, HALF), (1, 0, 2))
        return jnp.stack([routers, others], axis=2).astype(BF)

    def summed_cores(n1, mixed, grads):
        keep, send = whole_call(
            weight_grad_kernel,
            [shape((2, 4, HALF, HALF))] * 2,
            "weight_grads",
            [info, n1, mixed, grads[0]],
        )
        return keep, swap(send)

    keep1, got1 = summed_cores(n11, mixed1, grads1)
    small1 = small_rows(*grads1[2:]).reshape(64, 2, HALF)
    keep0, got0 = summed_cores(n10, mixed0, grads0)
    small0 = small_rows(*grads0[2:]).reshape(64, 2, HALF)
    expert_got = [swap(g) for g in expert_grads[2:]]
    keep0, *expert_got = lax.optimization_barrier((keep0, *expert_got))

    small_grads = jnp.pad(small0, ((0, 0), (0, 6), (0, 0))) + jnp.pad(small1, ((0, 0), (2, 4), (0, 0)))
    pieces = merge_call([keep0, got0, keep1, got1], small_grads)
    pieces = lax.all_to_all(pieces, BOTH, split_axis=0, concat_axis=0, tiled=True)
    total = jnp.sum(pieces.astype(F32), axis=0).astype(BF)
    expert_totals = [k.astype(F32) + g.astype(F32) for k, g in zip(expert_grads[:2], expert_got)]

    def by_micro(first, second):
        mine, theirs = pick(first, second), swap(pick(second, first))
        return jnp.stack([pick(mine, theirs), pick(theirs, mine)])

    section_out = by_micro(middle, result)
    input_grad = by_micro(grads0[1], grads1[1])
    total, section_out, input_grad, *expert_totals = lax.optimization_barrier(
        (total, section_out, input_grad, *expert_totals)
    )
    per_layer = jnp.stack(
        [
            jnp.concatenate([total[:48], total[96:98], jnp.zeros((6, HALF), BF)]),
            jnp.concatenate([total[48:96], total[98:100], jnp.zeros((6, HALF), BF)]),
        ]
    )
    spread = jnp.broadcast_to(per_layer[:, None], (2, 32, 56, HALF)).reshape(64, 56, HALF)
    whole = lax.all_to_all(
        spread, ("section", "replica"), split_axis=0, concat_axis=0, tiled=True
    ).reshape(2, 32, 56, HALF)
    full = jnp.concatenate([whole[0, :, :48], whole[1, :, :48]], axis=2).astype(F32)
    full = full.reshape(4, HALF, WIDTH)
    smalls = whole[0, :, 48:50].astype(F32) + whole[1, :, 48:50].astype(F32)
    router_grad = jnp.transpose(smalls[:, 0], (1, 0))
    table_grad = jnp.transpose(smalls[2 : 2 + HEADS, 1, : NB // 2], (1, 0))

    return (
        section_out[None],
        input_grad[None],
        full[0][None],
        full[1][None],
        full[2][None],
        full[3][None],
        smalls[0, 1][None],
        smalls[1, 1][None],
        router_grad[None],
        table_grad[None],
        expert_totals[0][None, None],
        expert_totals[1][None, None],
    )


def solution(mesh):
    in_specs = (
        P(None, ("shard", "replica"), None),
        P(None, ("shard", "replica"), None),
        P(None, ("shard", "replica"), None),
        P("section", None, ("shard", "replica"), None),
        P("section", "shard", None),
        P("section", "shard", None),
        P("section", "shard", None),
        P("section", "shard", None),
        P("section", "shard"),
        P("section", "shard"),
        P("section", "shard", None),
        P("section", "shard", None),
        P("section", "replica", None, "shard"),
        P("section", "replica", "shard", None),
    )
    out_specs = (
        P("section", None, ("shard", "replica"), None),
        P("section", None, ("shard", "replica"), None),
        P("section", "shard", None),
        P("section", "shard", None),
        P("section", "shard", None),
        P("section", "shard", None),
        P("section", "shard"),
        P("section", "shard"),
        P("section", "shard", None),
        P("section", "shard", None),
        P("section", "replica", None, "shard"),
        P("section", "replica", "shard", None),
    )
    return jax.shard_map(shards, mesh=mesh, in_specs=in_specs, out_specs=out_specs, check_vma=False)
```

```python
import jax
import jax.numpy as jnp
import numpy as np
from jax import lax
from jax.experimental import pallas as pl
from jax.experimental.pallas import tpu as pltpu
from jax.sharding import PartitionSpec as P

HEADS = 12
HEAD_DIM = 64
NB = 32
MAXDIST = 128
DOCS = 4
ROWS = 128
WIDTH = 768
HALF = 384
EXPERTS = 32
SLOTS = 8
CAPACITY = 6
TIGHT = 4 * CAPACITY
ROW_PLACES = (0, 2 * CAPACITY)
GRAD_PLACES = (CAPACITY, 3 * CAPACITY)
GROUP = 8
MIB = 1024 * 1024
BF = jnp.bfloat16
F32 = jnp.float32

norm_eps = 1e-06
BOTH = ("shard", "replica")


def bucket_of_distance(length):
    distance = np.arange(length)
    exact_count = NB // 2
    log_ratio = np.log(np.maximum(distance, 1) / exact_count) / np.log(MAXDIST / exact_count)
    far_bucket = exact_count + np.floor(log_ratio * (NB - exact_count)).astype(np.int32)
    return np.where(distance < exact_count, distance, np.minimum(far_bucket, NB - 1)).astype(
        np.int32
    )


def swap(block):
    return lax.ppermute(block, "section", [(0, 1), (1, 0)])


def dot(left, right):
    return jnp.dot(left, right, preferred_element_type=F32)


def dot_t(left, right):
    return lax.dot_general(left, right, (((1,), (1,)), ((), ())), preferred_element_type=F32)


def t_dot(left, right):
    return lax.dot_general(left, right, (((0,), (0,)), ((), ())), preferred_element_type=F32)


def in_halves(matrix, lower):
    first, second = matrix[:, :HALF], matrix[:, HALF:]
    return jnp.where(lower, first, second), jnp.where(lower, second, first)


PARTS = 4


class Weights:
    def __init__(self, info_ref, layer, sources, buffers, sems, order):
        self.sources, self.buffers, self.sems, self.here = sources, buffers, sems, set()
        for matrix in order:
            for number in (2 * matrix, 2 * matrix + 1):

                @pl.when(info_ref[0] == layer)
                def _():
                    self.copy(number, 0).start()

                @pl.when(info_ref[0] != layer)
                def _():
                    self.copy(number, 1).start()

    def copy(self, number, place):
        return pltpu.make_async_copy(
            self.sources[2 * number + place], self.buffers.at[number], self.sems.at[number]
        )

    def take(self, number):
        if number not in self.here:
            self.here.add(number)
            self.copy(number, 0).wait()
        return self.buffers[number]

    def pair(self, matrix):
        return self.take(2 * matrix), self.take(2 * matrix + 1)


def project(matrix, lower, halves):
    own_part, other_part = in_halves(matrix, lower)
    return dot(own_part, halves[0]) + dot(other_part, halves[1])


def project_back(matrix, lower, halves):
    own_part = dot_t(matrix, halves[0])
    other_part = dot_t(matrix, halves[1])
    return jnp.concatenate(
        [jnp.where(lower, own_part, other_part), jnp.where(lower, other_part, own_part)], axis=1
    )


def segments(info_ref, axis):
    places = lax.broadcasted_iota(jnp.int32, (ROWS, ROWS), axis)
    found = jnp.zeros((ROWS, ROWS), jnp.int32)
    for run in range(DOCS):
        found = found + (places >= info_ref[2 + run]).astype(jnp.int32)
    return found


def attend_mask(info_ref):
    rows = lax.broadcasted_iota(jnp.int32, (ROWS, ROWS), 0)
    columns = lax.broadcasted_iota(jnp.int32, (ROWS, ROWS), 1)
    return (segments(info_ref, 0) == segments(info_ref, 1)) & (columns <= rows)


def head_prob(queries_own, key_pair, bias_ref, head, mask):
    bias = pltpu.roll(
        jnp.broadcast_to(bias_ref[head : head + 1, :], (ROWS, ROWS)),
        0,
        axis=1,
        stride=1,
        stride_axis=0,
    )
    scores = dot_t(queries_own, key_pair) * HEAD_DIM ** (-0.5) + bias
    scores = jnp.where(mask, scores, -1e30)
    exponent = jnp.exp(scores - jnp.max(scores, axis=-1, keepdims=True))
    return exponent / jnp.sum(exponent, axis=-1, keepdims=True)


def pair_masks():
    lane = lax.broadcasted_iota(jnp.int32, (ROWS, 2 * HEAD_DIM), 1)
    return lane < HEAD_DIM


def only(first, head_in_pair, pair):
    keep = first if head_in_pair == 0 else jnp.logical_not(first)
    return jnp.where(keep, pair, jnp.zeros_like(pair))


def route_hot(routes_ref):
    experts = lax.broadcasted_iota(jnp.int32, (ROWS, EXPERTS), 1)
    return (routes_ref[...] == experts).astype(F32)


def token_slots(routes_ref, info_ref, hot):
    routed = segments(info_ref, 0)[:, :1] < DOCS - 1
    routed_hot = jnp.where(routed, hot, 0.0)
    rows = lax.broadcasted_iota(jnp.int32, (ROWS, ROWS), 0)
    columns = lax.broadcasted_iota(jnp.int32, (ROWS, ROWS), 1)
    earlier = dot((columns < rows).astype(BF), routed_hot.astype(BF))
    place = jnp.sum(routed_hot * earlier, axis=-1, keepdims=True).astype(jnp.int32)
    return jnp.where(routed, place, -1), routes_ref[...]


def slot_table(place, route, group, offset, count):
    lanes = lax.broadcasted_iota(jnp.int32, (ROWS, count), 1) % (EXPERTS * group)
    wanted = jnp.where(place >= 0, route * group + offset + place, -1)
    return (lanes == wanted).astype(BF)


def pack_kernel(router_ref, gain_one_ref, gain_two_ref, table_ref, out_ref):
    table = jnp.pad(table_ref[...].astype(F32), ((0, 0), (0, HALF - HEADS)))
    out_ref[...] = jnp.concatenate(
        [
            router_ref[...].astype(F32).T,
            gain_one_ref[...].astype(F32),
            gain_two_ref[...].astype(F32),
            jnp.zeros((14, HALF), F32),
            table,
        ],
        axis=0,
    ).astype(BF)


def small_halves(info_ref, layer, small_refs):
    here = info_ref[0] == layer
    own = jnp.where(here, small_refs[0][...], small_refs[1][...])
    return own, jnp.where(here, small_refs[2][...], small_refs[3][...])


def unpack_small(small, hot_ref, lower, gains_ref, bias_ref):
    gains = [half[EXPERTS : EXPERTS + 16, :].astype(F32)[:8] for half in small]
    gains_ref[...] = jnp.concatenate(
        [jnp.where(lower, gains[0], gains[1]), jnp.where(lower, gains[1], gains[0])], axis=1
    )
    tables = [half[EXPERTS + 16 :, :ROWS] for half in small]
    low = jnp.where(lower, tables[0], tables[1])
    high = jnp.where(lower, tables[1], tables[0])
    bias = t_dot(low, hot_ref[: NB // 2, :]) + t_dot(high, hot_ref[NB // 2 :, :])
    bias_ref[...] = bias[:16, :]


def forward_attention(inputs_f, info_ref, routes_ref, weights, small, hot_ref, outs):
    lower = info_ref[1] == 0
    n1_ref, q_ref, k_ref, v_ref, mixed_ref, resid_ref, n2_ref, prob_ref, gate_ref = outs[:9]
    gains_ref, bias_ref = outs[9:]
    unpack_small(small, hot_ref, lower, gains_ref, bias_ref)
    scale = lax.rsqrt(jnp.mean(inputs_f * inputs_f, axis=-1, keepdims=True) + norm_eps)
    normed = (inputs_f * scale * gains_ref[0:1, :]).astype(BF)
    n1_ref[...] = normed
    q_ref[...] = project(normed, lower, weights.pair(0)).astype(BF)
    k_ref[...] = project(normed, lower, weights.pair(1)).astype(BF)
    v_ref[...] = project(normed, lower, weights.pair(2)).astype(BF)
    mask = attend_mask(info_ref)
    first = pair_masks()
    for pair in range(HEADS // 2):
        here = slice(pair * 128, pair * 128 + 128)
        q_pair, k_pair, v_pair = q_ref[:, here], k_ref[:, here], v_ref[:, here]
        made = []
        for member in range(2):
            prob = head_prob(only(first, member, q_pair), k_pair, bias_ref, 2 * pair + member, mask)
            made.append(dot(prob.astype(BF), v_pair))
        mixed_ref[:, here] = jnp.where(first, made[0], made[1]).astype(BF)
    resid = inputs_f + project(mixed_ref[...], lower, weights.pair(3))
    resid_ref[...] = resid
    scale = lax.rsqrt(jnp.mean(resid * resid, axis=-1, keepdims=True) + norm_eps)
    normed_two = (resid * scale * gains_ref[1:2, :]).astype(BF)
    n2_ref[...] = normed_two
    own_part, other_part = in_halves(normed_two, lower)
    logits = dot_t(own_part, small[0][:EXPERTS]) + dot_t(other_part, small[1][:EXPERTS])
    logit_exp = jnp.exp(logits - jnp.max(logits, axis=-1, keepdims=True))
    prob = logit_exp / jnp.sum(logit_exp, axis=-1, keepdims=True)
    prob_ref[...] = prob
    hot = route_hot(routes_ref)
    gate = jnp.sum(prob * hot, axis=-1, keepdims=True)
    gate_ref[...] = gate
    place, route = token_slots(routes_ref, info_ref, hot)
    return normed_two, gate, place, route


def first_forward_kernel(info_ref, routes_ref, x_ref, *refs):
    small, hot_ref = small_halves(info_ref, 0, refs[16:20]), refs[20]
    outs, send_ref = refs[21:32], refs[32]
    weights = Weights(info_ref, 0, refs[:16], refs[33], refs[34], (0, 1, 2, 3))
    normed_two, _, place, route = forward_attention(
        x_ref[info_ref[0]].astype(F32), info_ref, routes_ref, weights, small, hot_ref, outs
    )
    table = slot_table(place, route, SLOTS, 0, EXPERTS * SLOTS)
    rows = t_dot(table, normed_two).astype(BF)
    send_ref[: EXPERTS * SLOTS, :] = rows
    send_ref[EXPERTS * SLOTS :, :] = rows


def second_forward_kernel(
    info_ref, routes_ref, routes_before_ref, resid_ref, gate_ref, back_ref, cot_ref, *refs
):
    small, hot_ref, outs = small_halves(info_ref, 1, refs[16:20]), refs[20], refs[21:32]
    send_ref, x_ref, combined_ref = refs[32:35]
    weights = Weights(info_ref, 1, refs[:16], refs[35], refs[36], (0, 1, 2, 3))
    place, route = token_slots(routes_before_ref, info_ref, route_hot(routes_before_ref))
    combined = dot(slot_table(place, route, SLOTS, 0, 2 * EXPERTS * SLOTS), back_ref[...])
    combined_ref[...] = combined
    inputs = (resid_ref[...] + gate_ref[...] * combined).astype(BF)
    x_ref[...] = inputs
    normed_two, gate, place, route = forward_attention(
        inputs.astype(F32), info_ref, routes_ref, weights, small, hot_ref, outs
    )
    made_grad = (gate * cot_ref[info_ref[0]].astype(F32)).astype(BF)
    rows = jnp.zeros((EXPERTS * TIGHT, HALF), F32)
    for matrix, offsets in ((normed_two, ROW_PLACES), (made_grad, GRAD_PLACES)):
        for half, offset in enumerate(offsets):
            table = slot_table(place, route, TIGHT, offset, EXPERTS * TIGHT)
            rows = rows + t_dot(table, matrix[:, half * HALF : half * HALF + HALF])
    rows = rows.astype(BF)
    send_ref[: EXPERTS * TIGHT, :] = rows
    send_ref[EXPERTS * TIGHT :, :] = rows


def backward_attention(
    inputs,
    grad_out,
    combined,
    grad_two_rows,
    info_ref,
    routes_ref,
    kept,
    weights,
    gains_ref,
    small,
    bias_ref,
    outs,
):
    lower = info_ref[1] == 0
    q_ref, k_ref, v_ref, resid_ref, n2_ref, prob_ref, gate_ref = kept
    grads_ref, input_grad_ref, gain_grad_ref, router_grad_ref, diag_ref = outs
    hot = route_hot(routes_ref)
    grad_gate = jnp.sum(grad_out * combined, axis=-1, keepdims=True)
    grad_logits = (grad_gate * gate_ref[...] * (hot - prob_ref[...])).astype(BF)
    router_grad_ref[...] = t_dot(grad_logits, n2_ref[...])
    own_part, other_part = dot(grad_logits, small[0][:EXPERTS]), dot(grad_logits, small[1][:EXPERTS])
    grad_two = grad_two_rows + jnp.concatenate(
        [jnp.where(lower, own_part, other_part), jnp.where(lower, other_part, own_part)], axis=1
    )
    resid = resid_ref[...]
    scale = lax.rsqrt(jnp.mean(resid * resid, axis=-1, keepdims=True) + norm_eps)
    gain_grad_ref[1:2, :] = jnp.sum(grad_two * resid * scale, axis=0, keepdims=True)
    gained = gains_ref[1:2, :] * grad_two
    grad_resid = (
        grad_out
        + scale * gained
        - resid * (scale * scale * scale) * jnp.mean(resid * gained, axis=-1, keepdims=True)
    )
    grad_attn = grad_resid.astype(BF)
    grads_ref[3] = grad_attn
    grad_mixed = project_back(grad_attn, lower, weights.pair(3)).astype(BF)
    mask = attend_mask(info_ref)
    first = pair_masks()
    rows = lax.broadcasted_iota(jnp.int32, (ROWS, ROWS), 0)
    columns = lax.broadcasted_iota(jnp.int32, (ROWS, ROWS), 1)
    flip = (rows + columns == ROWS - 1).astype(BF)
    for pair in range(HEADS // 2):
        here = slice(pair * 128, pair * 128 + 128)
        q_pair, k_pair, v_pair = q_ref[:, here], k_ref[:, here], v_ref[:, here]
        mixed_pair = grad_mixed[:, here]
        made = []
        for member in range(2):
            head = 2 * pair + member
            prob = head_prob(only(first, member, q_pair), k_pair, bias_ref, head, mask)
            grad_prob = dot_t(only(first, member, mixed_pair), v_pair)
            grad_value = t_dot(prob.astype(BF), mixed_pair)
            grad_scores = prob * (grad_prob - jnp.sum(prob * grad_prob, axis=-1, keepdims=True))
            grad_scores = grad_scores.astype(BF)
            turned = pltpu.roll(
                dot(flip, grad_scores), 0, axis=1, stride=1, stride_axis=0
            )
            diag_ref[head : head + 1, :] = jnp.sum(turned, axis=0, keepdims=True)
            made.append(
                (
                    dot(grad_scores, k_pair) * HEAD_DIM ** (-0.5),
                    t_dot(grad_scores, q_pair) * HEAD_DIM ** (-0.5),
                    grad_value,
                )
            )
        for number in range(3):
            grads_ref[number, :, here] = jnp.where(
                first, made[0][number], made[1][number]
            ).astype(BF)
    diag_ref[HEADS:, :] = jnp.zeros((16 - HEADS, ROWS), F32)
    grad_one = project_back(grads_ref[0], lower, weights.pair(0))
    grad_one = grad_one + project_back(grads_ref[1], lower, weights.pair(1))
    grad_one = grad_one + project_back(grads_ref[2], lower, weights.pair(2))
    scale = lax.rsqrt(jnp.mean(inputs * inputs, axis=-1, keepdims=True) + norm_eps)
    gain_grad_ref[0:1, :] = jnp.sum(grad_one * inputs * scale, axis=0, keepdims=True)
    gain_grad_ref[2:, :] = jnp.zeros((6, WIDTH), F32)
    gained = gains_ref[0:1, :] * grad_one
    input_grad = (
        grad_resid
        + scale * gained
        - inputs * (scale * scale * scale) * jnp.mean(inputs * gained, axis=-1, keepdims=True)
    ).astype(BF)
    input_grad_ref[...] = input_grad
    return input_grad


def last_backward_kernel(
    info_ref, routes_ref, routes_before_ref, gate_before_ref, cot_ref, back_ref, *refs
):
    x_ref, kept, gains_ref, bias_ref = refs[0], refs[1:8], refs[24], refs[29]
    small = small_halves(info_ref, 1, refs[25:29])
    outs, result_ref, send_ref = refs[30:35], refs[35], refs[36]
    weights = Weights(info_ref, 1, refs[8:24], refs[37], refs[38], (3, 0, 1, 2))
    gate_ref, resid_ref = kept[6], kept[3]
    place, route = token_slots(routes_ref, info_ref, route_hot(routes_ref))
    gathered = []
    for offsets in (ROW_PLACES, GRAD_PLACES):
        tables = [slot_table(place, route, TIGHT, o, 2 * EXPERTS * TIGHT) for o in offsets]
        gathered.append(jnp.concatenate([dot(t, back_ref[...]) for t in tables], axis=1))
    combined, grad_rows = gathered
    result_ref[...] = (resid_ref[...] + gate_ref[...] * combined).astype(BF)
    input_grad = backward_attention(
        x_ref[...].astype(F32),
        cot_ref[info_ref[0]].astype(F32),
        combined,
        grad_rows,
        info_ref,
        routes_ref,
        kept,
        weights,
        gains_ref,
        small,
        bias_ref,
        outs,
    )
    made_grad = (gate_before_ref[...] * input_grad.astype(F32)).astype(BF)
    place, route = token_slots(routes_before_ref, info_ref, route_hot(routes_before_ref))
    rows = t_dot(slot_table(place, route, SLOTS, 0, EXPERTS * SLOTS), made_grad).astype(BF)
    send_ref[: EXPERTS * SLOTS, :] = rows
    send_ref[EXPERTS * SLOTS :, :] = rows


def first_backward_kernel(info_ref, routes_ref, combined_ref, grad_ref, back_ref, *refs):
    x_ref, kept, gains_ref, bias_ref = refs[0], refs[1:8], refs[24], refs[29]
    small = small_halves(info_ref, 0, refs[25:29])
    outs = refs[30:35]
    weights = Weights(info_ref, 0, refs[8:24], refs[35], refs[36], (3, 0, 1, 2))
    place, route = token_slots(routes_ref, info_ref, route_hot(routes_ref))
    grad_rows = dot(slot_table(place, route, SLOTS, 0, 2 * EXPERTS * SLOTS), back_ref[...])
    backward_attention(
        x_ref[info_ref[0]].astype(F32),
        grad_ref[...].astype(F32),
        combined_ref[...],
        grad_rows,
        info_ref,
        routes_ref,
        kept,
        weights,
        gains_ref,
        small,
        bias_ref,
        outs,
    )


def weight_grad_kernel(info_ref, n1_ref, mixed_ref, grads_ref, keep_ref, send_ref):
    first_core = info_ref[0] == 0
    n1_turned, mixed_turned = n1_ref[...].T, mixed_ref[...].T
    for number in range(4):
        left = mixed_turned if number == 3 else n1_turned
        kept, sent = in_halves(grads_ref[number], first_core)
        for half in range(2):
            rows = left[half * HALF : half * HALF + HALF, :]
            keep_ref[half, number] = dot(rows, kept).astype(BF)
            send_ref[half, number] = dot(rows, sent).astype(BF)


def merge_kernel(*refs):
    far, out_far = refs[:5], refs[5]
    keep0_ref, got0_ref, keep1_ref, got1_ref, small_ref, out_ref, sems = refs[6:]
    near, size = refs[6:11], 64 // PARTS

    def copy(source, target, number, part):
        here = pl.ds(part * size, size)
        return pltpu.make_async_copy(source.at[here], target.at[here], sems.at[number, part])

    for part in range(PARTS):
        for number in range(5):
            copy(far[number], near[number], number, part).start()
    for part in range(PARTS):
        here = slice(part * size, part * size + size)
        for number in range(5):
            copy(far[number], near[number], number, part).wait()
        out_ref[here] = jnp.concatenate(
            [
                (keep0_ref[here].astype(F32) + got0_ref[here].astype(F32)).astype(BF),
                (keep1_ref[here].astype(F32) + got1_ref[here].astype(F32)).astype(BF),
                small_ref[here],
            ],
            axis=1,
        )
        copy(out_ref, out_far, 5, part).start()
    for part in range(PARTS):
        copy(out_ref, out_far, 5, part).wait()


def gelu_parts(hidden):
    slope = np.sqrt(2 / np.pi).astype(np.float32)
    square = hidden * hidden
    curve = jnp.tanh(slope * hidden * (1.0 + 0.044715 * square))
    gate = 0.5 * (1.0 + curve)
    grad = gate + 0.5 * hidden * (1.0 - curve * curve) * slope * (1.0 + 3 * 0.044715 * square)
    return hidden * gate, grad


class Chunks:
    def __init__(self, info_ref, layer, refs, win, wout, sems):
        self.info_ref, self.layer, self.refs = info_ref, layer, refs
        self.win, self.wout, self.sems = win, wout, sems
        for chunk in range(win.shape[0]):

            @pl.when(info_ref[0] == layer)
            def _():
                for copy in self.copies(0, chunk):
                    copy.start()

            @pl.when(info_ref[0] != layer)
            def _():
                for copy in self.copies(1, chunk):
                    copy.start()

    def copies(self, place, chunk):
        here = pl.ds(pl.multiple_of(chunk * BLOCK, BLOCK), BLOCK)
        return (
            pltpu.make_async_copy(
                self.refs[place].at[:, here], self.win.at[chunk], self.sems.at[0, chunk]
            ),
            pltpu.make_async_copy(
                self.refs[2 + place].at[here, :], self.wout.at[chunk], self.sems.at[1, chunk]
            ),
        )

    def take(self, chunk):
        for copy in self.copies(0, chunk):
            copy.wait()
        return self.win[chunk], self.wout[chunk]

    def grads_to(self, targets, din, dout, sems):
        self.targets, self.din, self.dout, self.out_sems = targets, din, dout, sems

    def grad_copies(self, place, chunk):
        here = pl.ds(pl.multiple_of(chunk * BLOCK, BLOCK), BLOCK)
        return (
            pltpu.make_async_copy(
                self.din.at[chunk], self.targets[2 * place].at[:, here], self.out_sems.at[0, chunk]
            ),
            pltpu.make_async_copy(
                self.dout.at[chunk],
                self.targets[2 * place + 1].at[here, :],
                self.out_sems.at[1, chunk],
            ),
        )

    def put(self, chunk):
        @pl.when(self.info_ref[0] == self.layer)
        def _():
            for copy in self.grad_copies(0, chunk):
                copy.start()

        @pl.when(self.info_ref[0] != self.layer)
        def _():
            for copy in self.grad_copies(1, chunk):
                copy.start()

    def finish(self):
        for chunk in range(self.din.shape[0]):
            for copy in self.grad_copies(0, chunk):
                copy.wait()


def expert_forward_kernel(info_ref, rows_ref, *refs):
    made_ref, win, wout, sems, made_sum = refs[4:]
    chunks = Chunks(info_ref, 0, refs[:4], win, wout, sems)
    made_sum[...] = jnp.zeros_like(made_sum)

    @pl.loop(0, win.shape[0])
    def _(chunk):
        w_in, w_out = chunks.take(chunk)
        act, _ = gelu_parts(dot(rows_ref[...], w_in))
        made_sum[...] += dot(act.astype(BF), w_out)

    made_ref[...] = made_sum[...].astype(BF)


def expert_backward_kernel(info_ref, rows_ref, grad_ref, *refs):
    back_ref, targets = refs[8], refs[9:13]
    win, wout, sems, din, dout, out_sems, rows_turned, rows_sum = refs[13:]
    chunks = Chunks(info_ref, 0, refs[:4], win, wout, sems)
    chunks.grads_to(targets, din, dout, out_sems)
    rows_sum[...] = jnp.zeros_like(rows_sum)
    rows_turned[...] = rows_ref[...].T

    @pl.loop(0, win.shape[0])
    def _(chunk):
        w_in, w_out = chunks.take(chunk)
        act, slope = gelu_parts(dot(rows_ref[...], w_in))
        grad_pre = (slope * dot_t(grad_ref[...], w_out)).astype(BF)
        dout[chunk] = t_dot(act.astype(BF), grad_ref[...]).astype(BF)
        din[chunk] = dot(rows_turned[...], grad_pre).astype(BF)
        chunks.put(chunk)
        rows_sum[...] += dot_t(grad_pre, w_in)

    back_ref[...] = rows_sum[...].astype(BF)
    chunks.finish()


def piece_order():
    order = np.zeros((GROUP * TIGHT, GROUP * TIGHT), np.float32)
    row = 0
    for offset in ROW_PLACES + GRAD_PLACES:
        for piece in range(GROUP):
            for slot in range(CAPACITY):
                order[row, piece * TIGHT + offset + slot] = 1
                row += 1
    return jnp.asarray(np.stack([order, order.T]), BF)


def expert_both_kernel(info_ref, both_ref, order_ref, *refs):
    back_ref, targets = refs[4], refs[5:9]
    win, wout, sems, din, dout, out_sems, rows, grads, rows_turned, made_sum, rows_sum = refs[9:]
    chunks = Chunks(info_ref, 1, refs[:4], win, wout, sems)
    chunks.grads_to(targets, din, dout, out_sems)
    packed, count = GROUP * TIGHT, GROUP * CAPACITY
    groups = both_ref.shape[0] // packed
    for group in range(groups):
        here = slice(group * count, group * count + count)
        block = dot(order_ref[0], both_ref[group * packed : group * packed + packed, :]).astype(BF)
        rows[here, :HALF] = block[:count]
        rows[here, HALF:] = block[count : 2 * count]
        grads[here, :HALF] = block[2 * count : 3 * count]
        grads[here, HALF:] = block[3 * count :]
    made_sum[...] = jnp.zeros_like(made_sum)
    rows_sum[...] = jnp.zeros_like(rows_sum)
    rows_turned[...] = rows[...].T

    @pl.loop(0, win.shape[0])
    def _(chunk):
        w_in, w_out = chunks.take(chunk)
        act, slope = gelu_parts(dot(rows[...], w_in))
        act = act.astype(BF)
        grad_pre = (slope * dot_t(grads[...], w_out)).astype(BF)
        dout[chunk] = t_dot(act, grads[...]).astype(BF)
        din[chunk] = dot(rows_turned[...], grad_pre).astype(BF)
        chunks.put(chunk)
        made_sum[...] += dot(act, w_out)
        rows_sum[...] += dot_t(grad_pre, w_in)

    for group in range(groups):
        here = slice(group * count, group * count + count)
        block = jnp.concatenate(
            [
                made_sum[here, :HALF],
                made_sum[here, HALF:],
                rows_sum[here, :HALF],
                rows_sum[here, HALF:],
            ],
            axis=0,
        ).astype(BF)
        back_ref[group * packed : group * packed + packed, :] = dot(order_ref[1], block).astype(BF)
    chunks.finish()


def shape(dims, kind=BF):
    return jax.ShapeDtypeStruct(dims, kind)


SMEM = pl.BlockSpec(memory_space=pltpu.SMEM)
VMEM = pl.BlockSpec(memory_space=pltpu.VMEM)
HBM = pl.BlockSpec(memory_space=pltpu.HBM)
BLOCK = 512


def whole_call(kernel, out_shape, name, before, weights=(), after=(), **more):
    scratch = []
    if len(weights) == 16:
        scratch = [pltpu.VMEM((8, HALF, WIDTH), BF), pltpu.SemaphoreType.DMA((8,))]
    return pl.pallas_call(
        kernel,
        out_shape=out_shape,
        in_specs=[SMEM] + [VMEM] * (len(before) - 1) + [HBM] * len(weights) + [VMEM] * len(after),
        out_specs=more.pop("out_specs", [VMEM] * len(out_shape)),
        scratch_shapes=more.pop("scratch", scratch),
        name=name,
        compiler_params=pltpu.CompilerParams(vmem_limit_bytes=60 * MIB),
        **more,
    )(*before, *weights, *after)


def merge_call(sums, smalls):
    return pl.pallas_call(
        merge_kernel,
        out_shape=shape((64, 104, HALF)),
        in_specs=[HBM] * 5,
        out_specs=HBM,
        scratch_shapes=[pltpu.VMEM((64, 48, HALF), BF)] * 4
        + [pltpu.VMEM((64, 8, HALF), BF), pltpu.VMEM((64, 104, HALF), BF)]
        + [pltpu.SemaphoreType.DMA((6, PARTS))],
        name="merge_grads",
        compiler_params=pltpu.CompilerParams(vmem_limit_bytes=60 * MIB),
    )(*[part.reshape(64, 48, HALF) for part in sums], smalls)


def expert_scratch(hidden, grads):
    count = hidden // BLOCK
    moved = [
        pltpu.VMEM((count, WIDTH, BLOCK), BF),
        pltpu.VMEM((count, BLOCK, WIDTH), BF),
        pltpu.SemaphoreType.DMA((2, count)),
    ]
    return moved * (2 if grads else 1)


def forward_shapes():
    tokens = shape((ROWS, WIDTH))
    return [
        tokens,
        tokens,
        tokens,
        tokens,
        tokens,
        shape((ROWS, WIDTH), F32),
        tokens,
        shape((ROWS, EXPERTS), F32),
        shape((ROWS, 1), F32),
        shape((8, WIDTH), F32),
        shape((16, ROWS), F32),
    ]


def backward_shapes():
    return [
        shape((4, ROWS, WIDTH)),
        shape((ROWS, WIDTH)),
        shape((8, WIDTH), F32),
        shape((EXPERTS, WIDTH), F32),
        shape((16, ROWS), F32),
    ]


def exchange(block):
    dims = block.shape
    pieces = lax.all_to_all(
        block.reshape((64, dims[0] // 64, dims[1])), BOTH, split_axis=0, concat_axis=0, tiled=True
    )
    return pieces.reshape(dims)


def shards(
    block_in,
    cotangent,
    lengths,
    routes,
    query_weight,
    key_weight,
    value_weight,
    out_weight,
    attn_gain,
    moe_gain,
    router,
    rel_table,
    expert_in,
    expert_out,
):
    core = lax.axis_index("section")
    half = lax.axis_index("shard")
    first_core = core == 0
    lower = half == 0

    def pick(left, right):
        return jnp.where(first_core, left, right)

    small = pl.pallas_call(
        pack_kernel, out_shape=shape((64, HALF)), name="pack_small"
    )(router[0], attn_gain, moe_gain, rel_table[0])
    small_arrived = lax.ppermute(small, "shard", [(0, 1), (1, 0)])

    weights_own = [w[0] for w in (query_weight, key_weight, value_weight, out_weight)]

    def cross_one_core(block, section, flip):
        pairs = []
        for part in range(64):
            source = section * 64 + part
            target = section * 64 + (part ^ 32 ^ flip)
            pairs.append((source, target))
        return lax.ppermute(block, ("section", "shard", "replica"), pairs)

    arrived0 = [cross_one_core(w, 0, number % 2) for number, w in enumerate(weights_own)]
    weights_swapped = [swap(w) for w in weights_own]
    small, small_arrived = lax.optimization_barrier((small, small_arrived, arrived0[0]))[:2]
    smalls = [small, swap(small), small_arrived, swap(small_arrived)]
    passed0 = [swap(w) for w in arrived0[:3]]
    bucket_hot = np.eye(NB, dtype=np.float32)[bucket_of_distance(ROWS)]
    turned = bucket_hot[(-np.arange(ROWS)) % ROWS]

    turned_hot = jnp.asarray(turned.T, BF)

    routes_other = swap(pick(routes[0, 1], routes[0, 0]))
    routes_mine = pick(routes[0, 0], routes[0, 1])
    layer_routes = [pick(routes_mine, routes_other), pick(routes_other, routes_mine)]
    runs = pick(lengths[0, 0], lengths[1, 0])
    info = jnp.concatenate(
        [jnp.stack([core, half]).astype(jnp.int32), jnp.cumsum(runs, dtype=jnp.int32)]
    )

    tied = lax.optimization_barrier(
        (arrived0[3], info, *layer_routes, *smalls, *weights_swapped)
    )
    arrived0[3], info = tied[:2]
    layer_routes, smalls, weights_swapped = list(tied[2:4]), list(tied[4:8]), list(tied[8:])
    passed0.append(swap(arrived0[3]))
    later = lax.optimization_barrier(tuple(weights_own) + tuple(arrived0))[:4]
    arrived1 = [cross_one_core(w, 1, number % 2) for number, w in enumerate(later)]
    passed1 = [swap(w) for w in arrived1]
    weights = [[], []]
    for number in range(4):
        own = [weights_own[number], weights_swapped[number]]
        weights[0] += own + [arrived0[number], passed0[number]]
        weights[1] += own + [arrived1[number], passed1[number]]
    experts = []
    for w in lax.optimization_barrier((expert_in[0, 0], expert_out[0, 0], *passed0))[:2]:
        experts += [w, swap(w)]

    *kept0, send = whole_call(
        first_forward_kernel,
        forward_shapes() + [shape((512, WIDTH))],
        "attend_first",
        [info, layer_routes[0], block_in],
        weights[0],
        [*smalls, turned_hot],
    )
    rows0 = exchange(send)
    hidden = expert_in.shape[3]
    sum_scratch = pltpu.VMEM((512, WIDTH), F32)
    (made,) = whole_call(
        expert_forward_kernel,
        [shape((512, WIDTH))],
        "expert_first",
        [info, rows0],
        experts,
        scratch=expert_scratch(hidden, False) + [sum_scratch],
    )
    back = exchange(made)
    n10, q0, k0, v0, mixed0, resid0, n20, prob0, gate0, gains0, bias0 = kept0
    *kept1, send, middle, combined0 = whole_call(
        second_forward_kernel,
        forward_shapes()
        + [shape((64 * TIGHT, HALF)), shape((ROWS, WIDTH)), shape((ROWS, WIDTH), F32)],
        "attend_second",
        [info, layer_routes[1], layer_routes[0], resid0, gate0, back, cotangent],
        weights[1],
        [*smalls, turned_hot],
    )
    both = exchange(send)
    grad_shapes = [shape((WIDTH, hidden)), shape((hidden, WIDTH))] * 2
    back, *expert_grads = whole_call(
        expert_both_kernel,
        [shape((64 * TIGHT, HALF))] + grad_shapes,
        "expert_second",
        [info, both, piece_order()],
        experts,
        out_specs=[VMEM] + [HBM] * 4,
        scratch=expert_scratch(hidden, True)
        + [pltpu.VMEM((64 * CAPACITY, WIDTH), BF)] * 2
        + [pltpu.VMEM((WIDTH, 64 * CAPACITY), BF)]
        + [pltpu.VMEM((64 * CAPACITY, WIDTH), F32)] * 2,
    )
    back = exchange(back)
    n11, q1, k1, v1, mixed1, resid1, n21, prob1, gate1, gains1, bias1 = kept1
    *grads1, result, send = whole_call(
        last_backward_kernel,
        backward_shapes() + [shape((ROWS, WIDTH)), shape((512, WIDTH))],
        "attend_second_back",
        [info, layer_routes[1], layer_routes[0], gate0, cotangent, back]
        + [middle, q1, k1, v1, resid1, n21, prob1, gate1],
        weights[1],
        [gains1, *smalls, bias1],
    )
    made_grads = exchange(send)
    back, *expert_grads = whole_call(
        expert_backward_kernel,
        [shape((512, WIDTH))] + grad_shapes,
        "expert_first_back",
        [info, rows0, made_grads],
        experts + expert_grads,
        out_specs=[VMEM] + [HBM] * 4,
        scratch=expert_scratch(hidden, True) + [pltpu.VMEM((WIDTH, 512), BF), sum_scratch],
        input_output_aliases={7: 1, 8: 2, 9: 3, 10: 4},
    )
    back = exchange(back)
    grads0 = whole_call(
        first_backward_kernel,
        backward_shapes(),
        "attend_first_back",
        [info, layer_routes[0], combined0, grads1[1], back]
        + [block_in, q0, k0, v0, resid0, n20, prob0, gate0],
        weights[0],
        [gains0, *smalls, bias0],
    )

    def small_rows(gain_grad, router_grad, diag):
        table = lax.dot_general(
            diag[:HEADS],
            jnp.asarray(bucket_hot[::-1]),
            (((1,), (0,)), ((), ())),
            precision=lax.Precision.HIGHEST,
            preferred_element_type=F32,
        )
        table = jnp.transpose(table.reshape(HEADS, 2, NB // 2), (1, 0, 2))
        table = jnp.pad(table, ((0, 0), (0, 0), (0, HALF - NB // 2)))
        gains = jnp.transpose(gain_grad[:2].reshape(2, 2, HALF), (1, 0, 2))
        others = jnp.concatenate([gains, table, jnp.zeros((2, EXPERTS - HEADS - 2, HALF), F32)], axis=1)
        routers = jnp.transpose(router_grad.reshape(EXPERTS, 2, HALF), (1, 0, 2))
        return jnp.stack([routers, others], axis=2).astype(BF)

    def summed_cores(n1, mixed, grads):
        keep, send = whole_call(
            weight_grad_kernel,
            [shape((2, 4, HALF, HALF))] * 2,
            "weight_grads",
            [info, n1, mixed, grads[0]],
        )
        return keep, swap(send)

    keep1, got1 = summed_cores(n11, mixed1, grads1)
    small1 = small_rows(*grads1[2:]).reshape(64, 2, HALF)
    keep0, got0 = summed_cores(n10, mixed0, grads0)
    small0 = small_rows(*grads0[2:]).reshape(64, 2, HALF)
    expert_got = [swap(g) for g in expert_grads[2:]]
    keep0, *expert_got = lax.optimization_barrier((keep0, *expert_got))

    small_grads = jnp.pad(small0, ((0, 0), (0, 6), (0, 0))) + jnp.pad(small1, ((0, 0), (2, 4), (0, 0)))
    pieces = merge_call([keep0, got0, keep1, got1], small_grads)
    pieces = lax.all_to_all(pieces, BOTH, split_axis=0, concat_axis=0, tiled=True)
    total = jnp.sum(pieces.astype(F32), axis=0).astype(BF)
    expert_totals = [k.astype(F32) + g.astype(F32) for k, g in zip(expert_grads[:2], expert_got)]

    def by_micro(first, second):
        mine, theirs = pick(first, second), swap(pick(second, first))
        return jnp.stack([pick(mine, theirs), pick(theirs, mine)])

    section_out = by_micro(middle, result)
    input_grad = by_micro(grads0[1], grads1[1])
    total, section_out, input_grad, *expert_totals = lax.optimization_barrier(
        (total, section_out, input_grad, *expert_totals)
    )
    per_layer = jnp.stack(
        [
            jnp.concatenate([total[:48], total[96:98], jnp.zeros((6, HALF), BF)]),
            jnp.concatenate([total[48:96], total[98:100], jnp.zeros((6, HALF), BF)]),
        ]
    )
    spread = jnp.broadcast_to(per_layer[:, None], (2, 32, 56, HALF)).reshape(64, 56, HALF)
    whole = lax.all_to_all(
        spread, ("section", "replica"), split_axis=0, concat_axis=0, tiled=True
    ).reshape(2, 32, 56, HALF)
    full = jnp.concatenate([whole[0, :, :48], whole[1, :, :48]], axis=2).astype(F32)
    full = full.reshape(4, HALF, WIDTH)
    smalls = whole[0, :, 48:50].astype(F32) + whole[1, :, 48:50].astype(F32)
    router_grad = jnp.transpose(smalls[:, 0], (1, 0))
    table_grad = jnp.transpose(smalls[2 : 2 + HEADS, 1, : NB // 2], (1, 0))

    return (
        section_out[None],
        input_grad[None],
        full[0][None],
        full[1][None],
        full[2][None],
        full[3][None],
        smalls[0, 1][None],
        smalls[1, 1][None],
        router_grad[None],
        table_grad[None],
        expert_totals[0][None, None],
        expert_totals[1][None, None],
    )


def solution(mesh):
    in_specs = (
        P(None, ("shard", "replica"), None),
        P(None, ("shard", "replica"), None),
        P(None, ("shard", "replica"), None),
        P("section", None, ("shard", "replica"), None),
        P("section", "shard", None),
        P("section", "shard", None),
        P("section", "shard", None),
        P("section", "shard", None),
        P("section", "shard"),
        P("section", "shard"),
        P("section", "shard", None),
        P("section", "shard", None),
        P("section", "replica", None, "shard"),
        P("section", "replica", "shard", None),
    )
    out_specs = (
        P("section", None, ("shard", "replica"), None),
        P("section", None, ("shard", "replica"), None),
        P("section", "shard", None),
        P("section", "shard", None),
        P("section", "shard", None),
        P("section", "shard", None),
        P("section", "shard"),
        P("section", "shard"),
        P("section", "shard", None),
        P("section", "shard", None),
        P("section", "replica", None, "shard"),
        P("section", "replica", "shard", None),
    )
    return jax.shard_map(shards, mesh=mesh, in_specs=in_specs, out_specs=out_specs, check_vma=False)
```

```python
import jax
import jax.numpy as jnp
import numpy as np
from jax import lax
from jax.experimental import pallas as pl
from jax.experimental.pallas import tpu as pltpu
from jax.sharding import PartitionSpec as P

HEADS = 12
HEAD_DIM = 64
NB = 32
MAXDIST = 128
DOCS = 4
ROWS = 128
WIDTH = 768
HALF = 384
EXPERTS = 32
SLOTS = 8
CAPACITY = 6
TIGHT = 4 * CAPACITY
ROW_PLACES = (0, 2 * CAPACITY)
GRAD_PLACES = (CAPACITY, 3 * CAPACITY)
GROUP = 8
MIB = 1024 * 1024
BF = jnp.bfloat16
F32 = jnp.float32

norm_eps = 1e-06
BOTH = ("shard", "replica")


def bucket_of_distance(length):
    distance = np.arange(length)
    exact_count = NB // 2
    log_ratio = np.log(np.maximum(distance, 1) / exact_count) / np.log(MAXDIST / exact_count)
    far_bucket = exact_count + np.floor(log_ratio * (NB - exact_count)).astype(np.int32)
    return np.where(distance < exact_count, distance, np.minimum(far_bucket, NB - 1)).astype(
        np.int32
    )


def swap(block):
    return lax.ppermute(block, "section", [(0, 1), (1, 0)])


def dot(left, right):
    return jnp.dot(left, right, preferred_element_type=F32)


def dot_t(left, right):
    return lax.dot_general(left, right, (((1,), (1,)), ((), ())), preferred_element_type=F32)


def t_dot(left, right):
    return lax.dot_general(left, right, (((0,), (0,)), ((), ())), preferred_element_type=F32)


def in_halves(matrix, lower):
    first, second = matrix[:, :HALF], matrix[:, HALF:]
    return jnp.where(lower, first, second), jnp.where(lower, second, first)


PARTS = 4


class Weights:
    def __init__(self, info_ref, layer, sources, buffers, sems, order):
        self.sources, self.buffers, self.sems, self.here = sources, buffers, sems, set()
        for matrix in order:
            for number in (2 * matrix, 2 * matrix + 1):

                @pl.when(info_ref[0] == layer)
                def _():
                    self.copy(number, 0).start()

                @pl.when(info_ref[0] != layer)
                def _():
                    self.copy(number, 1).start()

    def copy(self, number, place):
        return pltpu.make_async_copy(
            self.sources[2 * number + place], self.buffers.at[number], self.sems.at[number]
        )

    def take(self, number):
        if number not in self.here:
            self.here.add(number)
            self.copy(number, 0).wait()
        return self.buffers[number]

    def pair(self, matrix):
        return self.take(2 * matrix), self.take(2 * matrix + 1)


def project(matrix, lower, halves):
    own_part, other_part = in_halves(matrix, lower)
    return dot(own_part, halves[0]) + dot(other_part, halves[1])


def project_back(matrix, lower, halves):
    own_part = dot_t(matrix, halves[0])
    other_part = dot_t(matrix, halves[1])
    return jnp.concatenate(
        [jnp.where(lower, own_part, other_part), jnp.where(lower, other_part, own_part)], axis=1
    )


def segments(info_ref, axis):
    places = lax.broadcasted_iota(jnp.int32, (ROWS, ROWS), axis)
    found = jnp.zeros((ROWS, ROWS), jnp.int32)
    for run in range(DOCS):
        found = found + (places >= info_ref[2 + run]).astype(jnp.int32)
    return found


def attend_mask(info_ref):
    rows = lax.broadcasted_iota(jnp.int32, (ROWS, ROWS), 0)
    columns = lax.broadcasted_iota(jnp.int32, (ROWS, ROWS), 1)
    return (segments(info_ref, 0) == segments(info_ref, 1)) & (columns <= rows)


def head_prob(queries_own, key_pair, bias_ref, head, mask):
    bias = pltpu.roll(
        jnp.broadcast_to(bias_ref[head : head + 1, :], (ROWS, ROWS)),
        0,
        axis=1,
        stride=1,
        stride_axis=0,
    )
    scores = dot_t(queries_own, key_pair) * HEAD_DIM ** (-0.5) + bias
    scores = jnp.where(mask, scores, -1e30)
    exponent = jnp.exp(scores - jnp.max(scores, axis=-1, keepdims=True))
    return exponent * (1.0 / jnp.sum(exponent, axis=-1, keepdims=True))


def pair_masks():
    lane = lax.broadcasted_iota(jnp.int32, (ROWS, 2 * HEAD_DIM), 1)
    return lane < HEAD_DIM


def only(first, head_in_pair, pair):
    keep = first if head_in_pair == 0 else jnp.logical_not(first)
    return jnp.where(keep, pair, jnp.zeros_like(pair))


def route_hot(routes_ref):
    experts = lax.broadcasted_iota(jnp.int32, (ROWS, EXPERTS), 1)
    return (routes_ref[...] == experts).astype(F32)


def token_slots(routes_ref, info_ref, hot):
    routed = segments(info_ref, 0)[:, :1] < DOCS - 1
    routed_hot = jnp.where(routed, hot, 0.0)
    rows = lax.broadcasted_iota(jnp.int32, (ROWS, ROWS), 0)
    columns = lax.broadcasted_iota(jnp.int32, (ROWS, ROWS), 1)
    earlier = dot((columns < rows).astype(BF), routed_hot.astype(BF))
    place = jnp.sum(routed_hot * earlier, axis=-1, keepdims=True).astype(jnp.int32)
    return jnp.where(routed, place, -1), routes_ref[...]


def slot_table(place, route, group, offset, count):
    lanes = lax.broadcasted_iota(jnp.int32, (ROWS, EXPERTS * group), 1)
    wanted = jnp.where(place >= 0, route * group + offset + place, -1)
    table = (lanes == wanted).astype(BF)
    return jnp.concatenate([table] * (count // (EXPERTS * group)), axis=1)


def pack_kernel(router_ref, gain_one_ref, gain_two_ref, table_ref, out_ref):
    table = jnp.pad(table_ref[...].astype(F32), ((0, 0), (0, HALF - HEADS)))
    out_ref[...] = jnp.concatenate(
        [
            router_ref[...].astype(F32).T,
            gain_one_ref[...].astype(F32),
            gain_two_ref[...].astype(F32),
            jnp.zeros((14, HALF), F32),
            table,
        ],
        axis=0,
    ).astype(BF)


def small_halves(info_ref, layer, small_refs):
    here = info_ref[0] == layer
    own = jnp.where(here, small_refs[0][...], small_refs[1][...])
    return own, jnp.where(here, small_refs[2][...], small_refs[3][...])


def unpack_small(small, hot_ref, lower, gains_ref, bias_ref):
    gains = [half[EXPERTS : EXPERTS + 16, :].astype(F32)[:8] for half in small]
    gains_ref[...] = jnp.concatenate(
        [jnp.where(lower, gains[0], gains[1]), jnp.where(lower, gains[1], gains[0])], axis=1
    )
    tables = [half[EXPERTS + 16 :, :ROWS] for half in small]
    low = jnp.where(lower, tables[0], tables[1])
    high = jnp.where(lower, tables[1], tables[0])
    bias = t_dot(low, hot_ref[: NB // 2, :]) + t_dot(high, hot_ref[NB // 2 :, :])
    bias_ref[...] = bias[:16, :]


def forward_attention(inputs_f, info_ref, routes_ref, weights, small, hot_ref, outs):
    lower = info_ref[1] == 0
    n1_ref, q_ref, k_ref, v_ref, mixed_ref, resid_ref, n2_ref, prob_ref, gate_ref = outs[:9]
    gains_ref, bias_ref = outs[9:]
    unpack_small(small, hot_ref, lower, gains_ref, bias_ref)
    scale = lax.rsqrt(jnp.mean(inputs_f * inputs_f, axis=-1, keepdims=True) + norm_eps)
    normed = (inputs_f * scale * gains_ref[0:1, :]).astype(BF)
    n1_ref[...] = normed
    q_ref[...] = project(normed, lower, weights.pair(0)).astype(BF)
    k_ref[...] = project(normed, lower, weights.pair(1)).astype(BF)
    v_ref[...] = project(normed, lower, weights.pair(2)).astype(BF)
    mask = attend_mask(info_ref)
    first = pair_masks()
    for pair in range(HEADS // 2):
        here = slice(pair * 128, pair * 128 + 128)
        q_pair, k_pair, v_pair = q_ref[:, here], k_ref[:, here], v_ref[:, here]
        made = []
        for member in range(2):
            prob = head_prob(only(first, member, q_pair), k_pair, bias_ref, 2 * pair + member, mask)
            made.append(dot(prob.astype(BF), v_pair))
        mixed_ref[:, here] = jnp.where(first, made[0], made[1]).astype(BF)
    resid = inputs_f + project(mixed_ref[...], lower, weights.pair(3))
    resid_ref[...] = resid
    scale = lax.rsqrt(jnp.mean(resid * resid, axis=-1, keepdims=True) + norm_eps)
    normed_two = (resid * scale * gains_ref[1:2, :]).astype(BF)
    n2_ref[...] = normed_two
    own_part, other_part = in_halves(normed_two, lower)
    logits = dot_t(own_part, small[0][:EXPERTS]) + dot_t(other_part, small[1][:EXPERTS])
    logit_exp = jnp.exp(logits - jnp.max(logits, axis=-1, keepdims=True))
    prob = logit_exp / jnp.sum(logit_exp, axis=-1, keepdims=True)
    prob_ref[...] = prob
    hot = route_hot(routes_ref)
    gate = jnp.sum(prob * hot, axis=-1, keepdims=True)
    gate_ref[...] = gate
    place, route = token_slots(routes_ref, info_ref, hot)
    return normed_two, gate, place, route


def first_forward_kernel(info_ref, routes_ref, x_ref, *refs):
    small, hot_ref = small_halves(info_ref, 0, refs[16:20]), refs[20]
    outs, send_ref = refs[21:32], refs[32]
    weights = Weights(info_ref, 0, refs[:16], refs[33], refs[34], (0, 1, 2, 3))
    normed_two, _, place, route = forward_attention(
        x_ref[info_ref[0]].astype(F32), info_ref, routes_ref, weights, small, hot_ref, outs
    )
    table = slot_table(place, route, SLOTS, 0, EXPERTS * SLOTS)
    rows = t_dot(table, normed_two).astype(BF)
    send_ref[: EXPERTS * SLOTS, :] = rows
    send_ref[EXPERTS * SLOTS :, :] = rows


def second_forward_kernel(
    info_ref, routes_ref, routes_before_ref, resid_ref, gate_ref, back_ref, cot_ref, *refs
):
    small, hot_ref, outs = small_halves(info_ref, 1, refs[16:20]), refs[20], refs[21:32]
    send_ref, x_ref, combined_ref = refs[32:35]
    weights = Weights(info_ref, 1, refs[:16], refs[35], refs[36], (0, 1, 2, 3))
    place, route = token_slots(routes_before_ref, info_ref, route_hot(routes_before_ref))
    combined = dot(slot_table(place, route, SLOTS, 0, 2 * EXPERTS * SLOTS), back_ref[...])
    combined_ref[...] = combined
    inputs = (resid_ref[...] + gate_ref[...] * combined).astype(BF)
    x_ref[...] = inputs
    normed_two, gate, place, route = forward_attention(
        inputs.astype(F32), info_ref, routes_ref, weights, small, hot_ref, outs
    )
    made_grad = (gate * cot_ref[info_ref[0]].astype(F32)).astype(BF)
    rows = jnp.zeros((EXPERTS * TIGHT, HALF), F32)
    for matrix, offsets in ((normed_two, ROW_PLACES), (made_grad, GRAD_PLACES)):
        for half, offset in enumerate(offsets):
            table = slot_table(place, route, TIGHT, offset, EXPERTS * TIGHT)
            rows = rows + t_dot(table, matrix[:, half * HALF : half * HALF + HALF])
    rows = rows.astype(BF)
    send_ref[: EXPERTS * TIGHT, :] = rows
    send_ref[EXPERTS * TIGHT :, :] = rows


def backward_attention(
    inputs,
    grad_out,
    combined,
    grad_two_rows,
    info_ref,
    routes_ref,
    kept,
    weights,
    gains_ref,
    small,
    bias_ref,
    outs,
):
    lower = info_ref[1] == 0
    q_ref, k_ref, v_ref, resid_ref, n2_ref, prob_ref, gate_ref = kept
    grads_ref, input_grad_ref, gain_grad_ref, router_grad_ref, diag_ref = outs
    hot = route_hot(routes_ref)
    grad_gate = jnp.sum(grad_out * combined, axis=-1, keepdims=True)
    grad_logits = (grad_gate * gate_ref[...] * (hot - prob_ref[...])).astype(BF)
    router_grad_ref[...] = t_dot(grad_logits, n2_ref[...])
    own_part, other_part = dot(grad_logits, small[0][:EXPERTS]), dot(grad_logits, small[1][:EXPERTS])
    grad_two = grad_two_rows + jnp.concatenate(
        [jnp.where(lower, own_part, other_part), jnp.where(lower, other_part, own_part)], axis=1
    )
    resid = resid_ref[...]
    scale = lax.rsqrt(jnp.mean(resid * resid, axis=-1, keepdims=True) + norm_eps)
    gain_grad_ref[1:2, :] = jnp.sum(grad_two * resid * scale, axis=0, keepdims=True)
    gained = gains_ref[1:2, :] * grad_two
    grad_resid = (
        grad_out
        + scale * gained
        - resid * (scale * scale * scale) * jnp.mean(resid * gained, axis=-1, keepdims=True)
    )
    grad_attn = grad_resid.astype(BF)
    grads_ref[3] = grad_attn
    grad_mixed = project_back(grad_attn, lower, weights.pair(3)).astype(BF)
    mask = attend_mask(info_ref)
    first = pair_masks()
    rows = lax.broadcasted_iota(jnp.int32, (ROWS, ROWS), 0)
    columns = lax.broadcasted_iota(jnp.int32, (ROWS, ROWS), 1)
    flip = (rows + columns == ROWS - 1).astype(BF)
    for pair in range(HEADS // 2):
        here = slice(pair * 128, pair * 128 + 128)
        q_pair, k_pair, v_pair = q_ref[:, here], k_ref[:, here], v_ref[:, here]
        mixed_pair = grad_mixed[:, here]
        made = []
        for member in range(2):
            head = 2 * pair + member
            prob = head_prob(only(first, member, q_pair), k_pair, bias_ref, head, mask)
            grad_prob = dot_t(only(first, member, mixed_pair), v_pair)
            grad_value = t_dot(prob.astype(BF), mixed_pair)
            grad_scores = prob * (grad_prob - jnp.sum(prob * grad_prob, axis=-1, keepdims=True))
            grad_scores = grad_scores.astype(BF)
            turned = pltpu.roll(
                dot(flip, grad_scores), 0, axis=1, stride=1, stride_axis=0
            )
            diag_ref[head : head + 1, :] = jnp.sum(turned, axis=0, keepdims=True)
            made.append(
                (
                    dot(grad_scores, k_pair) * HEAD_DIM ** (-0.5),
                    t_dot(grad_scores, q_pair) * HEAD_DIM ** (-0.5),
                    grad_value,
                )
            )
        for number in range(3):
            grads_ref[number, :, here] = jnp.where(
                first, made[0][number], made[1][number]
            ).astype(BF)
    diag_ref[HEADS:, :] = jnp.zeros((16 - HEADS, ROWS), F32)
    grad_one = project_back(grads_ref[0], lower, weights.pair(0))
    grad_one = grad_one + project_back(grads_ref[1], lower, weights.pair(1))
    grad_one = grad_one + project_back(grads_ref[2], lower, weights.pair(2))
    scale = lax.rsqrt(jnp.mean(inputs * inputs, axis=-1, keepdims=True) + norm_eps)
    gain_grad_ref[0:1, :] = jnp.sum(grad_one * inputs * scale, axis=0, keepdims=True)
    gain_grad_ref[2:, :] = jnp.zeros((6, WIDTH), F32)
    gained = gains_ref[0:1, :] * grad_one
    input_grad = (
        grad_resid
        + scale * gained
        - inputs * (scale * scale * scale) * jnp.mean(inputs * gained, axis=-1, keepdims=True)
    ).astype(BF)
    input_grad_ref[...] = input_grad
    return input_grad


def last_backward_kernel(
    info_ref, routes_ref, routes_before_ref, gate_before_ref, cot_ref, back_ref, *refs
):
    x_ref, kept, gains_ref, bias_ref = refs[0], refs[1:8], refs[24], refs[29]
    small = small_halves(info_ref, 1, refs[25:29])
    outs, result_ref, send_ref = refs[30:35], refs[35], refs[36]
    weights = Weights(info_ref, 1, refs[8:24], refs[37], refs[38], (3, 0, 1, 2))
    gate_ref, resid_ref = kept[6], kept[3]
    place, route = token_slots(routes_ref, info_ref, route_hot(routes_ref))
    gathered = []
    for offsets in (ROW_PLACES, GRAD_PLACES):
        tables = [slot_table(place, route, TIGHT, o, 2 * EXPERTS * TIGHT) for o in offsets]
        gathered.append(jnp.concatenate([dot(t, back_ref[...]) for t in tables], axis=1))
    combined, grad_rows = gathered
    result_ref[...] = (resid_ref[...] + gate_ref[...] * combined).astype(BF)
    input_grad = backward_attention(
        x_ref[...].astype(F32),
        cot_ref[info_ref[0]].astype(F32),
        combined,
        grad_rows,
        info_ref,
        routes_ref,
        kept,
        weights,
        gains_ref,
        small,
        bias_ref,
        outs,
    )
    made_grad = (gate_before_ref[...] * input_grad.astype(F32)).astype(BF)
    place, route = token_slots(routes_before_ref, info_ref, route_hot(routes_before_ref))
    rows = t_dot(slot_table(place, route, SLOTS, 0, EXPERTS * SLOTS), made_grad).astype(BF)
    send_ref[: EXPERTS * SLOTS, :] = rows
    send_ref[EXPERTS * SLOTS :, :] = rows


def first_backward_kernel(info_ref, routes_ref, combined_ref, grad_ref, back_ref, *refs):
    x_ref, kept, gains_ref, bias_ref = refs[0], refs[1:8], refs[24], refs[29]
    small = small_halves(info_ref, 0, refs[25:29])
    outs = refs[30:35]
    weights = Weights(info_ref, 0, refs[8:24], refs[35], refs[36], (3, 0, 1, 2))
    place, route = token_slots(routes_ref, info_ref, route_hot(routes_ref))
    grad_rows = dot(slot_table(place, route, SLOTS, 0, 2 * EXPERTS * SLOTS), back_ref[...])
    backward_attention(
        x_ref[info_ref[0]].astype(F32),
        grad_ref[...].astype(F32),
        combined_ref[...],
        grad_rows,
        info_ref,
        routes_ref,
        kept,
        weights,
        gains_ref,
        small,
        bias_ref,
        outs,
    )


def weight_grad_kernel(info_ref, n1_ref, mixed_ref, grads_ref, keep_ref, send_ref):
    first_core = info_ref[0] == 0
    n1_turned, mixed_turned = n1_ref[...].T, mixed_ref[...].T
    for number in range(4):
        left = mixed_turned if number == 3 else n1_turned
        kept, sent = in_halves(grads_ref[number], first_core)
        for half in range(2):
            rows = left[half * HALF : half * HALF + HALF, :]
            keep_ref[half, number] = dot(rows, kept).astype(BF)
            send_ref[half, number] = dot(rows, sent).astype(BF)


def merge_kernel(*refs):
    far, out_far = refs[:5], refs[5]
    keep0_ref, got0_ref, keep1_ref, got1_ref, small_ref, out_ref, sems = refs[6:]
    near, size = refs[6:11], 64 // PARTS

    def copy(source, target, number, part):
        here = pl.ds(part * size, size)
        return pltpu.make_async_copy(source.at[here], target.at[here], sems.at[number, part])

    for part in range(PARTS):
        for number in range(5):
            copy(far[number], near[number], number, part).start()
    for part in range(PARTS):
        here = slice(part * size, part * size + size)
        for number in range(5):
            copy(far[number], near[number], number, part).wait()
        out_ref[here] = jnp.concatenate(
            [
                (keep0_ref[here].astype(F32) + got0_ref[here].astype(F32)).astype(BF),
                (keep1_ref[here].astype(F32) + got1_ref[here].astype(F32)).astype(BF),
                small_ref[here],
            ],
            axis=1,
        )
        copy(out_ref, out_far, 5, part).start()
    for part in range(PARTS):
        copy(out_ref, out_far, 5, part).wait()


def gelu_parts(hidden):
    slope = np.sqrt(2 / np.pi).astype(np.float32)
    square = hidden * hidden
    curve = jnp.tanh(slope * hidden * (1.0 + 0.044715 * square))
    gate = 0.5 * (1.0 + curve)
    grad = gate + 0.5 * hidden * (1.0 - curve * curve) * slope * (1.0 + 3 * 0.044715 * square)
    return hidden * gate, grad


class Chunks:
    def __init__(self, info_ref, layer, refs, win, wout, sems):
        self.info_ref, self.layer, self.refs = info_ref, layer, refs
        self.win, self.wout, self.sems = win, wout, sems
        for chunk in range(win.shape[0]):

            @pl.when(info_ref[0] == layer)
            def _():
                for copy in self.copies(0, chunk):
                    copy.start()

            @pl.when(info_ref[0] != layer)
            def _():
                for copy in self.copies(1, chunk):
                    copy.start()

    def copies(self, place, chunk):
        here = pl.ds(pl.multiple_of(chunk * BLOCK, BLOCK), BLOCK)
        return (
            pltpu.make_async_copy(
                self.refs[place].at[:, here], self.win.at[chunk], self.sems.at[0, chunk]
            ),
            pltpu.make_async_copy(
                self.refs[2 + place].at[here, :], self.wout.at[chunk], self.sems.at[1, chunk]
            ),
        )

    def take(self, chunk):
        for copy in self.copies(0, chunk):
            copy.wait()
        return self.win[chunk], self.wout[chunk]

    def grads_to(self, targets, din, dout, sems):
        self.targets, self.din, self.dout, self.out_sems = targets, din, dout, sems

    def grad_copies(self, place, chunk):
        here = pl.ds(pl.multiple_of(chunk * BLOCK, BLOCK), BLOCK)
        return (
            pltpu.make_async_copy(
                self.din.at[chunk], self.targets[2 * place].at[:, here], self.out_sems.at[0, chunk]
            ),
            pltpu.make_async_copy(
                self.dout.at[chunk],
                self.targets[2 * place + 1].at[here, :],
                self.out_sems.at[1, chunk],
            ),
        )

    def put(self, chunk):
        @pl.when(self.info_ref[0] == self.layer)
        def _():
            for copy in self.grad_copies(0, chunk):
                copy.start()

        @pl.when(self.info_ref[0] != self.layer)
        def _():
            for copy in self.grad_copies(1, chunk):
                copy.start()

    def finish(self):
        for chunk in range(self.din.shape[0]):
            for copy in self.grad_copies(0, chunk):
                copy.wait()


def expert_forward_kernel(info_ref, rows_ref, *refs):
    made_ref, win, wout, sems, made_sum = refs[4:]
    chunks = Chunks(info_ref, 0, refs[:4], win, wout, sems)
    made_sum[...] = jnp.zeros_like(made_sum)

    @pl.loop(0, win.shape[0])
    def _(chunk):
        w_in, w_out = chunks.take(chunk)
        act, _ = gelu_parts(dot(rows_ref[...], w_in))
        made_sum[...] += dot(act.astype(BF), w_out)

    made_ref[...] = made_sum[...].astype(BF)


def expert_backward_kernel(info_ref, rows_ref, grad_ref, *refs):
    back_ref, targets = refs[8], refs[9:13]
    win, wout, sems, din, dout, out_sems, rows_turned, rows_sum = refs[13:]
    chunks = Chunks(info_ref, 0, refs[:4], win, wout, sems)
    chunks.grads_to(targets, din, dout, out_sems)
    rows_sum[...] = jnp.zeros_like(rows_sum)
    rows_turned[...] = rows_ref[...].T

    @pl.loop(0, win.shape[0])
    def _(chunk):
        w_in, w_out = chunks.take(chunk)
        act, slope = gelu_parts(dot(rows_ref[...], w_in))
        grad_pre = (slope * dot_t(grad_ref[...], w_out)).astype(BF)
        dout[chunk] = t_dot(act.astype(BF), grad_ref[...]).astype(BF)
        din[chunk] = dot(rows_turned[...], grad_pre).astype(BF)
        chunks.put(chunk)
        rows_sum[...] += dot_t(grad_pre, w_in)

    back_ref[...] = rows_sum[...].astype(BF)
    chunks.finish()


def piece_order():
    order = np.zeros((GROUP * TIGHT, GROUP * TIGHT), np.float32)
    row = 0
    for offset in ROW_PLACES + GRAD_PLACES:
        for piece in range(GROUP):
            for slot in range(CAPACITY):
                order[row, piece * TIGHT + offset + slot] = 1
                row += 1
    return jnp.asarray(np.stack([order, order.T]), BF)


def expert_both_kernel(info_ref, both_ref, order_ref, *refs):
    back_ref, targets = refs[4], refs[5:9]
    win, wout, sems, din, dout, out_sems, rows, grads, rows_turned, made_sum, rows_sum = refs[9:]
    chunks = Chunks(info_ref, 1, refs[:4], win, wout, sems)
    chunks.grads_to(targets, din, dout, out_sems)
    packed, count = GROUP * TIGHT, GROUP * CAPACITY
    groups = both_ref.shape[0] // packed
    for group in range(groups):
        here = slice(group * count, group * count + count)
        block = dot(order_ref[0], both_ref[group * packed : group * packed + packed, :]).astype(BF)
        rows[here, :HALF] = block[:count]
        rows[here, HALF:] = block[count : 2 * count]
        grads[here, :HALF] = block[2 * count : 3 * count]
        grads[here, HALF:] = block[3 * count :]
    made_sum[...] = jnp.zeros_like(made_sum)
    rows_sum[...] = jnp.zeros_like(rows_sum)
    rows_turned[...] = rows[...].T

    @pl.loop(0, win.shape[0])
    def _(chunk):
        w_in, w_out = chunks.take(chunk)
        act, slope = gelu_parts(dot(rows[...], w_in))
        act = act.astype(BF)
        grad_pre = (slope * dot_t(grads[...], w_out)).astype(BF)
        dout[chunk] = t_dot(act, grads[...]).astype(BF)
        din[chunk] = dot(rows_turned[...], grad_pre).astype(BF)
        chunks.put(chunk)
        made_sum[...] += dot(act, w_out)
        rows_sum[...] += dot_t(grad_pre, w_in)

    for group in range(groups):
        here = slice(group * count, group * count + count)
        block = jnp.concatenate(
            [
                made_sum[here, :HALF],
                made_sum[here, HALF:],
                rows_sum[here, :HALF],
                rows_sum[here, HALF:],
            ],
            axis=0,
        ).astype(BF)
        back_ref[group * packed : group * packed + packed, :] = dot(order_ref[1], block).astype(BF)
    chunks.finish()


def shape(dims, kind=BF):
    return jax.ShapeDtypeStruct(dims, kind)


SMEM = pl.BlockSpec(memory_space=pltpu.SMEM)
VMEM = pl.BlockSpec(memory_space=pltpu.VMEM)
HBM = pl.BlockSpec(memory_space=pltpu.HBM)
BLOCK = 512


def whole_call(kernel, out_shape, name, before, weights=(), after=(), **more):
    scratch = []
    if len(weights) == 16:
        scratch = [pltpu.VMEM((8, HALF, WIDTH), BF), pltpu.SemaphoreType.DMA((8,))]
    return pl.pallas_call(
        kernel,
        out_shape=out_shape,
        in_specs=[SMEM] + [VMEM] * (len(before) - 1) + [HBM] * len(weights) + [VMEM] * len(after),
        out_specs=more.pop("out_specs", [VMEM] * len(out_shape)),
        scratch_shapes=more.pop("scratch", scratch),
        name=name,
        compiler_params=pltpu.CompilerParams(vmem_limit_bytes=60 * MIB),
        **more,
    )(*before, *weights, *after)


def merge_call(sums, smalls):
    return pl.pallas_call(
        merge_kernel,
        out_shape=shape((64, 104, HALF)),
        in_specs=[HBM] * 5,
        out_specs=HBM,
        scratch_shapes=[pltpu.VMEM((64, 48, HALF), BF)] * 4
        + [pltpu.VMEM((64, 8, HALF), BF), pltpu.VMEM((64, 104, HALF), BF)]
        + [pltpu.SemaphoreType.DMA((6, PARTS))],
        name="merge_grads",
        compiler_params=pltpu.CompilerParams(vmem_limit_bytes=60 * MIB),
    )(*[part.reshape(64, 48, HALF) for part in sums], smalls)


def expert_scratch(hidden, grads):
    count = hidden // BLOCK
    moved = [
        pltpu.VMEM((count, WIDTH, BLOCK), BF),
        pltpu.VMEM((count, BLOCK, WIDTH), BF),
        pltpu.SemaphoreType.DMA((2, count)),
    ]
    return moved * (2 if grads else 1)


def forward_shapes():
    tokens = shape((ROWS, WIDTH))
    return [
        tokens,
        tokens,
        tokens,
        tokens,
        tokens,
        shape((ROWS, WIDTH), F32),
        tokens,
        shape((ROWS, EXPERTS), F32),
        shape((ROWS, 1), F32),
        shape((8, WIDTH), F32),
        shape((16, ROWS), F32),
    ]


def backward_shapes():
    return [
        shape((4, ROWS, WIDTH)),
        shape((ROWS, WIDTH)),
        shape((8, WIDTH), F32),
        shape((EXPERTS, WIDTH), F32),
        shape((16, ROWS), F32),
    ]


def exchange(block):
    dims = block.shape
    pieces = lax.all_to_all(
        block.reshape((64, dims[0] // 64, dims[1])), BOTH, split_axis=0, concat_axis=0, tiled=True
    )
    return pieces.reshape(dims)


def shards(
    block_in,
    cotangent,
    lengths,
    routes,
    query_weight,
    key_weight,
    value_weight,
    out_weight,
    attn_gain,
    moe_gain,
    router,
    rel_table,
    expert_in,
    expert_out,
):
    core = lax.axis_index("section")
    half = lax.axis_index("shard")
    first_core = core == 0
    lower = half == 0

    def pick(left, right):
        return jnp.where(first_core, left, right)

    small = pl.pallas_call(
        pack_kernel, out_shape=shape((64, HALF)), name="pack_small"
    )(router[0], attn_gain, moe_gain, rel_table[0])
    small_arrived = lax.ppermute(small, "shard", [(0, 1), (1, 0)])

    weights_own = [w[0] for w in (query_weight, key_weight, value_weight, out_weight)]

    def cross_one_core(block, section, flip):
        pairs = []
        for part in range(64):
            source = section * 64 + part
            target = section * 64 + (part ^ 32 ^ flip)
            pairs.append((source, target))
        return lax.ppermute(block, ("section", "shard", "replica"), pairs)

    arrived0 = [cross_one_core(w, 0, number % 2) for number, w in enumerate(weights_own)]
    weights_swapped = [swap(w) for w in weights_own]
    small, small_arrived = lax.optimization_barrier((small, small_arrived, arrived0[0]))[:2]
    smalls = [small, swap(small), small_arrived, swap(small_arrived)]
    passed0 = [swap(w) for w in arrived0[:3]]
    bucket_hot = np.eye(NB, dtype=np.float32)[bucket_of_distance(ROWS)]
    turned = bucket_hot[(-np.arange(ROWS)) % ROWS]

    turned_hot = jnp.asarray(turned.T, BF)

    routes_other = swap(pick(routes[0, 1], routes[0, 0]))
    routes_mine = pick(routes[0, 0], routes[0, 1])
    layer_routes = [pick(routes_mine, routes_other), pick(routes_other, routes_mine)]
    runs = pick(lengths[0, 0], lengths[1, 0])
    info = jnp.concatenate(
        [jnp.stack([core, half]).astype(jnp.int32), jnp.cumsum(runs, dtype=jnp.int32)]
    )

    tied = lax.optimization_barrier(
        (arrived0[3], info, *layer_routes, *smalls, *weights_swapped)
    )
    arrived0[3], info = tied[:2]
    layer_routes, smalls, weights_swapped = list(tied[2:4]), list(tied[4:8]), list(tied[8:])
    passed0.append(swap(arrived0[3]))
    later = lax.optimization_barrier(tuple(weights_own) + tuple(arrived0))[:4]
    arrived1 = [cross_one_core(w, 1, number % 2) for number, w in enumerate(later)]
    passed1 = [swap(w) for w in arrived1]
    weights = [[], []]
    for number in range(4):
        own = [weights_own[number], weights_swapped[number]]
        weights[0] += own + [arrived0[number], passed0[number]]
        weights[1] += own + [arrived1[number], passed1[number]]
    experts = []
    for w in lax.optimization_barrier((expert_in[0, 0], expert_out[0, 0], *passed0))[:2]:
        experts += [w, swap(w)]

    *kept0, send = whole_call(
        first_forward_kernel,
        forward_shapes() + [shape((512, WIDTH))],
        "attend_first",
        [info, layer_routes[0], block_in],
        weights[0],
        [*smalls, turned_hot],
    )
    rows0 = exchange(send)
    hidden = expert_in.shape[3]
    sum_scratch = pltpu.VMEM((512, WIDTH), F32)
    (made,) = whole_call(
        expert_forward_kernel,
        [shape((512, WIDTH))],
        "expert_first",
        [info, rows0],
        experts,
        scratch=expert_scratch(hidden, False) + [sum_scratch],
    )
    back = exchange(made)
    n10, q0, k0, v0, mixed0, resid0, n20, prob0, gate0, gains0, bias0 = kept0
    *kept1, send, middle, combined0 = whole_call(
        second_forward_kernel,
        forward_shapes()
        + [shape((64 * TIGHT, HALF)), shape((ROWS, WIDTH)), shape((ROWS, WIDTH), F32)],
        "attend_second",
        [info, layer_routes[1], layer_routes[0], resid0, gate0, back, cotangent],
        weights[1],
        [*smalls, turned_hot],
    )
    both = exchange(send)
    grad_shapes = [shape((WIDTH, hidden)), shape((hidden, WIDTH))] * 2
    back, *expert_grads = whole_call(
        expert_both_kernel,
        [shape((64 * TIGHT, HALF))] + grad_shapes,
        "expert_second",
        [info, both, piece_order()],
        experts,
        out_specs=[VMEM] + [HBM] * 4,
        scratch=expert_scratch(hidden, True)
        + [pltpu.VMEM((64 * CAPACITY, WIDTH), BF)] * 2
        + [pltpu.VMEM((WIDTH, 64 * CAPACITY), BF)]
        + [pltpu.VMEM((64 * CAPACITY, WIDTH), F32)] * 2,
    )
    back = exchange(back)
    n11, q1, k1, v1, mixed1, resid1, n21, prob1, gate1, gains1, bias1 = kept1
    *grads1, result, send = whole_call(
        last_backward_kernel,
        backward_shapes() + [shape((ROWS, WIDTH)), shape((512, WIDTH))],
        "attend_second_back",
        [info, layer_routes[1], layer_routes[0], gate0, cotangent, back]
        + [middle, q1, k1, v1, resid1, n21, prob1, gate1],
        weights[1],
        [gains1, *smalls, bias1],
    )
    made_grads = exchange(send)
    back, *expert_grads = whole_call(
        expert_backward_kernel,
        [shape((512, WIDTH))] + grad_shapes,
        "expert_first_back",
        [info, rows0, made_grads],
        experts + expert_grads,
        out_specs=[VMEM] + [HBM] * 4,
        scratch=expert_scratch(hidden, True) + [pltpu.VMEM((WIDTH, 512), BF), sum_scratch],
        input_output_aliases={7: 1, 8: 2, 9: 3, 10: 4},
    )
    back = exchange(back)
    grads0 = whole_call(
        first_backward_kernel,
        backward_shapes(),
        "attend_first_back",
        [info, layer_routes[0], combined0, grads1[1], back]
        + [block_in, q0, k0, v0, resid0, n20, prob0, gate0],
        weights[0],
        [gains0, *smalls, bias0],
    )

    def small_rows(gain_grad, router_grad, diag):
        table = lax.dot_general(
            diag[:HEADS],
            jnp.asarray(bucket_hot[::-1]),
            (((1,), (0,)), ((), ())),
            precision=lax.Precision.HIGHEST,
            preferred_element_type=F32,
        )
        table = jnp.transpose(table.reshape(HEADS, 2, NB // 2), (1, 0, 2))
        table = jnp.pad(table, ((0, 0), (0, 0), (0, HALF - NB // 2)))
        gains = jnp.transpose(gain_grad[:2].reshape(2, 2, HALF), (1, 0, 2))
        others = jnp.concatenate([gains, table, jnp.zeros((2, EXPERTS - HEADS - 2, HALF), F32)], axis=1)
        routers = jnp.transpose(router_grad.reshape(EXPERTS, 2, HALF), (1, 0, 2))
        return jnp.stack([routers, others], axis=2).astype(BF)

    def summed_cores(n1, mixed, grads):
        keep, send = whole_call(
            weight_grad_kernel,
            [shape((2, 4, HALF, HALF))] * 2,
            "weight_grads",
            [info, n1, mixed, grads[0]],
        )
        return keep, swap(send)

    keep1, got1 = summed_cores(n11, mixed1, grads1)
    small1 = small_rows(*grads1[2:]).reshape(64, 2, HALF)
    keep0, got0 = summed_cores(n10, mixed0, grads0)
    small0 = small_rows(*grads0[2:]).reshape(64, 2, HALF)
    expert_got = [swap(g) for g in expert_grads[2:]]
    keep0, *expert_got = lax.optimization_barrier((keep0, *expert_got))

    small_grads = jnp.pad(small0, ((0, 0), (0, 6), (0, 0))) + jnp.pad(small1, ((0, 0), (2, 4), (0, 0)))
    pieces = merge_call([keep0, got0, keep1, got1], small_grads)
    pieces = lax.all_to_all(pieces, BOTH, split_axis=0, concat_axis=0, tiled=True)
    total = jnp.sum(pieces.astype(F32), axis=0).astype(BF)
    expert_totals = [k.astype(F32) + g.astype(F32) for k, g in zip(expert_grads[:2], expert_got)]

    def by_micro(first, second):
        mine, theirs = pick(first, second), swap(pick(second, first))
        return jnp.stack([pick(mine, theirs), pick(theirs, mine)])

    section_out = by_micro(middle, result)
    input_grad = by_micro(grads0[1], grads1[1])
    total, section_out, input_grad, *expert_totals = lax.optimization_barrier(
        (total, section_out, input_grad, *expert_totals)
    )
    per_layer = jnp.stack(
        [
            jnp.concatenate([total[:48], total[96:98], jnp.zeros((6, HALF), BF)]),
            jnp.concatenate([total[48:96], total[98:100], jnp.zeros((6, HALF), BF)]),
        ]
    )
    spread = jnp.broadcast_to(per_layer[:, None], (2, 32, 56, HALF)).reshape(64, 56, HALF)
    whole = lax.all_to_all(
        spread, ("section", "replica"), split_axis=0, concat_axis=0, tiled=True
    ).reshape(2, 32, 56, HALF)
    full = jnp.concatenate([whole[0, :, :48], whole[1, :, :48]], axis=2).astype(F32)
    full = full.reshape(4, HALF, WIDTH)
    smalls = whole[0, :, 48:50].astype(F32) + whole[1, :, 48:50].astype(F32)
    router_grad = jnp.transpose(smalls[:, 0], (1, 0))
    table_grad = jnp.transpose(smalls[2 : 2 + HEADS, 1, : NB // 2], (1, 0))

    return (
        section_out[None],
        input_grad[None],
        full[0][None],
        full[1][None],
        full[2][None],
        full[3][None],
        smalls[0, 1][None],
        smalls[1, 1][None],
        router_grad[None],
        table_grad[None],
        expert_totals[0][None, None],
        expert_totals[1][None, None],
    )


def solution(mesh):
    in_specs = (
        P(None, ("shard", "replica"), None),
        P(None, ("shard", "replica"), None),
        P(None, ("shard", "replica"), None),
        P("section", None, ("shard", "replica"), None),
        P("section", "shard", None),
        P("section", "shard", None),
        P("section", "shard", None),
        P("section", "shard", None),
        P("section", "shard"),
        P("section", "shard"),
        P("section", "shard", None),
        P("section", "shard", None),
        P("section", "replica", None, "shard"),
        P("section", "replica", "shard", None),
    )
    out_specs = (
        P("section", None, ("shard", "replica"), None),
        P("section", None, ("shard", "replica"), None),
        P("section", "shard", None),
        P("section", "shard", None),
        P("section", "shard", None),
        P("section", "shard", None),
        P("section", "shard"),
        P("section", "shard"),
        P("section", "shard", None),
        P("section", "shard", None),
        P("section", "replica", None, "shard"),
        P("section", "replica", "shard", None),
    )
    return jax.shard_map(shards, mesh=mesh, in_specs=in_specs, out_specs=out_specs, check_vma=False)
```
